256 devices in a mesh: elem: 32 (over z, x), plane: 8 (over y, core).
Axes of the slice: x: 4, y: 4, z: 8, core: 2. Of those that a mesh axis runs over, the one named last changes fastest.
Arguments:
- velocity: float32 [3, 128, 8, 8, 4096], P(None, 'plane', None, None, 'elem'), may hold values from -6 to 6
- elem_scale: float32 [2, 4096], P(None, 'elem'), may hold values from 0.6 to 1.6
- elem_ids: int32 [32, 128], P('elem'), may hold values from 0 to 4095, as said below
- edge_blocks: int32 [32, 2, 64], P('elem'), may hold values from 256 to 511, as said below
Outputs:
- velocity_new: float32 [3, 128, 8, 8, 4096], P(None, 'plane', None, None, 'elem')
- residual: float32 [3, 128, 8, 8, 4096], P(None, 'plane', None, None, 'elem')
The draws below stay inside these ranges and needn't reach their ends.
Inputs may be any that keep to these rules, and one draw needn't show every extreme that they name: `elem_ids`: row d holds, in storage order, the ids of the 128 elements of radial rows 2d and 2d + 1; the element in radial row r at position j around has id r * 64 + j. edge_blocks[d, 0, j] is 256 plus the storage slot, within row d of elem_ids, of the element in radial row 2d at position j around; edge_blocks[d, 1, j] is 384 plus the storage slot of the element in radial row 2d + 1 at position j.
All inputs are finite; a program needn't handle non-finite values.
Results may differ from the reference program's by a relative error of at most 0.0009.
Values sent between devices are 32-bit elements; how exact they have to be, the bound alone decides.
A program may use at most 128 MiB of HBM per device.

```python
import math
import jax
import jax.numpy as jnp
import numpy as np
from jax import lax

NODES = 8
Z = 128
ED = 128
ITERS = 2
GW = 64
NE = 4096
N_ELEM = 32


def shuffled(part_key):
    return jax.random.permutation(part_key, ED).astype(jnp.int32)


def band_orders(key):
    part_keys = jax.random.split(key, N_ELEM)
    return jax.vmap(shuffled)(part_keys)


def draw_elem_ids(key, part):
    orders = band_orders(key)
    return (orders + ED * jnp.arange(N_ELEM, dtype=jnp.int32)[:, None]).astype(jnp.int32)


def draw_edge_blocks(key, part):
    orders = band_orders(key)
    inverse = jnp.argsort(orders, axis=1, stable=True).astype(jnp.int32)
    lower = 2 * ED + inverse[:, :GW]
    upper = 3 * ED + inverse[:, GW:]
    return jnp.stack([lower, upper], axis=1).astype(jnp.int32)


def block_levels(own_key, dims, cuts, low, top_value):
    loudness = 1.0
    for axis_at, parts in cuts:
        steps = jax.random.uniform(jax.random.fold_in(jax.random.fold_in(own_key, 6), axis_at), (parts,), jnp.float32, low / len(cuts), top_value / len(cuts))
        loudness = loudness * jnp.repeat(jnp.exp(steps), dims[axis_at] // parts).reshape((-1,) + (1,) * (len(dims) - 1 - axis_at))
    return loudness


def noise(own_key, shape, spread, bound, cuts=(), held_as=jnp.bfloat16):
    entries = spread * jax.random.normal(own_key, shape, jnp.float32)
    if cuts:
        entries = entries * block_levels(own_key, shape, cuts, -0.22, 0.18)
    return jnp.clip(entries, -bound, bound).astype(held_as)


def setup_inputs(seed: int = 0) -> dict:
    splits = jax.random.split(jax.random.key(seed), 5)
    velocity = noise(splits[0], (3, Z, NODES, NODES, NE), 1.0, 6.0, ((1, 8), (4, 32)), jnp.float32)
    elem_scale = jnp.clip(jnp.exp(math.log(1.6) - 0.98082923 * jax.random.uniform(splits[1], (2, NE), jnp.float32) ** block_levels(splits[1], (2, NE), ((1, 32),), -0.2, 0.2)), 0.6, 1.6)
    elem_ids = draw_elem_ids(jax.random.fold_in(splits[4], 71), 0)
    edge_blocks = draw_edge_blocks(jax.random.fold_in(splits[4], 71), 0)
    return dict(velocity=velocity, elem_scale=elem_scale, elem_ids=elem_ids, edge_blocks=edge_blocks)


penalty = 8.0
lam_zero = 4.0
wave_step = 0.1
highest = lax.Precision.HIGHEST


def node_tables(number):
    degree = number - 1
    points = -np.cos(np.pi * np.arange(number) / degree)
    scales = np.ones(number)
    scales[0] = 2.0
    scales[-1] = 2.0
    barycentric = ((-1.0) ** np.arange(number)) / scales
    derivative = np.zeros((number, number))
    for row_at in range(number):
        for col_at in range(number):
            if row_at != col_at:
                derivative[row_at, col_at] = (barycentric[col_at] / barycentric[row_at]) / (points[row_at] - points[col_at])
        derivative[row_at, row_at] = -np.sum(derivative[row_at])
    weights = np.zeros(number)
    for node_at in range(number):
        running = 0.0
        for harmonic in range(1, degree // 2 + 1):
            factor = 1.0 if 2 * harmonic == degree else 2.0
            running += factor / (4.0 * harmonic * harmonic - 1.0) * np.cos(2.0 * np.pi * node_at * harmonic / degree)
        end_factor = 1.0 if node_at in (0, degree) else 2.0
        weights[node_at] = end_factor / degree * (1.0 - running)
    stiffness = derivative.T @ (weights[:, None] * derivative)
    return jnp.asarray(derivative, jnp.float32), jnp.asarray(weights, jnp.float32), jnp.asarray(stiffness, jnp.float32)


def mode_table(planes):
    mode_slots = jnp.arange(planes, dtype=jnp.int32)
    harmonic = mode_slots // 2
    phase_index = (harmonic[:, None] * mode_slots[None, :]) % planes
    angles = (2.0 * math.pi / planes) * phase_index.astype(jnp.float32)
    cosine = jnp.cos(angles) * (2.0 / planes)
    sine_rows = jnp.sin(angles) * (2.0 / planes)
    fourier = jnp.where((mode_slots % 2 == 0)[:, None], cosine, sine_rows)
    mean_row = jnp.ones((planes,), jnp.float32) / planes
    alternating = jnp.where(mode_slots % 2 == 0, 1.0, -1.0).astype(jnp.float32) / planes
    return fourier.at[0].set(mean_row).at[1].set(alternating)


def element_geometry(members, scale_pair, circle, radial):
    row_index = (members // circle).astype(jnp.float32)
    growth = 1.0 + 2.0 * row_index / (radial - 1)
    return scale_pair[0] * growth, scale_pair[1]


def neighbour_table(members, circle):
    row_index = members // circle
    beside_all = members % circle
    targets = jnp.stack([row_index * circle + (beside_all - 1) % circle, row_index * circle + (beside_all + 1) % circle, members - circle, members + circle])
    return (targets[:, :, None] == members[None, None, :]).astype(jnp.float32)


def with_products(velocity):
    return jnp.stack([velocity[0], velocity[1], velocity[2], velocity[0] * velocity[0], velocity[0] * velocity[1], velocity[0] * velocity[2], velocity[1] * velocity[1], velocity[1] * velocity[2], velocity[2] * velocity[2]])


def edge_values(values):
    traces = jnp.stack([values[:, 0, :, :], values[:, -1, :, :], values[:, :, 0, :], values[:, :, -1, :]], axis=2)
    return traces.reshape(values.shape[0] * values.shape[1], 4 * values.shape[3])


def helmholtz(values, rim_values, helm_shift, circ_size, radial_size, linkage, blocks, from_below, from_above, derivative, weights, stiffness):
    systems = values.shape[0]
    number = values.shape[1]
    elements = values.shape[3]
    sides = rim_values.reshape(systems * number, 4, elements)
    swapped = jnp.stack([sides[:, 1], sides[:, 0], sides[:, 3], sides[:, 2]], axis=1)
    facing = jnp.einsum("kst,sat->ksa", swapped, linkage, precision=highest)
    facing = facing.reshape(systems * number, 4 * elements)
    facing = facing.at[:, blocks[0]].add(from_below).at[:, blocks[1]].add(from_above)
    mismatch = (rim_values - facing).reshape(systems, number, 4, elements)
    coupling = penalty * weights[None, :, None, None] * mismatch
    mass_diag = (weights[:, None] * weights[None, :])[None, :, :, None] * (circ_size * radial_size)[None, None, None, :]
    result = helm_shift[:, None, None, None] * mass_diag * values
    result = result + (radial_size / circ_size)[None, None, None, :] * weights[None, None, :, None] * jnp.einsum("ac,kcbe->kabe", stiffness, values, precision=highest)
    result = result + (circ_size / radial_size)[None, None, None, :] * weights[None, :, None, None] * jnp.einsum("bc,kace->kabe", stiffness, values, precision=highest)
    result = result.at[:, 0, :, :].add(coupling[:, :, 0]).at[:, -1, :, :].add(coupling[:, :, 1])
    result = result.at[:, :, 0, :].add(coupling[:, :, 2]).at[:, :, -1, :].add(coupling[:, :, 3])
    return result


def right_side(modal, circ_size, radial_size, pair_waves, derivative, weights):
    flux_index = ((3, 4, 5), (4, 6, 7), (5, 7, 8))
    modes = modal.shape[1]
    mass_diag = (weights[:, None] * weights[None, :])[:, :, None] * (circ_size * radial_size)[None, None, :]
    components = []
    for component in range(3):
        flux_x = modal[flux_index[component][0]]
        flux_y = modal[flux_index[component][1]]
        flux_z = modal[flux_index[component][2]].reshape((modes // 2, 2) + modal.shape[2:])
        grad_x = jnp.einsum("ac,mcbe->mabe", derivative, flux_x, precision=highest) / circ_size
        grad_y = jnp.einsum("bc,mace->mabe", derivative, flux_y, precision=highest) / radial_size
        grad_z = jnp.stack([flux_z[:, 1], -flux_z[:, 0]], axis=1) * (wave_step * pair_waves)[:, None, None, None, None]
        advect = grad_x + grad_y + grad_z.reshape(modal.shape[1:])
        components.append(mass_diag[None] * (lam_zero * modal[component] - advect))
    return jnp.stack(components)


def reference(velocity, elem_scale, elem_ids, edge_blocks):
    derivative, weights, stiffness = node_tables(NODES)
    fourier = mode_table(Z)
    circle = ED // 2
    radial = 2 * N_ELEM
    pair_waves = jnp.arange(Z // 2, dtype=jnp.int32).astype(jnp.float32)
    mode_slots = jnp.arange(Z, dtype=jnp.int32)
    wavenumber = jnp.where(mode_slots == 1, Z // 2, mode_slots // 2).astype(jnp.float32)
    shift_all = lam_zero + (wave_step * wavenumber) ** 2
    vel_blocks = velocity.reshape(3, Z, NODES, NODES, N_ELEM, ED)
    scale_blocks = elem_scale.reshape(2, N_ELEM, ED)

    def forcing_part(part_index):
        part_vel = jnp.take(vel_blocks, part_index, axis=4)
        circ_size, radial_size = element_geometry(elem_ids[part_index], scale_blocks[:, part_index], circle, radial)
        modal = jnp.einsum("mz,fzabe->fmabe", fourier, with_products(part_vel), precision=highest)
        return right_side(modal, circ_size, radial_size, pair_waves, derivative, weights)

    forcing_all = lax.map(forcing_part, jnp.arange(N_ELEM, dtype=jnp.int32))

    def geometry_part(members, scale_pair):
        return element_geometry(members, scale_pair, circle, radial)

    circ_all, radial_all = jax.vmap(geometry_part, in_axes=(0, 1))(elem_ids, scale_blocks)

    def linkage_part(members):
        return neighbour_table(members, circle)

    linkage_all = jax.vmap(linkage_part)(elem_ids)

    def take_rows(rim_values, indices):
        return rim_values[:, indices]

    def solve_mode(mode_slot):
        forcing_mode = jnp.take(forcing_all, mode_slot, axis=2)
        helm_shift = shift_all[mode_slot] * jnp.ones((3,), jnp.float32)

        def apply_operator(values):
            rim_values = jax.vmap(edge_values)(values)
            upper = jax.vmap(take_rows)(rim_values, edge_blocks[:, 1])
            lower = jax.vmap(take_rows)(rim_values, edge_blocks[:, 0])
            empty_rim = jnp.zeros_like(upper[:1])
            from_below = jnp.concatenate([empty_rim, upper[:-1]])
            from_above = jnp.concatenate([lower[1:], empty_rim])
            return jax.vmap(helmholtz, in_axes=(0, 0, None, 0, 0, 0, 0, 0, 0, None, None, None))(values, rim_values, helm_shift, circ_all, radial_all, linkage_all, edge_blocks, from_below, from_above, derivative, weights, stiffness)

        def inner_dot(first_vec, second_vec):
            return jnp.sum(first_vec * second_vec, axis=(0, 2, 3, 4))

        solution = jnp.zeros_like(forcing_mode)
        residual = forcing_mode
        direction = forcing_mode
        norm_now = inner_dot(residual, residual)
        for sweep in range(ITERS):
            applied = apply_operator(direction)
            step_len = norm_now / inner_dot(direction, applied)
            solution = solution + step_len[None, :, None, None, None] * direction
            residual = residual - step_len[None, :, None, None, None] * applied
            norm_next = inner_dot(residual, residual)
            direction = residual + (norm_next / norm_now)[None, :, None, None, None] * direction
            norm_now = norm_next
        return solution, residual

    solutions, residuals = lax.map(solve_mode, jnp.arange(Z, dtype=jnp.int32))
    velocity_new = jnp.transpose(solutions, (2, 0, 3, 4, 1, 5)).reshape(3, Z, NODES, NODES, NE)
    residual_out = jnp.transpose(residuals, (2, 0, 3, 4, 1, 5)).reshape(3, Z, NODES, NODES, NE)
    return (velocity_new, residual_out)
```

```python
import functools
import math

import jax
import jax.numpy as jnp
import ml_dtypes
import numpy as np
from jax import lax
from jax.experimental import pallas as pl
from jax.experimental.pallas import tpu as pltpu
from jax.sharding import PartitionSpec as P

MESH = pl.DeviceIdType.MESH
F32 = jnp.float32
BF16 = jnp.bfloat16

N = 8
ED = 128
Z = 128
NP = 8
ZL = Z // NP
EG = ED // NP
SYS = 3 * ZL
NX = 4
NZ = 8
NE = NX * NZ
PEN = 8.0
LAM = 4.0
STEP = 0.1


def node_tables():
    degree = N - 1
    points = -np.cos(np.pi * np.arange(N) / degree)
    scales = np.ones(N)
    scales[0] = 2.0
    scales[-1] = 2.0
    bary = (-1.0) ** np.arange(N) / scales
    deriv = np.zeros((N, N))
    for i in range(N):
        for j in range(N):
            if i != j:
                deriv[i, j] = bary[j] / bary[i] / (points[i] - points[j])
        deriv[i, i] = -np.sum(deriv[i])
    weights = np.zeros(N)
    for i in range(N):
        running = 0.0
        for k in range(1, degree // 2 + 1):
            factor = 1.0 if 2 * k == degree else 2.0
            running += factor / (4.0 * k * k - 1.0) * np.cos(2.0 * np.pi * i * k / degree)
        weights[i] = (1.0 if i in (0, degree) else 2.0) / degree * (1.0 - running)
    stiff = deriv.T @ (weights[:, None] * deriv)
    return deriv, weights, stiff


def mode_matrix():
    slots = np.arange(Z)
    harmonic = slots // 2
    angles = 2.0 * math.pi / Z * (harmonic[:, None] * slots[None, :] % Z)
    four = np.where((slots % 2 == 0)[:, None], np.cos(angles), np.sin(angles)) * (2.0 / Z)
    four[0] = 1.0 / Z
    four[1] = np.where(slots % 2 == 0, 1.0, -1.0) / Z
    dz = np.zeros((Z, Z))
    wave = STEP * np.arange(Z // 2)
    dz[0::2] = wave[:, None] * four[1::2]
    dz[1::2] = -wave[:, None] * four[0::2]
    return np.concatenate([four, -dz], axis=1)


def halves(table):
    high = table.astype(np.float32).astype(ml_dtypes.bfloat16)
    low = (table - high.astype(np.float64)).astype(np.float32).astype(ml_dtypes.bfloat16)
    return np.stack([high, low])


DERIV, WEIGHTS, STIFF = node_tables()


def split(x):
    high = x.astype(BF16)
    return high, (x - high.astype(F32)).astype(BF16)


def dot(x, y):
    return jnp.dot(x, y, preferred_element_type=F32)


def pick(x, table):
    high, low = split(x)
    return dot(high, table) + dot(low, table)


def block_transpose(rows):
    rows = list(rows)
    lane = lax.broadcasted_iota(jnp.int32, rows[0].shape, rows[0].ndim - 1) // EG
    for d in (1, 2, 4):
        clear = (lane & d) == 0
        for i in range(NP):
            if i & d == 0:
                x, y = rows[i], rows[i + d]
                axis = x.ndim - 1
                rows[i] = jnp.where(clear, x, pltpu.roll(y, EG * d, axis))
                rows[i + d] = jnp.where(clear, pltpu.roll(x, ED - EG * d, axis), y)
    return rows


def stiff_times(v):
    even = [v[p] + v[N - 1 - p] for p in range(N // 2)]
    odd = [v[p] - v[N - 1 - p] for p in range(N // 2)]
    out = [None] * N
    for a in range(N // 2):
        s = [0.5 * (STIFF[a, p] + STIFF[a, N - 1 - p]) for p in range(N // 2)]
        t = [0.5 * (STIFF[a, p] - STIFF[a, N - 1 - p]) for p in range(N // 2)]
        e = sum(float(s[p]) * even[p] for p in range(1, N // 2)) + float(s[0]) * even[0]
        o = sum(float(t[p]) * odd[p] for p in range(1, N // 2)) + float(t[0]) * odd[0]
        out[a] = e + o
        out[N - 1 - a] = e - o
    return out


def kernel(
    vel,
    scale,
    ids,
    wlane,
    fmat,
    dkron,
    dtab,
    r_out,
    q_out,
    p_out,
    coef_out,
    vin,
    xsend,
    xbuf,
    acc,
    bbuf,
    fsend,
    fbuf,
    res,
    qv,
    pv,
    geo,
    hel,
    tables,
    face,
    edge,
    hsend,
    hrecv,
    dots,
    rbuf1,
    rbuf2,
    in_sem,
    out_sem,
    s1,
    r1,
    s2,
    r2,
    hs,
    hr,
    as1,
    ar1,
    as2,
    ar2,
):
    e = lax.axis_index("elem")
    me = lax.axis_index("plane")
    y, core = me // 2, lax.rem(me, 2)
    z, x = e // NX, lax.rem(e, NX)
    plane_offsets = [(dy, dc) for dy in (2, 1, 3, 0) for dc in (0, 1) if (dy, dc) != (0, 0)]
    plane_peers = [lax.rem(y + dy, 4) * 2 + lax.rem(core + dc, 2) for dy, dc in plane_offsets]
    x_peers = [z * NX + lax.rem(x + d, NX) for d in (2, 1, 3)]
    z_peers = [lax.rem(z + d, NZ) * NX + x for d in (4, 3, 5, 2, 6, 1, 7)]
    up, down = lax.rem(e + 1, NE), lax.rem(e + NE - 1, NE)

    load = pltpu.make_async_copy(vel, vin, in_sem)
    load.start()
    barrier = pltpu.get_barrier_semaphore()
    for t in plane_peers:
        pl.semaphore_signal(barrier, inc=1, device_id=(e, t), device_id_type=MESH)
    for t in x_peers + z_peers + [up, down]:
        pl.semaphore_signal(barrier, inc=1, device_id=(t, me), device_id_type=MESH)

    lid = ids[...] & (ED - 1)
    growth = 1.0 + 2.0 * (ids[...] // 64).astype(F32) / 63.0
    circ = scale[0:1, :] * growth
    radial = scale[1:2, :]
    geo[0:1, :] = circ * radial
    geo[1:2, :] = radial / circ
    geo[2:3, :] = circ / radial
    lane_row = lax.broadcasted_iota(jnp.int32, (1, ED), 1)
    for k, val in ((3, circ), (4, radial)):
        val = pltpu.roll(jnp.broadcast_to(val, (8, ED)), lax.rem(ED - EG * me, ED), 1)
        val = jnp.where(lax.broadcasted_iota(jnp.int32, (8, ED), 1) < EG, val, 0.0)
        for d in (1, 2, 4):
            val = val + pltpu.roll(val, EG * d, 1)
        geo[k : k + 1, :] = val[0:1, :]
    wl = wlane[...]
    g_circ, g_radial = geo[3:4, :], geo[4:5, :]
    geo[5:6, :] = g_circ * g_radial * wl
    geo[6:7, :] = g_circ * wl
    geo[7:8, :] = g_radial * wl
    load.wait()
    pl.semaphore_wait(barrier, NP - 1 + 3 + 7 + 2)

    def copy1(a, i):
        t = plane_peers[i]
        return pltpu.make_async_remote_copy(
            src_ref=xsend.at[a, t],
            dst_ref=xbuf.at[a, :, pl.ds(pl.multiple_of(me * ZL, ZL), ZL), :],
            send_sem=s1.at[a, i],
            recv_sem=r1.at[a, i],
            device_id=(e, t),
            device_id_type=MESH,
        )

    def copy2(a, i):
        t = plane_peers[i]
        return pltpu.make_async_remote_copy(
            src_ref=fsend.at[a, :, pl.ds(pl.multiple_of(t * ZL, ZL), ZL), :],
            dst_ref=fbuf.at[a, me],
            send_sem=s2.at[a, i],
            recv_sem=r2.at[a, i],
            device_id=(e, t),
            device_id_type=MESH,
        )

    def send_first(a, carry):
        for c in range(3):
            for h in range(ZL // 8):
                base = (c * ZL + h * 8) * N * N + a * N
                rows = [vin[pl.ds(base + b, 8, stride=N * N), :] for b in range(N)]
                for q, row in enumerate(block_transpose(rows)):
                    xsend[a, q, c, pl.ds(h * 8, 8), :] = row
        for i in range(NP - 1):
            copy1(a, i).start()
        mine = pl.ds(pl.multiple_of(me * ZL, ZL), ZL)
        xbuf[a, :, mine, :] = xsend[a, me]
        return carry

    lax.fori_loop(0, N, send_first, 0)

    acc[...] = jnp.zeros_like(acc)
    dots[...] = jnp.zeros_like(dots)
    row_i = lax.broadcasted_iota(jnp.int32, (ED, ED), 0)
    lane_i = lax.broadcasted_iota(jnp.int32, (ED, ED), 1)
    lid_l = jnp.broadcast_to(lid, (ED, ED))
    lid_t = jnp.transpose(lid_l.astype(F32)).astype(jnp.int32)

    def ones(where):
        return jnp.where(where, 1.0, 0.0).astype(BF16)

    tables[0] = ones(lid_t == ((lid_l & 64) | ((lid_l + 63) & 63)))
    tables[1] = ones(lid_t == ((lid_l & 64) | ((lid_l + 1) & 63)))
    tables[2] = ones((lid_t == (lid_l ^ 64)) & (lid_l >= 64))
    tables[3] = ones((lid_t == (lid_l ^ 64)) & (lid_l < 64))
    tables[4] = ones(lid_t == lane_i + 64)
    tables[5] = ones((lid_t == lane_i) & (lane_i >= 64))
    tables[6] = ones((lid_t == lane_i) & (lane_i < 64))
    tables[7] = ones(lid_t + 64 == lane_i)
    tables[8] = ones((row_i == lid_l) & (lid_l < 64))
    tables[9] = ones(row_i == lid_l + 64)
    tables[10] = ones(row_i + 64 == lid_l)
    tables[11] = ones((row_i == lid_l) & (lid_l >= 64))
    slot = me * ZL + (lax.broadcasted_iota(jnp.int32, (SYS, ED), 0) & (ZL - 1))
    kappa = jnp.where(slot == 1, Z // 2, slot // 2).astype(F32)
    hel[...] = (LAM + (STEP * kappa) * (STEP * kappa)) * geo[0:1, :]

    def arrive_first(p, carry):
        for i in range(NP - 1):
            copy1(p, i).wait_recv()
        w_p = dtab[N, p]
        mass = geo[5:6, :] * w_p
        g_y = geo[6:7, :] * w_p
        g_x = geo[7:8, :]
        for c in range(3):
            fy_high, fy_low = split(xbuf[p, 1] * xbuf[p, c])
            dy = dot(fy_high, dkron[0]) + dot(fy_low, dkron[0]) + dot(fy_high, dkron[1])
            acc[p, c] += (LAM * mass) * xbuf[p, c] - g_y * dy
            b_high, b_low = split(mass * (xbuf[p, 2] * xbuf[p, c]))
            bbuf[p, 0, c] = b_high
            bbuf[p, 1, c] = b_low
            for h in range(4):
                rows = pl.ds(h * 32, 32)
                fx = g_x * (xbuf[p, 0, rows, :] * xbuf[p, c, rows, :])
                for a in range(N):
                    acc[a, c, rows, :] += dtab[a, p] * fx
        return carry

    lax.fori_loop(0, N, arrive_first, 0)

    def send_second(a, carry):
        for c in range(3):
            a_high, a_low = split(acc[a, c])
            high = jnp.concatenate([a_high, bbuf[a, 0, c]], axis=0)
            low = jnp.concatenate([a_low, bbuf[a, 1, c]], axis=0)
            fsend[a, c] = dot(fmat[0], high) + dot(fmat[0], low) + dot(fmat[1], high)
        for i in range(NP - 1):
            copy2(a, i).start()
        fbuf[a, me] = fsend[a, :, pl.ds(pl.multiple_of(me * ZL, ZL), ZL), :]
        return carry

    lax.fori_loop(0, N, send_second, 0)

    def arrive_second(a, carry):
        for i in range(NP - 1):
            copy2(a, i).wait_recv()
        for c in range(3):
            for h in range(ZL // 8):
                rows = [fbuf[a, s, c, pl.ds(h * 8, 8), :] for s in range(NP)]
                for b, row in enumerate(block_transpose(rows)):
                    res[a * N + b, pl.ds(c * ZL + h * 8, 8), :] = row
        return carry

    lax.fori_loop(0, N, arrive_second, 0)
    r_copy = pltpu.make_async_copy(res, r_out, out_sem.at[0])
    r_copy.start()

    def halo(kind, way):
        return pltpu.make_async_remote_copy(
            src_ref=hsend.at[kind, way],
            dst_ref=hrecv.at[kind, way],
            send_sem=hs.at[kind, way],
            recv_sem=hr.at[kind, way],
            device_id=((up, down)[way], me),
            device_id_type=MESH,
        )

    def send_edges(v, kind):
        for a in range(N // 2):
            for way, b, t in ((0, N - 1, 4), (1, 0, 6)):
                hsend[kind, way, a] = pick(v[a * N + b], tables[t]) + pick(
                    v[(a + N // 2) * N + b], tables[t + 1]
                )
        halo(kind, 0).start()
        halo(kind, 1).start()

    def take_edges(kind):
        for way in (0, 1):
            halo(kind, way).wait_recv()
            there = (e > 0) if way == 0 else (e < NE - 1)
            for half in (0, 1):
                got = hrecv[kind, way].reshape(N // 2 * SYS, ED)
                got = pick(got, tables[8 + 2 * way + half])
                got = jnp.where(there, got, 0.0)
                edge[way, pl.ds(half * (N // 2), N // 2)] = got.reshape(N // 2, SYS, ED)

    def apply_local(v, q):
        face[0] = pick(v[(N - 1) * N : N * N].reshape(N * SYS, ED), tables[0]).reshape(N, SYS, ED)
        face[1] = pick(v[0:N].reshape(N * SYS, ED), tables[1]).reshape(N, SYS, ED)
        for a in range(N):
            face[2, a] = pick(v[a * N + N - 1], tables[2])
            face[3, a] = pick(v[a * N], tables[3])

        def tile(st, carry):
            rows = pl.ds(pl.multiple_of(st * 8, 8), 8)
            hm = hel[rows, :]
            kx = jnp.broadcast_to(geo[1:2, :], (8, ED))
            ky = jnp.broadcast_to(geo[2:3, :], (8, ED))
            for b in range(N):
                col = stiff_times([v[a * N + b, rows, :] for a in range(N)])
                scale_b = kx * float(WEIGHTS[b])
                for a in range(N):
                    q[a * N + b, rows, :] = scale_b * col[a]
            for a in range(N):
                vals = [v[a * N + b, rows, :] for b in range(N)]
                line = stiff_times(vals)
                scale_a = ky * float(WEIGHTS[a])
                hm_a = hm * float(WEIGHTS[a])
                for b in range(N):
                    out = q[a * N + b, rows, :] + scale_a * line[b]
                    out = out + (hm_a * float(WEIGHTS[b])) * vals[b]
                    if a == 0:
                        out = out + float(PEN * WEIGHTS[b]) * (vals[b] - face[0, b, rows, :])
                    if a == N - 1:
                        out = out + float(PEN * WEIGHTS[b]) * (vals[b] - face[1, b, rows, :])
                    if b == 0:
                        out = out + float(PEN * WEIGHTS[a]) * (vals[b] - face[2, a, rows, :])
                    if b == N - 1:
                        out = out + float(PEN * WEIGHTS[a]) * (vals[b] - face[3, a, rows, :])
                    q[a * N + b, rows, :] = out
            return carry

        lax.fori_loop(0, SYS // 8, tile, 0)

    def add_edges(q):
        for a in range(N):
            q[a * N] -= float(PEN * WEIGHTS[a]) * edge[0, a]
            q[a * N + N - 1] -= float(PEN * WEIGHTS[a]) * edge[1, a]

    send_edges(res, 0)
    apply_local(res, qv)
    send_edges(qv, 1)
    take_edges(0)
    add_edges(qv)
    q_copy = pltpu.make_async_copy(qv, q_out, out_sem.at[1])
    q_copy.start()
    apply_local(qv, pv)
    take_edges(1)
    inner = jnp.broadcast_to(lid < 64, (SYS, ED)) & (e > 0)
    outer = jnp.broadcast_to(lid >= 64, (SYS, ED)) & (e < NE - 1)
    for a in range(N):
        w_a = float(PEN * WEIGHTS[a])
        edge[0, a] -= jnp.where(inner, w_a * res[a * N], 0.0)
        edge[1, a] -= jnp.where(outer, w_a * res[a * N + N - 1], 0.0)
    add_edges(pv)
    p_copy = pltpu.make_async_copy(pv, p_out, out_sem.at[2])
    p_copy.start()

    def dot_tile(st, carry):
        rows = pl.ds(pl.multiple_of(st * 8, 8), 8)
        sums = [jnp.zeros((8, ED), F32) for _ in range(4)]
        for n in range(N * N):
            r_n, q_n, p_n = res[n, rows, :], qv[n, rows, :], pv[n, rows, :]
            for k, prod in enumerate((r_n * r_n, r_n * q_n, q_n * q_n, q_n * p_n)):
                sums[k] = sums[k] + prod
        for k in range(4):
            dots[k, rows, :] = sums[k]
        return carry

    lax.fori_loop(0, SYS // 8, dot_tile, 0)
    one_rows = jnp.ones((8, ED), F32)
    row8 = lax.broadcasted_iota(jnp.int32, (8, ED), 0)
    part = jnp.zeros((8, ED), F32)
    for k in range(4):
        summed = lax.dot_general(
            one_rows,
            dots[k],
            (((1,), (1,)), ((), ())),
            precision=lax.Precision.HIGHEST,
            preferred_element_type=F32,
        )
        part = jnp.where(row8 == k, summed, part)

    def reduce(value, buf, peers, send, recv):
        buf[0] = value
        copies = []
        for i, t in enumerate(peers):
            copies.append(
                pltpu.make_async_remote_copy(
                    src_ref=buf.at[0],
                    dst_ref=buf.at[i + 1],
                    send_sem=send.at[i],
                    recv_sem=recv.at[i],
                    device_id=(t, me),
                    device_id_type=MESH,
                )
            )
            copies[-1].start()
        for copy in copies:
            copy.wait_recv()
        total = buf[0]
        for i in range(len(peers)):
            total = total + buf[i + 1]
        return total, copies

    part, copies1 = reduce(part, rbuf1, x_peers, as1, ar1)
    part, copies2 = reduce(part, rbuf2, z_peers, as2, ar2)

    aa, bb, cc, ee = (part[k : k + 1, :] for k in range(4))
    alpha = aa / bb
    rr1 = alpha * alpha * cc - aa
    beta1 = 1.0 + rr1 / aa
    alpha1 = rr1 / (beta1 * beta1 * bb - 2.0 * beta1 * alpha * cc + alpha * alpha * ee)
    coef_s = alpha + alpha1 * beta1
    coef_t = alpha1 * alpha
    both = jnp.where(row8 == 0, coef_s, coef_t)
    both = jnp.where(lax.broadcasted_iota(jnp.int32, (8, ED), 1) < SYS, both, 0.0)
    both = jnp.transpose(jnp.concatenate([both] + [jnp.zeros((8, ED), F32)] * 15, axis=0))
    coef_out[0] = jnp.broadcast_to(both[0:SYS, 0:1], (SYS, ED))
    coef_out[1] = jnp.broadcast_to(both[0:SYS, 1:2], (SYS, ED))

    def drain(a, carry):
        for i in range(NP - 1):
            copy1(a, i).wait_send()
            copy2(a, i).wait_send()
        return carry

    lax.fori_loop(0, N, drain, 0)
    for kind in (0, 1):
        for way in (0, 1):
            halo(kind, way).wait_send()
    for copy in copies1 + copies2:
        copy.wait_send()
    r_copy.wait()
    q_copy.wait()
    p_copy.wait()


def finish_kernel(r, q, p, coef, x_out, r_out):
    s, t = coef[0], coef[1]
    for n in range(N * N):
        r_n, q_n, p_n = r[n], q[n], p[n]
        x_out[pl.ds(n, 8, stride=N * N), :] = s * r_n - t * q_n
        r_out[pl.ds(n, 8, stride=N * N), :] = r_n - s * q_n + t * p_n


def on_device(velocity, elem_scale, elem_ids, edge_blocks):
    vel = velocity.reshape(SYS * N * N, ED)
    wlane = jnp.asarray(np.repeat(WEIGHTS, EG)[None, :], F32)
    fmat = jnp.asarray(halves(mode_matrix()))
    dkron = jnp.asarray(halves(np.kron(DERIV.T, np.eye(EG))))
    dtab = np.zeros((N + 1, N))
    dtab[:N] = -WEIGHTS[:, None] * DERIV
    dtab[N] = WEIGHTS
    dtab = jnp.asarray(dtab, F32)
    vmem = pl.BlockSpec(memory_space=pltpu.VMEM)
    hbm = pl.BlockSpec(memory_space=pl.ANY)
    field = jax.ShapeDtypeStruct((N * N, SYS, ED), F32)
    dma = pltpu.SemaphoreType.DMA
    r0, q0, p0, coef = pl.pallas_call(
        kernel,
        out_shape=(field, field, field, jax.ShapeDtypeStruct((2, SYS, ED), F32)),
        in_specs=[hbm, vmem, vmem, vmem, vmem, vmem, pl.BlockSpec(memory_space=pltpu.SMEM)],
        out_specs=(hbm, hbm, hbm, vmem),
        scratch_shapes=[
            pltpu.VMEM((SYS * N * N, ED), F32),
            pltpu.VMEM((N, NP, 3, ZL, ED), F32),
            pltpu.VMEM((N, 3, Z, ED), F32),
            pltpu.VMEM((N, 3, Z, ED), F32),
            pltpu.VMEM((N, 2, 3, Z, ED), BF16),
            pltpu.VMEM((N, 3, Z, ED), F32),
            pltpu.VMEM((N, NP, 3, ZL, ED), F32),
            pltpu.VMEM((N * N, SYS, ED), F32),
            pltpu.VMEM((N * N, SYS, ED), F32),
            pltpu.VMEM((N * N, SYS, ED), F32),
            pltpu.VMEM((8, ED), F32),
            pltpu.VMEM((SYS, ED), F32),
            pltpu.VMEM((12, ED, ED), BF16),
            pltpu.VMEM((4, N, SYS, ED), F32),
            pltpu.VMEM((2, N, SYS, ED), F32),
            pltpu.VMEM((2, 2, N // 2, SYS, ED), F32),
            pltpu.VMEM((2, 2, N // 2, SYS, ED), F32),
            pltpu.VMEM((4, ED, ED), F32),
            pltpu.VMEM((NX, 8, ED), F32),
            pltpu.VMEM((NZ, 8, ED), F32),
            dma,
            dma((3,)),
            dma((N, NP - 1)),
            dma((N, NP - 1)),
            dma((N, NP - 1)),
            dma((N, NP - 1)),
            dma((2, 2)),
            dma((2, 2)),
            dma((NX - 1,)),
            dma((NX - 1,)),
            dma((NZ - 1,)),
            dma((NZ - 1,)),
        ],
        compiler_params=pltpu.CompilerParams(
            collective_id=0, has_side_effects=True, vmem_limit_bytes=48 * 1024 * 1024
        ),
        name="exchange_and_apply",
    )(vel, elem_scale, elem_ids, wlane, fmat, dkron, dtab)

    block = pl.BlockSpec((N * N, 8, ED), lambda i: (0, i, 0))
    out_block = pl.BlockSpec((8 * N * N, ED), lambda i: (i, 0))
    flat = jax.ShapeDtypeStruct((SYS * N * N, ED), F32)
    new, left = pl.pallas_call(
        finish_kernel,
        grid=(SYS // 8,),
        out_shape=(flat, flat),
        in_specs=[block, block, block, pl.BlockSpec((2, 8, ED), lambda i: (0, i, 0))],
        out_specs=(out_block, out_block),
        compiler_params=pltpu.CompilerParams(vmem_limit_bytes=16 * 1024 * 1024),
        name="finish",
    )(r0, q0, p0, coef)
    shape = (3, ZL, N, N, ED)
    return new.reshape(shape), left.reshape(shape)


def solution(mesh):
    in_specs = (
        P(None, "plane", None, None, "elem"),
        P(None, "elem"),
        P("elem", None),
        P("elem", None, None),
    )
    out_specs = (P(None, "plane", None, None, "elem"), P(None, "plane", None, None, "elem"))
    return jax.shard_map(
        on_device, mesh=mesh, in_specs=in_specs, out_specs=out_specs, check_vma=False
    )
```

```python
import functools
import math

import jax
import jax.numpy as jnp
import ml_dtypes
import numpy as np
from jax import lax
from jax.experimental import pallas as pl
from jax.experimental.pallas import tpu as pltpu
from jax.sharding import PartitionSpec as P

MESH = pl.DeviceIdType.MESH
F32 = jnp.float32
BF16 = jnp.bfloat16

N = 8
ED = 128
Z = 128
NP = 8
ZL = Z // NP
EG = ED // NP
SYS = 3 * ZL
NX = 4
NZ = 8
NE = NX * NZ
PAIRS = N // 2
PEN = 8.0
ROW_W = N * N
ROW_LANE = ROW_W + N
ROWS = 80
LAM = 4.0
STEP = 0.1


def node_tables():
    degree = N - 1
    points = -np.cos(np.pi * np.arange(N) / degree)
    scales = np.ones(N)
    scales[0] = 2.0
    scales[-1] = 2.0
    bary = (-1.0) ** np.arange(N) / scales
    deriv = np.zeros((N, N))
    for i in range(N):
        for j in range(N):
            if i != j:
                deriv[i, j] = bary[j] / bary[i] / (points[i] - points[j])
        deriv[i, i] = -np.sum(deriv[i])
    weights = np.zeros(N)
    for i in range(N):
        running = 0.0
        for k in range(1, degree // 2 + 1):
            factor = 1.0 if 2 * k == degree else 2.0
            running += factor / (4.0 * k * k - 1.0) * np.cos(2.0 * np.pi * i * k / degree)
        weights[i] = (1.0 if i in (0, degree) else 2.0) / degree * (1.0 - running)
    stiff = deriv.T @ (weights[:, None] * deriv)
    return deriv, weights, stiff


def mode_matrix():
    slots = np.arange(Z)
    harmonic = slots // 2
    angles = 2.0 * math.pi / Z * (harmonic[:, None] * slots[None, :] % Z)
    four = np.where((slots % 2 == 0)[:, None], np.cos(angles), np.sin(angles)) * (2.0 / Z)
    four[0] = 1.0 / Z
    four[1] = np.where(slots % 2 == 0, 1.0, -1.0) / Z
    dz = np.zeros((Z, Z))
    wave = STEP * np.arange(Z // 2)
    dz[0::2] = wave[:, None] * four[1::2]
    dz[1::2] = -wave[:, None] * four[0::2]
    return np.concatenate([four, -dz], axis=1)


def halves(table):
    high = table.astype(np.float32).astype(ml_dtypes.bfloat16)
    low = (table - high.astype(np.float64)).astype(np.float32).astype(ml_dtypes.bfloat16)
    return np.stack([high, low])


DERIV, WEIGHTS, STIFF = node_tables()


def split(x):
    high = x.astype(BF16)
    return high, (x - high.astype(F32)).astype(BF16)


def dot(x, y):
    return jnp.dot(x, y, preferred_element_type=F32)


def pick(x, table):
    high, low = split(x)
    return dot(high, table) + dot(low, table)


def block_transpose(rows):
    rows = list(rows)
    lane = lax.broadcasted_iota(jnp.int32, rows[0].shape, rows[0].ndim - 1) // EG
    for d in (1, 2, 4):
        clear = (lane & d) == 0
        for i in range(NP):
            if i & d == 0:
                x, y = rows[i], rows[i + d]
                axis = x.ndim - 1
                rows[i] = jnp.where(clear, x, pltpu.roll(y, EG * d, axis))
                rows[i + d] = jnp.where(clear, pltpu.roll(x, ED - EG * d, axis), y)
    return rows


def stiff_times(v):
    even = [v[p] + v[N - 1 - p] for p in range(N // 2)]
    odd = [v[p] - v[N - 1 - p] for p in range(N // 2)]
    out = [None] * N
    for a in range(N // 2):
        s = [0.5 * (STIFF[a, p] + STIFF[a, N - 1 - p]) for p in range(N // 2)]
        t = [0.5 * (STIFF[a, p] - STIFF[a, N - 1 - p]) for p in range(N // 2)]
        e = sum(float(s[p]) * even[p] for p in range(1, N // 2)) + float(s[0]) * even[0]
        o = sum(float(t[p]) * odd[p] for p in range(1, N // 2)) + float(t[0]) * odd[0]
        out[a] = e + o
        out[N - 1 - a] = e - o
    return out


def kernel(
    vel,
    scale_in,
    ids_in,
    rows_in,
    mats_in,
    res,
    qv,
    pv,
    coef_out,
    vin,
    scale,
    ids,
    ctab,
    mats,
    xsend,
    xbuf,
    acc,
    bbuf,
    fsend,
    fbuf,
    geo,
    hel,
    tables,
    face,
    edge,
    hsend,
    hrecv,
    dots,
    rbuf,
    in_sem,
    s1,
    r1,
    s2,
    r2,
    hs,
    hr,
    rs,
    rr,
):
    e = lax.axis_index("elem")
    me = lax.axis_index("plane")
    y, core = me // 2, lax.rem(me, 2)
    z, x = e // NX, lax.rem(e, NX)
    plane_offsets = [(dy, dc) for dy in (2, 1, 3, 0) for dc in (0, 1) if (dy, dc) != (0, 0)]
    plane_peers = [lax.rem(y + dy, 4) * 2 + lax.rem(core + dc, 2) for dy, dc in plane_offsets]
    elem_peers = [
        lax.rem(z + dz, NZ) * NX + lax.rem(x + dx, NX)
        for dz in (4, 3, 5, 2, 6, 1, 7, 0)
        for dx in (2, 1, 3, 0)
        if (dz, dx) != (0, 0)
    ]
    up, down = lax.rem(e + 1, NE), lax.rem(e + NE - 1, NE)

    pairs = ((vel, vin), (scale_in, scale), (ids_in, ids), (rows_in, ctab), (mats_in, mats))
    loads = [pltpu.make_async_copy(src, dst, in_sem.at[i]) for i, (src, dst) in enumerate(pairs)]
    for load in loads:
        load.start()
    barrier = pltpu.get_barrier_semaphore()
    for t in plane_peers:
        pl.semaphore_signal(barrier, inc=1, device_id=(e, t), device_id_type=MESH)
    for t in elem_peers:
        pl.semaphore_signal(barrier, inc=1, device_id=(t, me), device_id_type=MESH)

    for load in loads[1:]:
        load.wait()

    lid = ids[...] & (ED - 1)
    growth = 1.0 + 2.0 * (ids[...] // 64).astype(F32) / 63.0
    circ = scale[0:1, :] * growth
    radial = scale[1:2, :]
    geo[0:1, :] = circ * radial
    geo[1:2, :] = radial / circ
    geo[2:3, :] = circ / radial
    lane_row = lax.broadcasted_iota(jnp.int32, (1, ED), 1)
    for k, val in ((3, circ), (4, radial)):
        val = pltpu.roll(jnp.broadcast_to(val, (8, ED)), lax.rem(ED - EG * me, ED), 1)
        val = jnp.where(lax.broadcasted_iota(jnp.int32, (8, ED), 1) < EG, val, 0.0)
        for d in (1, 2, 4):
            val = val + pltpu.roll(val, EG * d, 1)
        geo[k : k + 1, :] = val[0:1, :]
    wl = ctab[ROW_LANE : ROW_LANE + 1, :]
    g_circ, g_radial = geo[3:4, :], geo[4:5, :]
    geo[5:6, :] = g_circ * g_radial * wl
    geo[6:7, :] = g_circ * wl
    geo[7:8, :] = g_radial * wl
    loads[0].wait()
    pl.semaphore_wait(barrier, NP - 1 + NE - 1)

    def copy1(a, i):
        t = plane_peers[i]
        return pltpu.make_async_remote_copy(
            src_ref=xsend.at[a, t],
            dst_ref=xbuf.at[a, :, pl.ds(pl.multiple_of(me * ZL, ZL), ZL), :],
            send_sem=s1.at[a, i],
            recv_sem=r1.at[a, i],
            device_id=(e, t),
            device_id_type=MESH,
        )

    def copy2(c, pair, i):
        t = plane_peers[i]
        return pltpu.make_async_remote_copy(
            src_ref=fsend.at[c, pl.ds(2 * pair, 2), pl.ds(pl.multiple_of(t * ZL, ZL), ZL), :],
            dst_ref=fbuf.at[c, me, pl.ds(2 * pair, 2)],
            send_sem=s2.at[c, pair, i],
            recv_sem=r2.at[c, pair, i],
            device_id=(e, t),
            device_id_type=MESH,
        )

    def send_first(a, carry):
        for c in range(3):
            for h in range(ZL // 8):
                base = (c * ZL + h * 8) * N * N + a * N
                rows = [vin[pl.ds(base + b, 8, stride=N * N), :] for b in range(N)]
                for q, row in enumerate(block_transpose(rows)):
                    xsend[a, q, c, pl.ds(h * 8, 8), :] = row
        for i in range(NP - 1):
            copy1(a, i).start()
        mine = pl.ds(pl.multiple_of(me * ZL, ZL), ZL)
        xbuf[a, :, mine, :] = xsend[a, me]
        return carry

    lax.fori_loop(0, N, send_first, 0)

    acc[...] = jnp.zeros_like(acc)
    dots[...] = jnp.zeros_like(dots)
    row_i = lax.broadcasted_iota(jnp.int32, (ED, ED), 0)
    lane_i = lax.broadcasted_iota(jnp.int32, (ED, ED), 1)
    lid_l = jnp.broadcast_to(lid, (ED, ED))
    lid_t = jnp.transpose(lid_l.astype(F32)).astype(jnp.int32)

    def ones(where):
        return jnp.where(where, 1.0, 0.0).astype(BF16)

    tables[0] = ones(lid_t == ((lid_l & 64) | ((lid_l + 63) & 63)))
    tables[1] = ones(lid_t == ((lid_l & 64) | ((lid_l + 1) & 63)))
    tables[2] = ones((lid_t == (lid_l ^ 64)) & (lid_l >= 64))
    tables[3] = ones((lid_t == (lid_l ^ 64)) & (lid_l < 64))
    tables[4] = ones(lid_t == lane_i + 64)
    tables[5] = ones((lid_t == lane_i) & (lane_i >= 64))
    tables[6] = ones((lid_t == lane_i) & (lane_i < 64))
    tables[7] = ones(lid_t + 64 == lane_i)
    tables[8] = ones((row_i == lid_l) & (lid_l < 64))
    tables[9] = ones(row_i == lid_l + 64)
    tables[10] = ones(row_i + 64 == lid_l)
    tables[11] = ones((row_i == lid_l) & (lid_l >= 64))
    slot = me * ZL + (lax.broadcasted_iota(jnp.int32, (SYS, ED), 0) & (ZL - 1))
    kappa = jnp.where(slot == 1, Z // 2, slot // 2).astype(F32)
    hel[...] = (LAM + (STEP * kappa) * (STEP * kappa)) * geo[0:1, :]

    def arrive_first(p, carry):
        for i in range(NP - 1):
            copy1(p, i).wait_recv()
        w_p = ctab[pl.ds(ROW_W + p, 1), :]
        mass = geo[5:6, :] * w_p
        g_y = geo[6:7, :] * w_p
        g_x = geo[7:8, :]
        for c in range(3):
            fy_high, fy_low = split(xbuf[p, 1] * xbuf[p, c])
            dy = dot(fy_high, mats[4]) + dot(fy_low, mats[4]) + dot(fy_high, mats[5])
            acc[p, c] += (LAM * mass) * xbuf[p, c] - g_y * dy
            b_high, b_low = split(mass * (xbuf[p, 2] * xbuf[p, c]))
            bbuf[p, 0, c] = b_high
            bbuf[p, 1, c] = b_low
            for h in range(4):
                rows = pl.ds(h * 32, 32)
                fx = g_x * (xbuf[p, 0, rows, :] * xbuf[p, c, rows, :])
                for a in range(N):
                    acc[a, c, rows, :] += ctab[pl.ds(p * N + a, 1), :] * fx
        return carry

    lax.fori_loop(0, N, arrive_first, 0)

    f_high = jnp.concatenate([mats[0], mats[1]], axis=1)
    f_low = jnp.concatenate([mats[2], mats[3]], axis=1)

    def send_second(step, carry):
        c, pair = step // PAIRS, lax.rem(step, PAIRS)
        for k in (0, 1):
            a = 2 * pair + k
            a_high, a_low = split(acc[a, c])
            high = jnp.concatenate([a_high, bbuf[a, 0, c]], axis=0)
            low = jnp.concatenate([a_low, bbuf[a, 1, c]], axis=0)
            fsend[c, a] = dot(f_high, high) + dot(f_high, low) + dot(f_low, high)
        for i in range(NP - 1):
            copy2(c, pair, i).start()
        mine = pl.ds(pl.multiple_of(me * ZL, ZL), ZL)
        fbuf[c, me, pl.ds(2 * pair, 2)] = fsend[c, pl.ds(2 * pair, 2), mine, :]
        return carry

    lax.fori_loop(0, 3 * PAIRS, send_second, 0)

    def sys_rows(c):
        return pl.ds(pl.multiple_of(c * ZL, ZL), ZL)

    def halo(c, kind, way):
        return pltpu.make_async_remote_copy(
            src_ref=hsend.at[c, kind, way],
            dst_ref=hrecv.at[c, kind, way],
            send_sem=hs.at[c, kind, way],
            recv_sem=hr.at[c, kind, way],
            device_id=((up, down)[way], me),
            device_id_type=MESH,
        )

    def side(v, rows, b, first, count):
        return jnp.concatenate([v[a * N + b, rows, :] for a in range(first, first + count)], axis=0)

    def send_edges(v, c, kind):
        rows = sys_rows(c)
        for way, b, t in ((0, N - 1, 4), (1, 0, 6)):
            got = pick(side(v, rows, b, 0, N // 2), tables[t])
            got = got + pick(side(v, rows, b, N // 2, N // 2), tables[t + 1])
            hsend[c, kind, way] = got.reshape(N // 2, ZL, ED)
            halo(c, kind, way).start()

    def take_edges(c, kind):
        for way in (0, 1):
            halo(c, kind, way).wait_recv()
            there = (e > 0) if way == 0 else (e < NE - 1)
            for half in (0, 1):
                got = hrecv[c, kind, way].reshape(N // 2 * ZL, ED)
                got = pick(got, tables[8 + 2 * way + half])
                got = jnp.where(there, got, 0.0)
                edge[way, pl.ds(half * (N // 2), N // 2)] = got.reshape(N // 2, ZL, ED)

    def apply_local(v, q, c):
        sys = sys_rows(c)
        shape = (N, ZL, ED)
        face[0] = pick(v[(N - 1) * N : N * N, sys, :].reshape(N * ZL, ED), tables[0]).reshape(shape)
        face[1] = pick(v[0:N, sys, :].reshape(N * ZL, ED), tables[1]).reshape(shape)
        face[2] = pick(side(v, sys, N - 1, 0, N), tables[2]).reshape(shape)
        face[3] = pick(side(v, sys, 0, 0, N), tables[3]).reshape(shape)

        def tile(h, carry):
            rows = pl.ds(pl.multiple_of(c * ZL + h * 8, 8), 8)
            frows = pl.ds(pl.multiple_of(h * 8, 8), 8)
            hm = hel[rows, :]
            kx = jnp.broadcast_to(geo[1:2, :], (8, ED))
            ky = jnp.broadcast_to(geo[2:3, :], (8, ED))
            for b in range(N):
                col = stiff_times([v[a * N + b, rows, :] for a in range(N)])
                scale_b = kx * float(WEIGHTS[b])
                for a in range(N):
                    q[a * N + b, rows, :] = scale_b * col[a]
            for a in range(N):
                vals = [v[a * N + b, rows, :] for b in range(N)]
                line = stiff_times(vals)
                scale_a = ky * float(WEIGHTS[a])
                hm_a = hm * float(WEIGHTS[a])
                for b in range(N):
                    out = q[a * N + b, rows, :] + scale_a * line[b]
                    out = out + (hm_a * float(WEIGHTS[b])) * vals[b]
                    if a == 0:
                        out = out + float(PEN * WEIGHTS[b]) * (vals[b] - face[0, b, frows, :])
                    if a == N - 1:
                        out = out + float(PEN * WEIGHTS[b]) * (vals[b] - face[1, b, frows, :])
                    if b == 0:
                        out = out + float(PEN * WEIGHTS[a]) * (vals[b] - face[2, a, frows, :])
                    if b == N - 1:
                        out = out + float(PEN * WEIGHTS[a]) * (vals[b] - face[3, a, frows, :])
                    q[a * N + b, rows, :] = out
            return carry

        lax.fori_loop(0, ZL // 8, tile, 0)

    def add_edges(q, c):
        rows = sys_rows(c)
        for a in range(N):
            q[a * N, rows, :] -= float(PEN * WEIGHTS[a]) * edge[0, a]
            q[a * N + N - 1, rows, :] -= float(PEN * WEIGHTS[a]) * edge[1, a]

    def arrive_second(c):
        def row(a, carry):
            for h in range(ZL // 8):
                rows = [fbuf[c, s, a, pl.ds(h * 8, 8), :] for s in range(NP)]
                for b, line in enumerate(block_transpose(rows)):
                    res[a * N + b, pl.ds(pl.multiple_of(c * ZL + h * 8, 8), 8), :] = line
            return carry

        def pair(k, carry):
            for i in range(NP - 1):
                copy2(c, k, i).wait_recv()
            return lax.fori_loop(2 * k, 2 * k + 2, row, carry)

        lax.fori_loop(0, PAIRS, pair, 0)

    def begin(c):
        arrive_second(c)
        send_edges(res, c, 0)
        apply_local(res, qv, c)
        send_edges(qv, c, 1)

    def end(c):
        take_edges(c, 0)
        add_edges(qv, c)
        apply_local(qv, pv, c)
        take_edges(c, 1)
        rows = sys_rows(c)
        inner = jnp.broadcast_to(lid < 64, (ZL, ED)) & (e > 0)
        outer = jnp.broadcast_to(lid >= 64, (ZL, ED)) & (e < NE - 1)
        for a in range(N):
            w_a = float(PEN * WEIGHTS[a])
            edge[0, a] -= jnp.where(inner, w_a * res[a * N, rows, :], 0.0)
            edge[1, a] -= jnp.where(outer, w_a * res[a * N + N - 1, rows, :], 0.0)
        add_edges(pv, c)

        def dot_tile(h, carry):
            rows = pl.ds(pl.multiple_of(c * ZL + h * 8, 8), 8)
            sums = [jnp.zeros((8, ED), F32) for _ in range(4)]
            for n in range(N * N):
                r_n, q_n, p_n = res[n, rows, :], qv[n, rows, :], pv[n, rows, :]
                for k, prod in enumerate((r_n * r_n, r_n * q_n, q_n * q_n, q_n * p_n)):
                    sums[k] = sums[k] + prod
            for k in range(4):
                dots[k, rows, :] = sums[k]
            return carry

        lax.fori_loop(0, ZL // 8, dot_tile, 0)

    begin(0)

    def component(c, carry):
        begin(c)
        end(c - 1)
        return carry

    lax.fori_loop(1, 3, component, 0)
    end(2)

    one_rows = jnp.ones((8, ED), F32)
    row8 = lax.broadcasted_iota(jnp.int32, (8, ED), 0)
    part = jnp.zeros((8, ED), F32)
    for k in range(4):
        summed = lax.dot_general(
            one_rows,
            dots[k],
            (((1,), (1,)), ((), ())),
            precision=lax.Precision.HIGHEST,
            preferred_element_type=F32,
        )
        part = jnp.where(row8 == k, summed, part)

    rbuf[0] = part

    def spread(i):
        return pltpu.make_async_remote_copy(
            src_ref=rbuf.at[0],
            dst_ref=rbuf.at[i + 1],
            send_sem=rs.at[i],
            recv_sem=rr.at[i],
            device_id=(elem_peers[i], me),
            device_id_type=MESH,
        )

    for i in range(NE - 1):
        spread(i).start()
    for i in range(NE - 1):
        spread(i).wait_recv()
    part = jnp.sum(rbuf[...], axis=0)

    aa, bb, cc, ee = (part[k : k + 1, :] for k in range(4))
    alpha = aa / bb
    rr1 = alpha * alpha * cc - aa
    beta1 = 1.0 + rr1 / aa
    alpha1 = rr1 / (beta1 * beta1 * bb - 2.0 * beta1 * alpha * cc + alpha * alpha * ee)
    coef_s = alpha + alpha1 * beta1
    coef_t = alpha1 * alpha
    both = jnp.where(row8 == 0, coef_s, coef_t)
    both = jnp.where(lax.broadcasted_iota(jnp.int32, (8, ED), 1) < SYS, both, 0.0)
    both = jnp.transpose(jnp.concatenate([both] + [jnp.zeros((8, ED), F32)] * 15, axis=0))
    coef_out[0] = jnp.broadcast_to(both[0:SYS, 0:1], (SYS, ED))
    coef_out[1] = jnp.broadcast_to(both[0:SYS, 1:2], (SYS, ED))

    def drain(a, carry):
        for i in range(NP - 1):
            copy1(a, i).wait_send()
        return carry

    def drain2(step, carry):
        for i in range(NP - 1):
            copy2(step // PAIRS, lax.rem(step, PAIRS), i).wait_send()
        return carry

    def drain3(c, carry):
        for kind in (0, 1):
            for way in (0, 1):
                halo(c, kind, way).wait_send()
        return carry

    lax.fori_loop(0, N, drain, 0)
    lax.fori_loop(0, 3 * PAIRS, drain2, 0)
    lax.fori_loop(0, 3, drain3, 0)
    for i in range(NE - 1):
        spread(i).wait_send()


def finish_kernel(r, q, p, coef, x_out, r_out, xs, rs, sem):
    def tile(st, carry):
        rows = pl.ds(pl.multiple_of(st * 8, 8), 8)
        s, t = coef[0, rows, :], coef[1, rows, :]
        for n in range(N * N):
            r_n, q_n, p_n = r[n, rows, :], q[n, rows, :], p[n, rows, :]
            xs[st, pl.ds(n, 8, stride=N * N), :] = s * r_n - t * q_n
            rs[st, pl.ds(n, 8, stride=N * N), :] = r_n - s * q_n + t * p_n
        for copy in out_copies(st):
            copy.start()
        return carry

    def out_copies(st):
        return (
            pltpu.make_async_copy(xs.at[st], x_out.at[st], sem.at[st, 0]),
            pltpu.make_async_copy(rs.at[st], r_out.at[st], sem.at[st, 1]),
        )

    def drain(st, carry):
        for copy in out_copies(st):
            copy.wait()
        return carry

    lax.fori_loop(0, SYS // 8, tile, 0)
    lax.fori_loop(0, SYS // 8, drain, 0)


def on_device(velocity, elem_scale, elem_ids, edge_blocks):
    vel = velocity.reshape(SYS * N * N, ED)
    rows = np.zeros((ROWS, ED))
    rows[: N * N] = (-WEIGHTS[:, None] * DERIV).T.reshape(N * N, 1)
    rows[ROW_W : ROW_W + N] = WEIGHTS[:, None]
    rows[ROW_LANE] = np.repeat(WEIGHTS, EG)
    rows = jnp.asarray(rows, F32)
    four = halves(mode_matrix()).reshape(2, Z, 2, Z).transpose(0, 2, 1, 3).reshape(4, Z, Z)
    mats = jnp.asarray(np.concatenate([four, halves(np.kron(DERIV.T, np.eye(EG)))]))
    operands = (vel, elem_scale, elem_ids, rows, mats)
    vmem = pl.BlockSpec(memory_space=pltpu.VMEM)
    hbm = pl.BlockSpec(memory_space=pltpu.HBM)
    field = jax.ShapeDtypeStruct((N * N, SYS, ED), F32)
    dma = pltpu.SemaphoreType.DMA
    r0, q0, p0, coef = pl.pallas_call(
        kernel,
        out_shape=(field, field, field, jax.ShapeDtypeStruct((2, SYS, ED), F32)),
        in_specs=[hbm] * 5,
        out_specs=(vmem,) * 4,
        scratch_shapes=[
            pltpu.VMEM((SYS * N * N, ED), F32),
            pltpu.VMEM((2, ED), F32),
            pltpu.VMEM((1, ED), jnp.int32),
            pltpu.VMEM((ROWS, ED), F32),
            pltpu.VMEM((6, ED, ED), BF16),
            pltpu.VMEM((N, NP, 3, ZL, ED), F32),
            pltpu.VMEM((N, 3, Z, ED), F32),
            pltpu.VMEM((N, 3, Z, ED), F32),
            pltpu.VMEM((N, 2, 3, Z, ED), BF16),
            pltpu.VMEM((3, N, Z, ED), F32),
            pltpu.VMEM((3, NP, N, ZL, ED), F32),
            pltpu.VMEM((8, ED), F32),
            pltpu.VMEM((SYS, ED), F32),
            pltpu.VMEM((12, ED, ED), BF16),
            pltpu.VMEM((4, N, ZL, ED), F32),
            pltpu.VMEM((2, N, ZL, ED), F32),
            pltpu.VMEM((3, 2, 2, N // 2, ZL, ED), F32),
            pltpu.VMEM((3, 2, 2, N // 2, ZL, ED), F32),
            pltpu.VMEM((4, ED, ED), F32),
            pltpu.VMEM((NE, 8, ED), F32),
            dma((5,)),
            dma((N, NP - 1)),
            dma((N, NP - 1)),
            dma((3, PAIRS, NP - 1)),
            dma((3, PAIRS, NP - 1)),
            dma((3, 2, 2)),
            dma((3, 2, 2)),
            dma((NE - 1,)),
            dma((NE - 1,)),
        ],
        compiler_params=pltpu.CompilerParams(
            collective_id=0, has_side_effects=True, vmem_limit_bytes=48 * 1024 * 1024
        ),
        name="exchange_and_apply",
    )(*[pltpu.with_memory_space_constraint(v, pltpu.HBM) for v in operands])

    flat = jax.ShapeDtypeStruct((SYS // 8, 8 * N * N, ED), F32)
    new, left = pl.pallas_call(
        finish_kernel,
        out_shape=(flat, flat),
        in_specs=[vmem] * 4,
        out_specs=(hbm, hbm),
        scratch_shapes=[
            pltpu.VMEM(flat.shape, F32),
            pltpu.VMEM(flat.shape, F32),
            dma((SYS // 8, 2)),
        ],
        compiler_params=pltpu.CompilerParams(vmem_limit_bytes=16 * 1024 * 1024),
        name="finish",
    )(r0, q0, p0, coef)
    shape = (3, ZL, N, N, ED)
    return new.reshape(shape), left.reshape(shape)


def solution(mesh):
    in_specs = (
        P(None, "plane", None, None, "elem"),
        P(None, "elem"),
        P("elem", None),
        P("elem", None, None),
    )
    out_specs = (P(None, "plane", None, None, "elem"), P(None, "plane", None, None, "elem"))
    return jax.shard_map(
        on_device, mesh=mesh, in_specs=in_specs, out_specs=out_specs, check_vma=False
    )
```

```python
import functools
import math

import jax
import jax.numpy as jnp
import ml_dtypes
import numpy as np
from jax import lax
from jax.experimental import pallas as pl
from jax.experimental.pallas import tpu as pltpu
from jax.sharding import PartitionSpec as P

MESH = pl.DeviceIdType.MESH
F32 = jnp.float32
BF16 = jnp.bfloat16

N = 8
ED = 128
Z = 128
NP = 8
ZL = Z // NP
EG = ED // NP
SYS = 3 * ZL
NX = 4
NZ = 8
NE = NX * NZ
PAIRS = N // 2
PEN = 8.0
ROW_W = N * N
ROW_LANE = ROW_W + N
ROWS = 80
LAM = 4.0
STEP = 0.1


def node_tables():
    degree = N - 1
    points = -np.cos(np.pi * np.arange(N) / degree)
    scales = np.ones(N)
    scales[0] = 2.0
    scales[-1] = 2.0
    bary = (-1.0) ** np.arange(N) / scales
    deriv = np.zeros((N, N))
    for i in range(N):
        for j in range(N):
            if i != j:
                deriv[i, j] = bary[j] / bary[i] / (points[i] - points[j])
        deriv[i, i] = -np.sum(deriv[i])
    weights = np.zeros(N)
    for i in range(N):
        running = 0.0
        for k in range(1, degree // 2 + 1):
            factor = 1.0 if 2 * k == degree else 2.0
            running += factor / (4.0 * k * k - 1.0) * np.cos(2.0 * np.pi * i * k / degree)
        weights[i] = (1.0 if i in (0, degree) else 2.0) / degree * (1.0 - running)
    stiff = deriv.T @ (weights[:, None] * deriv)
    return deriv, weights, stiff


def mode_matrix():
    slots = np.arange(Z)
    harmonic = slots // 2
    angles = 2.0 * math.pi / Z * (harmonic[:, None] * slots[None, :] % Z)
    four = np.where((slots % 2 == 0)[:, None], np.cos(angles), np.sin(angles)) * (2.0 / Z)
    four[0] = 1.0 / Z
    four[1] = np.where(slots % 2 == 0, 1.0, -1.0) / Z
    dz = np.zeros((Z, Z))
    wave = STEP * np.arange(Z // 2)
    dz[0::2] = wave[:, None] * four[1::2]
    dz[1::2] = -wave[:, None] * four[0::2]
    return np.concatenate([four, -dz], axis=1)


def halves(table):
    high = table.astype(np.float32).astype(ml_dtypes.bfloat16)
    low = (table - high.astype(np.float64)).astype(np.float32).astype(ml_dtypes.bfloat16)
    return np.stack([high, low])


DERIV, WEIGHTS, STIFF = node_tables()


def split(x):
    high = x.astype(BF16)
    return high, (x - high.astype(F32)).astype(BF16)


def dot(x, y):
    return jnp.dot(x, y, preferred_element_type=F32)


def pick(x, table):
    high, low = split(x)
    return dot(high, table) + dot(low, table)


def block_transpose(rows):
    rows = list(rows)
    lane = lax.broadcasted_iota(jnp.int32, rows[0].shape, rows[0].ndim - 1) // EG
    for d in (1, 2, 4):
        clear = (lane & d) == 0
        for i in range(NP):
            if i & d == 0:
                x, y = rows[i], rows[i + d]
                axis = x.ndim - 1
                rows[i] = jnp.where(clear, x, pltpu.roll(y, EG * d, axis))
                rows[i + d] = jnp.where(clear, pltpu.roll(x, ED - EG * d, axis), y)
    return rows


def stiff_times(v, wanted):
    even = [v[p] + v[N - 1 - p] for p in range(N // 2)]
    odd = [v[p] - v[N - 1 - p] for p in range(N // 2)]
    out = [None] * N
    for a in wanted:
        s = [0.5 * (STIFF[a, p] + STIFF[a, N - 1 - p]) for p in range(N // 2)]
        t = [0.5 * (STIFF[a, p] - STIFF[a, N - 1 - p]) for p in range(N // 2)]
        e = sum(float(s[p]) * even[p] for p in range(1, N // 2)) + float(s[0]) * even[0]
        o = sum(float(t[p]) * odd[p] for p in range(1, N // 2)) + float(t[0]) * odd[0]
        out[a] = e + o
        out[N - 1 - a] = e - o
    return out


def kernel(
    vel,
    scale_in,
    ids_in,
    rows_in,
    mats_in,
    res,
    qv,
    pv,
    coef_out,
    vin,
    scale,
    ids,
    ctab,
    mats,
    xsend,
    xbuf,
    acc,
    bbuf,
    fsend,
    fbuf,
    geo,
    hel,
    tables,
    face,
    edge,
    rsend,
    rrecv,
    qsend,
    qrecv,
    dots,
    rbuf,
    in_sem,
    s1,
    r1,
    s2,
    r2,
    hs1,
    hr1,
    hs2,
    hr2,
    rs,
    rr,
):
    e = lax.axis_index("elem")
    me = lax.axis_index("plane")
    y, core = me // 2, lax.rem(me, 2)
    z, x = e // NX, lax.rem(e, NX)
    plane_offsets = [(dy, dc) for dy in (2, 1, 3, 0) for dc in (0, 1) if (dy, dc) != (0, 0)]
    plane_peers = [lax.rem(y + dy, 4) * 2 + lax.rem(core + dc, 2) for dy, dc in plane_offsets]
    elem_peers = [
        lax.rem(z + dz, NZ) * NX + lax.rem(x + dx, NX)
        for dz in (4, 3, 5, 2, 6, 1, 7, 0)
        for dx in (2, 1, 3, 0)
        if (dz, dx) != (0, 0)
    ]
    up, down = lax.rem(e + 1, NE), lax.rem(e + NE - 1, NE)

    pairs = ((vel, vin), (scale_in, scale), (ids_in, ids), (rows_in, ctab), (mats_in, mats))
    loads = [pltpu.make_async_copy(src, dst, in_sem.at[i]) for i, (src, dst) in enumerate(pairs)]
    for load in loads:
        load.start()
    barrier = pltpu.get_barrier_semaphore()
    for t in plane_peers:
        pl.semaphore_signal(barrier, inc=1, device_id=(e, t), device_id_type=MESH)
    for t in elem_peers:
        pl.semaphore_signal(barrier, inc=1, device_id=(t, me), device_id_type=MESH)

    for load in loads[1:]:
        load.wait()

    lid = ids[...] & (ED - 1)
    growth = 1.0 + 2.0 * (ids[...] // 64).astype(F32) / 63.0
    circ = scale[0:1, :] * growth
    radial = scale[1:2, :]
    geo[0:1, :] = circ * radial
    geo[1:2, :] = radial / circ
    geo[2:3, :] = circ / radial
    lane_row = lax.broadcasted_iota(jnp.int32, (1, ED), 1)
    for k, val in ((3, circ), (4, radial)):
        val = pltpu.roll(jnp.broadcast_to(val, (8, ED)), lax.rem(ED - EG * me, ED), 1)
        val = jnp.where(lax.broadcasted_iota(jnp.int32, (8, ED), 1) < EG, val, 0.0)
        for d in (1, 2, 4):
            val = val + pltpu.roll(val, EG * d, 1)
        geo[k : k + 1, :] = val[0:1, :]
    wl = ctab[ROW_LANE : ROW_LANE + 1, :]
    g_circ, g_radial = geo[3:4, :], geo[4:5, :]
    geo[5:6, :] = g_circ * g_radial * wl
    geo[6:7, :] = g_circ * wl
    geo[7:8, :] = g_radial * wl

    def copy1(a, i):
        t = plane_peers[i]
        return pltpu.make_async_remote_copy(
            src_ref=xsend.at[a, t],
            dst_ref=xbuf.at[a, :, pl.ds(pl.multiple_of(me * ZL, ZL), ZL), :],
            send_sem=s1.at[a, i],
            recv_sem=r1.at[a, i],
            device_id=(e, t),
            device_id_type=MESH,
        )

    def copy2(c, pair, i):
        t = plane_peers[i]
        return pltpu.make_async_remote_copy(
            src_ref=fsend.at[c, pl.ds(2 * pair, 2), pl.ds(pl.multiple_of(t * ZL, ZL), ZL), :],
            dst_ref=fbuf.at[c, me, pl.ds(2 * pair, 2)],
            send_sem=s2.at[c, pair, i],
            recv_sem=r2.at[c, pair, i],
            device_id=(e, t),
            device_id_type=MESH,
        )

    def pack_first(a):
        for c in range(3):
            for h in range(ZL // 8):
                tile = vin[pl.ds(c * ZL + h * 8, 8), pl.ds(pl.multiple_of(a * N, N), N), :]
                tile = jnp.swapaxes(tile, 0, 1)
                for q, row in enumerate(block_transpose([tile[b] for b in range(N)])):
                    xsend[a, q, c, pl.ds(h * 8, 8), :] = row

    def send_first(a):
        for i in range(NP - 1):
            copy1(a, i).start()
        mine = pl.ds(pl.multiple_of(me * ZL, ZL), ZL)
        xbuf[a, :, mine, :] = xsend[a, me]

    loads[0].wait()
    pack_first(0)
    pl.semaphore_wait(barrier, NP - 1 + NE - 1)
    send_first(0)

    def first(a, carry):
        pack_first(a)
        send_first(a)
        return carry

    lax.fori_loop(1, N, first, 0)

    acc[...] = jnp.zeros_like(acc)
    dots[...] = jnp.zeros_like(dots)
    row_i = lax.broadcasted_iota(jnp.int32, (ED, ED), 0)
    lane_i = lax.broadcasted_iota(jnp.int32, (ED, ED), 1)
    lid_l = jnp.broadcast_to(lid, (ED, ED))
    lid_t = jnp.transpose(lid_l.astype(F32)).astype(jnp.int32)

    def ones(where):
        return jnp.where(where, 1.0, 0.0).astype(BF16)

    tables[0] = ones(lid_t == ((lid_l & 64) | ((lid_l + 63) & 63)))
    tables[1] = ones(lid_t == ((lid_l & 64) | ((lid_l + 1) & 63)))
    tables[2] = ones((lid_t == (lid_l ^ 64)) & (lid_l >= 64))
    tables[3] = ones((lid_t == (lid_l ^ 64)) & (lid_l < 64))
    tables[4] = ones(lid_t == lane_i + 64)
    tables[5] = ones((lid_t == lane_i) & (lane_i >= 64))
    tables[6] = ones((lid_t == lane_i) & (lane_i < 64))
    tables[7] = ones(lid_t + 64 == lane_i)
    tables[8] = ones((row_i == lid_l) & (lid_l < 64))
    tables[9] = ones(row_i == lid_l + 64)
    tables[10] = ones(row_i + 64 == lid_l)
    tables[11] = ones((row_i == lid_l) & (lid_l >= 64))
    slot = me * ZL + (lax.broadcasted_iota(jnp.int32, (SYS, ED), 0) & (ZL - 1))
    kappa = jnp.where(slot == 1, Z // 2, slot // 2).astype(F32)
    hel[...] = (LAM + (STEP * kappa) * (STEP * kappa)) * geo[0:1, :]

    def arrive_first(p, carry):
        for i in range(NP - 1):
            copy1(p, i).wait_recv()
        w_p = ctab[pl.ds(ROW_W + p, 1), :]
        mass = geo[5:6, :] * w_p
        g_y = geo[6:7, :] * w_p
        g_x = geo[7:8, :]
        for c in range(3):
            fy_high, fy_low = split(xbuf[p, 1] * xbuf[p, c])
            dy = dot(fy_high, mats[4]) + dot(fy_low, mats[4]) + dot(fy_high, mats[5])
            acc[p, c] += (LAM * mass) * xbuf[p, c] - g_y * dy
            b_high, b_low = split(mass * (xbuf[p, 2] * xbuf[p, c]))
            bbuf[p, 0, c] = b_high
            bbuf[p, 1, c] = b_low
            for h in range(4):
                rows = pl.ds(h * 32, 32)
                fx = g_x * (xbuf[p, 0, rows, :] * xbuf[p, c, rows, :])
                for a in range(N):
                    acc[a, c, rows, :] += ctab[pl.ds(p * N + a, 1), :] * fx
        return carry

    lax.fori_loop(0, N, arrive_first, 0)

    f_high = jnp.concatenate([mats[0], mats[1]], axis=1)
    f_low = jnp.concatenate([mats[2], mats[3]], axis=1)

    def send_second(step, carry):
        c, pair = step // PAIRS, lax.rem(step, PAIRS)
        for k in (0, 1):
            a = 2 * pair + k
            a_high, a_low = split(acc[a, c])
            high = jnp.concatenate([a_high, bbuf[a, 0, c]], axis=0)
            low = jnp.concatenate([a_low, bbuf[a, 1, c]], axis=0)
            fsend[c, a] = dot(f_high, high) + dot(f_high, low) + dot(f_low, high)
        for i in range(NP - 1):
            copy2(c, pair, i).start()
        mine = pl.ds(pl.multiple_of(me * ZL, ZL), ZL)
        fbuf[c, me, pl.ds(2 * pair, 2)] = fsend[c, pl.ds(2 * pair, 2), mine, :]
        return carry

    lax.fori_loop(0, 3 * PAIRS, send_second, 0)

    def sys_rows(c):
        return pl.ds(pl.multiple_of(c * ZL, ZL), ZL)

    def r_halo(c, way, pair):
        return pltpu.make_async_remote_copy(
            src_ref=rsend.at[c, way, pair],
            dst_ref=rrecv.at[c, way, pair],
            send_sem=hs1.at[c, way, pair],
            recv_sem=hr1.at[c, way, pair],
            device_id=((up, down)[way], me),
            device_id_type=MESH,
        )

    def q_halo(c, way):
        return pltpu.make_async_remote_copy(
            src_ref=qsend.at[c, way],
            dst_ref=qrecv.at[c, way],
            send_sem=hs2.at[c, way],
            recv_sem=hr2.at[c, way],
            device_id=((up, down)[way], me),
            device_id_type=MESH,
        )

    def side(v, rows, b, first, count):
        return jnp.concatenate([v[a * N + b, rows, :] for a in range(first, first + count)], axis=0)

    def pack_edges(v, c, pair, count):
        rows = sys_rows(c)
        packed = []
        for b, t in ((N - 1, 4), (0, 6)):
            for k in (0, 1):
                nodes = [v[(2 * (pair + i) + k) * N + b, rows, :] for i in range(count)]
                nodes = jnp.concatenate(nodes, axis=0) if count > 1 else nodes[0]
                packed.append(pick(nodes, tables[t + k]))
        return packed[0] + packed[1], packed[2] + packed[3]

    def send_r_edges(c, pair):
        for way, got in enumerate(pack_edges(res, c, pair, 1)):
            rsend[c, way, pair] = got
            r_halo(c, way, pair).start()

    def send_q_edges(c):
        for way, got in enumerate(pack_edges(qv, c, 0, PAIRS)):
            qsend[c, way] = got.reshape(PAIRS, ZL, ED)
            q_halo(c, way).start()

    def take_edges(recv, c):
        for way in (0, 1):
            there = (e > 0) if way == 0 else (e < NE - 1)
            got = recv[c, way].reshape(PAIRS * ZL, ED)
            for k in (0, 1):
                here = jnp.where(there, pick(got, tables[8 + 2 * way + k]), 0.0)
                here = here.reshape(PAIRS, ZL, ED)
                for pair in range(PAIRS):
                    edge[way, 2 * pair + k] = here[pair]

    def take_faces(v, c):
        sys = sys_rows(c)
        shape = (N, ZL, ED)
        face[2] = pick(side(v, sys, N - 1, 0, N), tables[2]).reshape(shape)
        face[3] = pick(side(v, sys, 0, 0, N), tables[3]).reshape(shape)
        face[0] = pick(v[(N - 1) * N : N * N, sys, :].reshape(N * ZL, ED), tables[0]).reshape(shape)
        face[1] = pick(v[0:N, sys, :].reshape(N * ZL, ED), tables[1]).reshape(shape)

    def apply_local(v, q, c, columns):
        def tile(h, carry):
            rows = pl.ds(pl.multiple_of(c * ZL + h * 8, 8), 8)
            frows = pl.ds(pl.multiple_of(h * 8, 8), 8)
            hm = hel[rows, :]
            kx = jnp.broadcast_to(geo[1:2, :], (8, ED))
            ky = jnp.broadcast_to(geo[2:3, :], (8, ED))
            nodes = [b for pair in columns for b in (pair, N - 1 - pair)]
            for b in nodes:
                col = stiff_times([v[a * N + b, rows, :] for a in range(N)], range(N // 2))
                scale_b = kx * float(WEIGHTS[b])
                for a in range(N):
                    q[a * N + b, rows, :] = scale_b * col[a]
            for a in range(N):
                vals = [v[a * N + b, rows, :] for b in range(N)]
                line = stiff_times(vals, columns)
                scale_a = ky * float(WEIGHTS[a])
                hm_a = hm * float(WEIGHTS[a])
                for b in nodes:
                    out = q[a * N + b, rows, :] + scale_a * line[b]
                    out = out + (hm_a * float(WEIGHTS[b])) * vals[b]
                    if a == 0:
                        out = out + float(PEN * WEIGHTS[b]) * (vals[b] - face[0, b, frows, :])
                    if a == N - 1:
                        out = out + float(PEN * WEIGHTS[b]) * (vals[b] - face[1, b, frows, :])
                    if b == 0:
                        out = out + float(PEN * WEIGHTS[a]) * (vals[b] - face[2, a, frows, :])
                    if b == N - 1:
                        out = out + float(PEN * WEIGHTS[a]) * (vals[b] - face[3, a, frows, :])
                    q[a * N + b, rows, :] = out
            return carry

        lax.fori_loop(0, ZL // 8, tile, 0)

    def add_edges(q, c):
        rows = sys_rows(c)
        for a in range(N):
            q[a * N, rows, :] -= float(PEN * WEIGHTS[a]) * edge[0, a]
            q[a * N + N - 1, rows, :] -= float(PEN * WEIGHTS[a]) * edge[1, a]

    def arrive_second(c, pair):
        for i in range(NP - 1):
            copy2(c, pair, i).wait_recv()
        for k in (0, 1):
            a = 2 * pair + k
            lines = block_transpose([fbuf[c, s, a] for s in range(NP)])
            for b, line in enumerate(lines):
                res[a * N + b, sys_rows(c), :] = line

    def begin(c):
        def pair(k, carry):
            arrive_second(c, k)
            send_r_edges(c, k)
            return carry

        lax.fori_loop(0, PAIRS, pair, 0)
        take_faces(res, c)
        apply_local(res, qv, c, (0,))
        send_q_edges(c)
        apply_local(res, qv, c, (1, 2, 3))

    def end(c):
        def wait_r(k, carry):
            for way in (0, 1):
                r_halo(c, way, k).wait_recv()
            return carry

        lax.fori_loop(0, PAIRS, wait_r, 0)
        take_edges(rrecv, c)
        add_edges(qv, c)
        take_faces(qv, c)
        apply_local(qv, pv, c, range(N // 2))

        def dot_tile(h, carry):
            rows = pl.ds(pl.multiple_of(c * ZL + h * 8, 8), 8)
            sums = [jnp.zeros((8, ED), F32) for _ in range(4)]
            for n in range(N * N):
                r_n, q_n, p_n = res[n, rows, :], qv[n, rows, :], pv[n, rows, :]
                for k, prod in enumerate((r_n * r_n, r_n * q_n, q_n * q_n, q_n * p_n)):
                    sums[k] = sums[k] + prod
            for k in range(4):
                dots[k, rows, :] = sums[k]
            return carry

        lax.fori_loop(0, ZL // 8, dot_tile, 0)
        for way in (0, 1):
            q_halo(c, way).wait_recv()
        take_edges(qrecv, c)
        rows = sys_rows(c)
        inner = jnp.broadcast_to(lid < 64, (ZL, ED)) & (e > 0)
        outer = jnp.broadcast_to(lid >= 64, (ZL, ED)) & (e < NE - 1)
        last = jnp.zeros((ZL, ED), F32)
        for a in range(N):
            w_a = float(PEN * WEIGHTS[a])
            for way, b, where in ((0, 0, inner), (1, N - 1, outer)):
                n = a * N + b
                got = w_a * (edge[way, a] - jnp.where(where, w_a * res[n, rows, :], 0.0))
                pv[n, rows, :] -= got
                last = last + qv[n, rows, :] * got
        dots[3, rows, :] -= last

    begin(0)

    def component(c, carry):
        begin(c)
        end(c - 1)
        return carry

    lax.fori_loop(1, 3, component, 0)
    end(2)

    one_rows = jnp.ones((8, ED), F32)
    row8 = lax.broadcasted_iota(jnp.int32, (8, ED), 0)
    part = jnp.zeros((8, ED), F32)
    for k in range(4):
        summed = lax.dot_general(
            one_rows,
            dots[k],
            (((1,), (1,)), ((), ())),
            precision=lax.Precision.HIGHEST,
            preferred_element_type=F32,
        )
        part = jnp.where(row8 == k, summed, part)

    rbuf[0] = part

    def spread(i):
        return pltpu.make_async_remote_copy(
            src_ref=rbuf.at[0],
            dst_ref=rbuf.at[i + 1],
            send_sem=rs.at[i],
            recv_sem=rr.at[i],
            device_id=(elem_peers[i], me),
            device_id_type=MESH,
        )

    for i in range(NE - 1):
        spread(i).start()
    for i in range(NE - 1):
        spread(i).wait_recv()
    part = jnp.sum(rbuf[...], axis=0)

    aa, bb, cc, ee = (part[k : k + 1, :] for k in range(4))
    alpha = aa / bb
    rr1 = alpha * alpha * cc - aa
    beta1 = 1.0 + rr1 / aa
    alpha1 = rr1 / (beta1 * beta1 * bb - 2.0 * beta1 * alpha * cc + alpha * alpha * ee)
    coef_s = alpha + alpha1 * beta1
    coef_t = alpha1 * alpha
    both = jnp.where(row8 == 0, coef_s, coef_t)
    both = jnp.where(lax.broadcasted_iota(jnp.int32, (8, ED), 1) < SYS, both, 0.0)
    both = jnp.transpose(jnp.concatenate([both] + [jnp.zeros((8, ED), F32)] * 15, axis=0))
    coef_out[0] = jnp.broadcast_to(both[0:SYS, 0:1], (SYS, ED))
    coef_out[1] = jnp.broadcast_to(both[0:SYS, 1:2], (SYS, ED))

    def drain(a, carry):
        for i in range(NP - 1):
            copy1(a, i).wait_send()
        return carry

    def drain2(step, carry):
        for i in range(NP - 1):
            copy2(step // PAIRS, lax.rem(step, PAIRS), i).wait_send()
        return carry

    def drain3(c, carry):
        for way in (0, 1):
            for pair in range(PAIRS):
                r_halo(c, way, pair).wait_send()
            q_halo(c, way).wait_send()
        return carry

    lax.fori_loop(0, N, drain, 0)
    lax.fori_loop(0, 3 * PAIRS, drain2, 0)
    lax.fori_loop(0, 3, drain3, 0)
    for i in range(NE - 1):
        spread(i).wait_send()


def finish_kernel(r, q, p, coef, x_out, r_out, xs, rs, sem):
    def tile(st, carry):
        rows = pl.ds(pl.multiple_of(st * 8, 8), 8)
        s, t = coef[0, rows, :], coef[1, rows, :]
        for a in range(N):
            new, left = [], []
            for n in range(a * N, a * N + N):
                r_n, q_n, p_n = r[n, rows, :], q[n, rows, :], p[n, rows, :]
                new.append(s * r_n - t * q_n)
                left.append(r_n - s * q_n + t * p_n)
            for buf, vals in ((xs, new), (rs, left)):
                vals = jnp.swapaxes(jnp.stack(vals), 0, 1)
                for k in range(8):
                    buf[st, pl.ds(k * N * N + a * N, N), :] = vals[k]
        for copy in out_copies(st):
            copy.start()
        return carry

    def out_copies(st):
        return (
            pltpu.make_async_copy(xs.at[st], x_out.at[st], sem.at[st, 0]),
            pltpu.make_async_copy(rs.at[st], r_out.at[st], sem.at[st, 1]),
        )

    def drain(st, carry):
        for copy in out_copies(st):
            copy.wait()
        return carry

    lax.fori_loop(0, SYS // 8, tile, 0)
    lax.fori_loop(0, SYS // 8, drain, 0)


def on_device(velocity, elem_scale, elem_ids, edge_blocks):
    vel = velocity.reshape(SYS, N * N, ED)
    rows = np.zeros((ROWS, ED))
    rows[: N * N] = (-WEIGHTS[:, None] * DERIV).T.reshape(N * N, 1)
    rows[ROW_W : ROW_W + N] = WEIGHTS[:, None]
    rows[ROW_LANE] = np.repeat(WEIGHTS, EG)
    rows = jnp.asarray(rows, F32)
    four = halves(mode_matrix()).reshape(2, Z, 2, Z).transpose(0, 2, 1, 3).reshape(4, Z, Z)
    mats = jnp.asarray(np.concatenate([four, halves(np.kron(DERIV.T, np.eye(EG)))]))
    operands = (vel, elem_scale, elem_ids, rows, mats)
    vmem = pl.BlockSpec(memory_space=pltpu.VMEM)
    hbm = pl.BlockSpec(memory_space=pltpu.HBM)
    field = jax.ShapeDtypeStruct((N * N, SYS, ED), F32)
    dma = pltpu.SemaphoreType.DMA
    r0, q0, p0, coef = pl.pallas_call(
        kernel,
        out_shape=(field, field, field, jax.ShapeDtypeStruct((2, SYS, ED), F32)),
        in_specs=[hbm] * 5,
        out_specs=(vmem,) * 4,
        scratch_shapes=[
            pltpu.VMEM((SYS, N * N, ED), F32),
            pltpu.VMEM((2, ED), F32),
            pltpu.VMEM((1, ED), jnp.int32),
            pltpu.VMEM((ROWS, ED), F32),
            pltpu.VMEM((6, ED, ED), BF16),
            pltpu.VMEM((N, NP, 3, ZL, ED), F32),
            pltpu.VMEM((N, 3, Z, ED), F32),
            pltpu.VMEM((N, 3, Z, ED), F32),
            pltpu.VMEM((N, 2, 3, Z, ED), BF16),
            pltpu.VMEM((3, N, Z, ED), F32),
            pltpu.VMEM((3, NP, N, ZL, ED), F32),
            pltpu.VMEM((8, ED), F32),
            pltpu.VMEM((SYS, ED), F32),
            pltpu.VMEM((12, ED, ED), BF16),
            pltpu.VMEM((4, N, ZL, ED), F32),
            pltpu.VMEM((2, N, ZL, ED), F32),
            pltpu.VMEM((3, 2, PAIRS, ZL, ED), F32),
            pltpu.VMEM((3, 2, PAIRS, ZL, ED), F32),
            pltpu.VMEM((3, 2, PAIRS, ZL, ED), F32),
            pltpu.VMEM((3, 2, PAIRS, ZL, ED), F32),
            pltpu.VMEM((4, ED, ED), F32),
            pltpu.VMEM((NE, 8, ED), F32),
            dma((5,)),
            dma((N, NP - 1)),
            dma((N, NP - 1)),
            dma((3, PAIRS, NP - 1)),
            dma((3, PAIRS, NP - 1)),
            dma((3, 2, PAIRS)),
            dma((3, 2, PAIRS)),
            dma((3, 2)),
            dma((3, 2)),
            dma((NE - 1,)),
            dma((NE - 1,)),
        ],
        compiler_params=pltpu.CompilerParams(
            collective_id=0, has_side_effects=True, vmem_limit_bytes=48 * 1024 * 1024
        ),
        name="exchange_and_apply",
    )(*[pltpu.with_memory_space_constraint(v, pltpu.HBM) for v in operands])

    flat = jax.ShapeDtypeStruct((SYS // 8, 8 * N * N, ED), F32)
    new, left = pl.pallas_call(
        finish_kernel,
        out_shape=(flat, flat),
        in_specs=[vmem] * 4,
        out_specs=(hbm, hbm),
        scratch_shapes=[
            pltpu.VMEM(flat.shape, F32),
            pltpu.VMEM(flat.shape, F32),
            dma((SYS // 8, 2)),
        ],
        compiler_params=pltpu.CompilerParams(vmem_limit_bytes=16 * 1024 * 1024),
        name="finish",
    )(r0, q0, p0, coef)
    shape = (3, ZL, N, N, ED)
    return new.reshape(shape), left.reshape(shape)


def solution(mesh):
    in_specs = (
        P(None, "plane", None, None, "elem"),
        P(None, "elem"),
        P("elem", None),
        P("elem", None, None),
    )
    out_specs = (P(None, "plane", None, None, "elem"), P(None, "plane", None, None, "elem"))
    return jax.shard_map(
        on_device, mesh=mesh, in_specs=in_specs, out_specs=out_specs, check_vma=False
    )
```

```python
import functools
import math

import jax
import jax.numpy as jnp
import ml_dtypes
import numpy as np
from jax import lax
from jax.experimental import pallas as pl
from jax.experimental.pallas import tpu as pltpu
from jax.sharding import PartitionSpec as P

MESH = pl.DeviceIdType.MESH
F32 = jnp.float32
BF16 = jnp.bfloat16

N = 8
ED = 128
Z = 128
NP = 8
ZL = Z // NP
HALVES = 2
GROUPS = NP * HALVES
EG = ED // GROUPS
AH = N // 2
SYS = 3 * ZL
NX = 4
NZ = 8
NE = NX * NZ
PEN = 8.0
ROW_SAME, ROW_SWAP, ROW_AB, ROW_B = 0, AH * AH, 2 * AH * AH, 2 * AH * AH + AH
ROWS = 40
LAM = 4.0
STEP = 0.1


def node_tables():
    degree = N - 1
    points = -np.cos(np.pi * np.arange(N) / degree)
    scales = np.ones(N)
    scales[0] = 2.0
    scales[-1] = 2.0
    bary = (-1.0) ** np.arange(N) / scales
    deriv = np.zeros((N, N))
    for i in range(N):
        for j in range(N):
            if i != j:
                deriv[i, j] = bary[j] / bary[i] / (points[i] - points[j])
        deriv[i, i] = -np.sum(deriv[i])
    weights = np.zeros(N)
    for i in range(N):
        running = 0.0
        for k in range(1, degree // 2 + 1):
            factor = 1.0 if 2 * k == degree else 2.0
            running += factor / (4.0 * k * k - 1.0) * np.cos(2.0 * np.pi * i * k / degree)
        weights[i] = (1.0 if i in (0, degree) else 2.0) / degree * (1.0 - running)
    stiff = deriv.T @ (weights[:, None] * deriv)
    return deriv, weights, stiff


def mode_matrix():
    slots = np.arange(Z)
    harmonic = slots // 2
    angles = 2.0 * math.pi / Z * (harmonic[:, None] * slots[None, :] % Z)
    four = np.where((slots % 2 == 0)[:, None], np.cos(angles), np.sin(angles)) * (2.0 / Z)
    four[0] = 1.0 / Z
    four[1] = np.where(slots % 2 == 0, 1.0, -1.0) / Z
    dz = np.zeros((Z, Z))
    wave = STEP * np.arange(Z // 2)
    dz[0::2] = wave[:, None] * four[1::2]
    dz[1::2] = -wave[:, None] * four[0::2]
    return np.concatenate([four, -dz], axis=1)


def halves(table):
    high = table.astype(np.float32).astype(ml_dtypes.bfloat16)
    low = (table - high.astype(np.float64)).astype(np.float32).astype(ml_dtypes.bfloat16)
    return np.stack([high, low])


DERIV, WEIGHTS, STIFF = node_tables()


def split(x):
    high = x.astype(BF16)
    return high, (x - high.astype(F32)).astype(BF16)


def dot(x, y):
    return jnp.dot(x, y, preferred_element_type=F32)


def pick(x, table):
    high, low = split(x)
    return dot(high, table) + dot(low, table)


def block_transpose(rows):
    rows = list(rows)
    axis = rows[0].ndim - 1
    lane = lax.broadcasted_iota(jnp.int32, rows[0].shape, axis) // EG
    d = 1
    while d < GROUPS:
        clear = (lane & d) == 0
        for i in range(GROUPS):
            if i & d == 0:
                x, y = rows[i], rows[i + d]
                rows[i] = jnp.where(clear, x, pltpu.roll(y, EG * d, axis))
                rows[i + d] = jnp.where(clear, pltpu.roll(x, ED - EG * d, axis), y)
        d *= 2
    return rows


def stiff_times(v, wanted):
    even = [v[p] + v[N - 1 - p] for p in range(N // 2)]
    odd = [v[p] - v[N - 1 - p] for p in range(N // 2)]
    out = [None] * N
    for a in wanted:
        s = [0.5 * (STIFF[a, p] + STIFF[a, N - 1 - p]) for p in range(N // 2)]
        t = [0.5 * (STIFF[a, p] - STIFF[a, N - 1 - p]) for p in range(N // 2)]
        e = sum(float(s[p]) * even[p] for p in range(1, N // 2)) + float(s[0]) * even[0]
        o = sum(float(t[p]) * odd[p] for p in range(1, N // 2)) + float(t[0]) * odd[0]
        out[a] = e + o
        out[N - 1 - a] = e - o
    return out


def kernel(
    vel,
    scale_in,
    ids_in,
    rows_in,
    mats_in,
    res,
    qv,
    pv,
    coef_out,
    vin,
    scale,
    ids,
    ctab,
    mats,
    xsend,
    xbuf,
    acc,
    bbuf,
    fsend,
    fbuf,
    geo,
    part_geo,
    hel,
    tables,
    face,
    edge,
    rsend,
    rrecv,
    qsend,
    qrecv,
    dots,
    rbuf,
    in_sem,
    s1,
    r1,
    s2,
    r2,
    hs1,
    hr1,
    hs2,
    hr2,
    rs,
    rr,
):
    e = lax.axis_index("elem")
    me = lax.axis_index("plane")
    y, core = me // 2, lax.rem(me, 2)
    z, x = e // NX, lax.rem(e, NX)
    plane_offsets = [(dy, dc) for dy in (2, 1, 3, 0) for dc in (0, 1) if (dy, dc) != (0, 0)]
    plane_peers = [lax.rem(y + dy, 4) * 2 + lax.rem(core + dc, 2) for dy, dc in plane_offsets]
    elem_peers = [
        lax.rem(z + dz, NZ) * NX + lax.rem(x + dx, NX)
        for dz in (4, 3, 5, 2, 6, 1, 7, 0)
        for dx in (2, 1, 3, 0)
        if (dz, dx) != (0, 0)
    ]
    up, down = lax.rem(e + 1, NE), lax.rem(e + NE - 1, NE)

    pairs = ((vel, vin), (scale_in, scale), (ids_in, ids), (rows_in, ctab), (mats_in, mats))
    loads = [pltpu.make_async_copy(src, dst, in_sem.at[i]) for i, (src, dst) in enumerate(pairs)]
    for load in loads:
        load.start()
    barrier = pltpu.get_barrier_semaphore()
    for t in plane_peers:
        pl.semaphore_signal(barrier, inc=1, device_id=(e, t), device_id_type=MESH)
    for t in elem_peers:
        pl.semaphore_signal(barrier, inc=1, device_id=(t, me), device_id_type=MESH)

    for load in loads[1:]:
        load.wait()

    lid = ids[...] & (ED - 1)
    growth = 1.0 + 2.0 * (ids[...] // 64).astype(F32) / 63.0
    circ = scale[0:1, :] * growth
    radial = scale[1:2, :]
    geo[0:1, :] = circ * radial
    geo[1:2, :] = radial / circ
    geo[2:3, :] = circ / radial
    for half in range(HALVES):
        share = []
        for val in (circ, radial):
            first = ED - EG * (HALVES * me + half)
            val = pltpu.roll(jnp.broadcast_to(val, (8, ED)), lax.rem(first, ED), 1)
            val = jnp.where(lax.broadcasted_iota(jnp.int32, (8, ED), 1) < EG, val, 0.0)
            for d in (1, 2, 4, 8):
                val = val + pltpu.roll(val, EG * d, 1)
            share.append(val[0:1, :])
        g_circ, g_radial = share
        part_geo[half, 0:1, :] = g_circ * g_radial
        part_geo[half, 1:2, :] = g_circ
        part_geo[half, 2:3, :] = g_radial * ctab[ROW_B : ROW_B + 1, :]

    def copy1(half, ah, i):
        t = plane_peers[i]
        return pltpu.make_async_remote_copy(
            src_ref=xsend.at[half, ah, t],
            dst_ref=xbuf.at[half, ah, :, pl.ds(pl.multiple_of(me * ZL, ZL), ZL), :],
            send_sem=s1.at[half, ah, i],
            recv_sem=r1.at[half, ah, i],
            device_id=(e, t),
            device_id_type=MESH,
        )

    def copy2(half, c, k, i):
        t = plane_peers[i]
        return pltpu.make_async_remote_copy(
            src_ref=fsend.at[half, c, pl.ds(2 * k, 2), pl.ds(pl.multiple_of(t * ZL, ZL), ZL), :],
            dst_ref=fbuf.at[half, c, me, pl.ds(2 * k, 2)],
            send_sem=s2.at[half, c, k, i],
            recv_sem=r2.at[half, c, k, i],
            device_id=(e, t),
            device_id_type=MESH,
        )

    def pack_first(ah):
        for c in range(3):
            for z8 in range(ZL // 8):
                nodes = pl.ds(pl.multiple_of(ah * 2 * N, 2 * N), 2 * N)
                tile = jnp.swapaxes(vin[pl.ds(c * ZL + z8 * 8, 8), nodes, :], 0, 1)
                for g, row in enumerate(block_transpose([tile[k] for k in range(2 * N)])):
                    xsend[g % HALVES, ah, g // HALVES, c, pl.ds(z8 * 8, 8), :] = row

    def send_first(half, ah):
        for i in range(NP - 1):
            copy1(half, ah, i).start()
        mine = pl.ds(pl.multiple_of(me * ZL, ZL), ZL)
        xbuf[half, ah, :, mine, :] = xsend[half, ah, me]

    loads[0].wait()
    pack_first(0)
    pl.semaphore_wait(barrier, NP - 1 + NE - 1)
    send_first(0, 0)

    def first(ah, carry):
        pack_first(ah)
        send_first(0, ah)
        return carry

    def first_rest(ah, carry):
        send_first(1, ah)
        return carry

    lax.fori_loop(1, AH, first, 0)
    lax.fori_loop(0, AH, first_rest, 0)

    acc[...] = jnp.zeros_like(acc)
    dots[...] = jnp.zeros_like(dots)
    row_i = lax.broadcasted_iota(jnp.int32, (ED, ED), 0)
    lane_i = lax.broadcasted_iota(jnp.int32, (ED, ED), 1)
    lid_l = jnp.broadcast_to(lid, (ED, ED))
    lid_t = jnp.transpose(lid_l.astype(F32)).astype(jnp.int32)

    def ones(where):
        return jnp.where(where, 1.0, 0.0).astype(BF16)

    tables[0] = ones(lid_t == ((lid_l & 64) | ((lid_l + 63) & 63)))
    tables[1] = ones(lid_t == ((lid_l & 64) | ((lid_l + 1) & 63)))
    tables[2] = ones((lid_t == (lid_l ^ 64)) & (lid_l >= 64))
    tables[3] = ones((lid_t == (lid_l ^ 64)) & (lid_l < 64))
    tables[4] = ones(lid_t == lane_i + 64)
    tables[5] = ones((lid_t == lane_i) & (lane_i >= 64))
    tables[6] = ones((lid_t == lane_i) & (lane_i < 64))
    tables[7] = ones(lid_t + 64 == lane_i)
    tables[8] = ones((row_i == lid_l) & (lid_l < 64))
    tables[9] = ones(row_i == lid_l + 64)
    tables[10] = ones(row_i + 64 == lid_l)
    tables[11] = ones((row_i == lid_l) & (lid_l >= 64))
    slot = me * ZL + (lax.broadcasted_iota(jnp.int32, (SYS, ED), 0) & (ZL - 1))
    kappa = jnp.where(slot == 1, Z // 2, slot // 2).astype(F32)
    hel[...] = (LAM + (STEP * kappa) * (STEP * kappa)) * geo[0:1, :]

    f_high = jnp.concatenate([mats[0], mats[1]], axis=1)
    f_low = jnp.concatenate([mats[2], mats[3]], axis=1)

    def between(half, carry):
        def arrive_first(ph, carry):
            for i in range(NP - 1):
                copy1(half, ph, i).wait_recv()
            w_ab = ctab[pl.ds(ROW_AB + ph, 1), :]
            mass = part_geo[half, 0:1, :] * w_ab
            g_y = part_geo[half, 1:2, :] * w_ab
            g_x = part_geo[half, 2:3, :]
            for c in range(3):
                fy_high, fy_low = split(xbuf[half, ph, 1] * xbuf[half, ph, c])
                dy = dot(fy_high, mats[4]) + dot(fy_low, mats[4]) + dot(fy_high, mats[5])
                acc[half, ph, c] += (LAM * mass) * xbuf[half, ph, c] - g_y * dy
                b_high, b_low = split(mass * (xbuf[half, ph, 2] * xbuf[half, ph, c]))
                bbuf[half, ph, 0, c] = b_high
                bbuf[half, ph, 1, c] = b_low
                for k in range(4):
                    rows = pl.ds(k * 32, 32)
                    fx = g_x * (xbuf[half, ph, 0, rows, :] * xbuf[half, ph, c, rows, :])
                    swap = pltpu.roll(fx, ED // 2, 1)
                    for ah in range(AH):
                        same = ctab[pl.ds(ROW_SAME + ph * AH + ah, 1), :]
                        other = ctab[pl.ds(ROW_SWAP + ph * AH + ah, 1), :]
                        acc[half, ah, c, rows, :] += same * fx + other * swap
            return carry

        def send_second(step, carry):
            c, k = step // 2, lax.rem(step, 2)
            for j in (0, 1):
                ah = 2 * k + j
                a_high, a_low = split(acc[half, ah, c])
                high = jnp.concatenate([a_high, bbuf[half, ah, 0, c]], axis=0)
                low = jnp.concatenate([a_low, bbuf[half, ah, 1, c]], axis=0)
                fsend[half, c, ah] = dot(f_high, high) + dot(f_high, low) + dot(f_low, high)
            for i in range(NP - 1):
                copy2(half, c, k, i).start()
            mine = pl.ds(pl.multiple_of(me * ZL, ZL), ZL)
            fbuf[half, c, me, pl.ds(2 * k, 2)] = fsend[half, c, pl.ds(2 * k, 2), mine, :]
            return carry

        lax.fori_loop(0, AH, arrive_first, 0)
        lax.fori_loop(0, 6, send_second, 0)
        return carry

    lax.fori_loop(0, HALVES, between, 0)

    def sys_rows(c):
        return pl.ds(pl.multiple_of(c * ZL, ZL), ZL)

    def r_halo(c, way, pair):
        return pltpu.make_async_remote_copy(
            src_ref=rsend.at[c, way, pair],
            dst_ref=rrecv.at[c, way, pair],
            send_sem=hs1.at[c, way, pair],
            recv_sem=hr1.at[c, way, pair],
            device_id=((up, down)[way], me),
            device_id_type=MESH,
        )

    def q_halo(c, way):
        return pltpu.make_async_remote_copy(
            src_ref=qsend.at[c, way],
            dst_ref=qrecv.at[c, way],
            send_sem=hs2.at[c, way],
            recv_sem=hr2.at[c, way],
            device_id=((up, down)[way], me),
            device_id_type=MESH,
        )

    def side(v, rows, b, first, count):
        return jnp.concatenate([v[a * N + b, rows, :] for a in range(first, first + count)], axis=0)

    def pack_edges(v, c, pair, count):
        rows = sys_rows(c)
        packed = []
        for b, t in ((N - 1, 4), (0, 6)):
            for k in (0, 1):
                nodes = [v[(2 * (pair + i) + k) * N + b, rows, :] for i in range(count)]
                nodes = jnp.concatenate(nodes, axis=0) if count > 1 else nodes[0]
                packed.append(pick(nodes, tables[t + k]))
        return packed[0] + packed[1], packed[2] + packed[3]

    def send_r_edges(c, pair):
        for way, got in enumerate(pack_edges(res, c, pair, 1)):
            rsend[c, way, pair] = got
            r_halo(c, way, pair).start()

    def send_q_edges(c):
        for way, got in enumerate(pack_edges(qv, c, 0, AH)):
            qsend[c, way] = got.reshape(AH, ZL, ED)
            q_halo(c, way).start()

    def take_edges(recv, c):
        for way in (0, 1):
            there = (e > 0) if way == 0 else (e < NE - 1)
            got = recv[c, way].reshape(AH * ZL, ED)
            for k in (0, 1):
                here = jnp.where(there, pick(got, tables[8 + 2 * way + k]), 0.0)
                here = here.reshape(AH, ZL, ED)
                for pair in range(AH):
                    edge[way, 2 * pair + k] = here[pair]

    def take_faces(v, c):
        sys = sys_rows(c)
        shape = (N, ZL, ED)
        face[2] = pick(side(v, sys, N - 1, 0, N), tables[2]).reshape(shape)
        face[3] = pick(side(v, sys, 0, 0, N), tables[3]).reshape(shape)
        face[0] = pick(v[(N - 1) * N : N * N, sys, :].reshape(N * ZL, ED), tables[0]).reshape(shape)
        face[1] = pick(v[0:N, sys, :].reshape(N * ZL, ED), tables[1]).reshape(shape)

    def apply_local(v, q, c, columns):
        def tile(h, carry):
            rows = pl.ds(pl.multiple_of(c * ZL + h * 8, 8), 8)
            frows = pl.ds(pl.multiple_of(h * 8, 8), 8)
            hm = hel[rows, :]
            kx = jnp.broadcast_to(geo[1:2, :], (8, ED))
            ky = jnp.broadcast_to(geo[2:3, :], (8, ED))
            nodes = [b for pair in columns for b in (pair, N - 1 - pair)]
            for b in nodes:
                col = stiff_times([v[a * N + b, rows, :] for a in range(N)], range(N // 2))
                scale_b = kx * float(WEIGHTS[b])
                for a in range(N):
                    q[a * N + b, rows, :] = scale_b * col[a]
            for a in range(N):
                vals = [v[a * N + b, rows, :] for b in range(N)]
                line = stiff_times(vals, columns)
                scale_a = ky * float(WEIGHTS[a])
                hm_a = hm * float(WEIGHTS[a])
                for b in nodes:
                    out = q[a * N + b, rows, :] + scale_a * line[b]
                    out = out + (hm_a * float(WEIGHTS[b])) * vals[b]
                    if a == 0:
                        out = out + float(PEN * WEIGHTS[b]) * (vals[b] - face[0, b, frows, :])
                    if a == N - 1:
                        out = out + float(PEN * WEIGHTS[b]) * (vals[b] - face[1, b, frows, :])
                    if b == 0:
                        out = out + float(PEN * WEIGHTS[a]) * (vals[b] - face[2, a, frows, :])
                    if b == N - 1:
                        out = out + float(PEN * WEIGHTS[a]) * (vals[b] - face[3, a, frows, :])
                    q[a * N + b, rows, :] = out
            return carry

        lax.fori_loop(0, ZL // 8, tile, 0)

    def add_edges(q, c):
        rows = sys_rows(c)
        for a in range(N):
            q[a * N, rows, :] -= float(PEN * WEIGHTS[a]) * edge[0, a]
            q[a * N + N - 1, rows, :] -= float(PEN * WEIGHTS[a]) * edge[1, a]

    def arrive_second(c, ah):
        groups = [fbuf[g % HALVES, c, g // HALVES, ah] for g in range(GROUPS)]
        for k, line in enumerate(block_transpose(groups)):
            res[ah * 2 * N + k, sys_rows(c), :] = line

    def dot_rows(first, k, count):
        return pl.ds(pl.multiple_of(first + (k % 2) * (ED // 2), 8), count)

    def begin(c):
        def arrive(ah, carry):
            arrive_second(c, ah)
            send_r_edges(c, ah)
            return carry

        def arrive_pair(k, carry):
            for half in range(HALVES):
                for i in range(NP - 1):
                    copy2(half, c, k, i).wait_recv()
            return lax.fori_loop(2 * k, 2 * k + 2, arrive, carry)

        lax.fori_loop(0, 2, arrive_pair, 0)
        take_faces(res, c)
        apply_local(res, qv, c, (0,))
        send_q_edges(c)
        apply_local(res, qv, c, (1, 2, 3))

    def end(c):
        def wait_r(k, carry):
            for way in (0, 1):
                r_halo(c, way, k).wait_recv()
            return carry

        lax.fori_loop(0, AH, wait_r, 0)
        take_edges(rrecv, c)
        add_edges(qv, c)
        take_faces(qv, c)
        apply_local(qv, pv, c, range(N // 2))

        def dot_tile(h, carry):
            rows = pl.ds(pl.multiple_of(c * ZL + h * 8, 8), 8)
            sums = [jnp.zeros((8, ED), F32) for _ in range(4)]
            for n in range(N * N):
                r_n, q_n, p_n = res[n, rows, :], qv[n, rows, :], pv[n, rows, :]
                for k, prod in enumerate((r_n * r_n, r_n * q_n, q_n * q_n, q_n * p_n)):
                    sums[k] = sums[k] + prod
            for k in range(4):
                dots[k // 2, dot_rows(c * ZL + h * 8, k, 8), :] = sums[k]
            return carry

        lax.fori_loop(0, ZL // 8, dot_tile, 0)
        for way in (0, 1):
            q_halo(c, way).wait_recv()
        take_edges(qrecv, c)
        rows = sys_rows(c)
        inner = jnp.broadcast_to(lid < 64, (ZL, ED)) & (e > 0)
        outer = jnp.broadcast_to(lid >= 64, (ZL, ED)) & (e < NE - 1)
        last = jnp.zeros((ZL, ED), F32)
        for a in range(N):
            w_a = float(PEN * WEIGHTS[a])
            for way, b, where in ((0, 0, inner), (1, N - 1, outer)):
                n = a * N + b
                got = w_a * (edge[way, a] - jnp.where(where, w_a * res[n, rows, :], 0.0))
                pv[n, rows, :] -= got
                last = last + qv[n, rows, :] * got
        dots[1, dot_rows(c * ZL, 3, ZL), :] -= last

    def begin_all(c, carry):
        begin(c)
        return carry

    def end_all(c, carry):
        end(c)
        return carry

    lax.fori_loop(0, 3, begin_all, 0)
    lax.fori_loop(0, 3, end_all, 0)

    one_rows = jnp.ones((8, ED), F32)
    for k in (0, 1):
        summed = lax.dot_general(
            one_rows,
            dots[k],
            (((1,), (1,)), ((), ())),
            precision=lax.Precision.HIGHEST,
            preferred_element_type=F32,
        )
        rbuf[0, k : k + 1, :] = summed[0:1, :]

    def spread(i):
        return pltpu.make_async_remote_copy(
            src_ref=rbuf.at[0],
            dst_ref=rbuf.at[i + 1],
            send_sem=rs.at[i],
            recv_sem=rr.at[i],
            device_id=(elem_peers[i], me),
            device_id_type=MESH,
        )

    for i in range(NE - 1):
        spread(i).start()
    for i in range(NE - 1):
        spread(i).wait_recv()
    part = jnp.sum(rbuf[...], axis=0)

    swapped = pltpu.roll(jnp.concatenate([part] * 4, axis=0), ED // 2, 1)
    aa, bb, cc, ee = part[0:1, :], swapped[0:1, :], part[1:2, :], swapped[1:2, :]
    alpha = aa / bb
    rr1 = alpha * alpha * cc - aa
    beta1 = 1.0 + rr1 / aa
    alpha1 = rr1 / (beta1 * beta1 * bb - 2.0 * beta1 * alpha * cc + alpha * alpha * ee)
    coef_s = alpha + alpha1 * beta1
    coef_t = alpha1 * alpha
    row8 = lax.broadcasted_iota(jnp.int32, (8, ED), 0)
    both = jnp.where(row8 == 0, coef_s, coef_t)
    both = jnp.where(lax.broadcasted_iota(jnp.int32, (8, ED), 1) < SYS, both, 0.0)
    both = jnp.transpose(jnp.concatenate([both] + [jnp.zeros((8, ED), F32)] * 15, axis=0))
    coef_out[0] = jnp.broadcast_to(both[0:SYS, 0:1], (SYS, ED))
    coef_out[1] = jnp.broadcast_to(both[0:SYS, 1:2], (SYS, ED))

    def drain(ah, carry):
        for half in range(HALVES):
            for i in range(NP - 1):
                copy1(half, ah, i).wait_send()
        return carry

    def drain2(step, carry):
        for half in range(HALVES):
            for i in range(NP - 1):
                copy2(half, step // 2, lax.rem(step, 2), i).wait_send()
        return carry

    def drain3(c, carry):
        for way in (0, 1):
            for pair in range(AH):
                r_halo(c, way, pair).wait_send()
            q_halo(c, way).wait_send()
        return carry

    lax.fori_loop(0, AH, drain, 0)
    lax.fori_loop(0, 6, drain2, 0)
    lax.fori_loop(0, 3, drain3, 0)
    for i in range(NE - 1):
        spread(i).wait_send()


def finish_kernel(r, q, p, coef, x_out, r_out, xs, rs, sem):
    def tile(st, carry):
        rows = pl.ds(pl.multiple_of(st * 8, 8), 8)
        s, t = coef[0, rows, :], coef[1, rows, :]
        for a in range(N):
            new, left = [], []
            for n in range(a * N, a * N + N):
                r_n, q_n, p_n = r[n, rows, :], q[n, rows, :], p[n, rows, :]
                new.append(s * r_n - t * q_n)
                left.append(r_n - s * q_n + t * p_n)
            for buf, vals in ((xs, new), (rs, left)):
                vals = jnp.swapaxes(jnp.stack(vals), 0, 1)
                for k in range(8):
                    buf[st, pl.ds(k * N * N + a * N, N), :] = vals[k]
        for copy in out_copies(st):
            copy.start()
        return carry

    def out_copies(st):
        return (
            pltpu.make_async_copy(xs.at[st], x_out.at[st], sem.at[st, 0]),
            pltpu.make_async_copy(rs.at[st], r_out.at[st], sem.at[st, 1]),
        )

    def drain(st, carry):
        for copy in out_copies(st):
            copy.wait()
        return carry

    lax.fori_loop(0, SYS // 8, tile, 0)
    lax.fori_loop(0, SYS // 8, drain, 0)


def on_device(velocity, elem_scale, elem_ids, edge_blocks):
    vel = velocity.reshape(SYS, N * N, ED)
    rows = np.zeros((ROWS, ED))
    table = -WEIGHTS[:, None] * DERIV
    for ph in range(AH):
        for ah in range(AH):
            for i in (0, 1):
                lanes = slice(i * ED // 2, (i + 1) * ED // 2)
                rows[ROW_SAME + ph * AH + ah, lanes] = table[2 * ah + i, 2 * ph + i]
                rows[ROW_SWAP + ph * AH + ah, lanes] = table[2 * ah + i, 2 * ph + 1 - i]
    for ah in range(AH):
        rows[ROW_AB + ah] = np.repeat(np.outer(WEIGHTS[2 * ah : 2 * ah + 2], WEIGHTS).ravel(), EG)
    rows[ROW_B] = np.repeat(np.tile(WEIGHTS, 2), EG)
    rows = jnp.asarray(rows, F32)
    four = halves(mode_matrix()).reshape(2, Z, 2, Z).transpose(0, 2, 1, 3).reshape(4, Z, Z)
    mats = jnp.asarray(np.concatenate([four, halves(np.kron(np.eye(2), np.kron(DERIV.T, np.eye(EG))))]))
    operands = (vel, elem_scale, elem_ids, rows, mats)
    vmem = pl.BlockSpec(memory_space=pltpu.VMEM)
    hbm = pl.BlockSpec(memory_space=pltpu.HBM)
    field = jax.ShapeDtypeStruct((N * N, SYS, ED), F32)
    dma = pltpu.SemaphoreType.DMA
    r0, q0, p0, coef = pl.pallas_call(
        kernel,
        out_shape=(field, field, field, jax.ShapeDtypeStruct((2, SYS, ED), F32)),
        in_specs=[hbm] * 5,
        out_specs=(vmem,) * 4,
        scratch_shapes=[
            pltpu.VMEM((SYS, N * N, ED), F32),
            pltpu.VMEM((2, ED), F32),
            pltpu.VMEM((1, ED), jnp.int32),
            pltpu.VMEM((ROWS, ED), F32),
            pltpu.VMEM((6, ED, ED), BF16),
            pltpu.VMEM((HALVES, AH, NP, 3, ZL, ED), F32),
            pltpu.VMEM((HALVES, AH, 3, Z, ED), F32),
            pltpu.VMEM((HALVES, AH, 3, Z, ED), F32),
            pltpu.VMEM((HALVES, AH, 2, 3, Z, ED), BF16),
            pltpu.VMEM((HALVES, 3, AH, Z, ED), F32),
            pltpu.VMEM((HALVES, 3, NP, AH, ZL, ED), F32),
            pltpu.VMEM((8, ED), F32),
            pltpu.VMEM((HALVES, 8, ED), F32),
            pltpu.VMEM((SYS, ED), F32),
            pltpu.VMEM((12, ED, ED), BF16),
            pltpu.VMEM((4, N, ZL, ED), F32),
            pltpu.VMEM((2, N, ZL, ED), F32),
            pltpu.VMEM((3, 2, AH, ZL, ED), F32),
            pltpu.VMEM((3, 2, AH, ZL, ED), F32),
            pltpu.VMEM((3, 2, AH, ZL, ED), F32),
            pltpu.VMEM((3, 2, AH, ZL, ED), F32),
            pltpu.VMEM((2, ED, ED), F32),
            pltpu.VMEM((NE, 2, ED), F32),
            dma((5,)),
            dma((HALVES, AH, NP - 1)),
            dma((HALVES, AH, NP - 1)),
            dma((HALVES, 3, 2, NP - 1)),
            dma((HALVES, 3, 2, NP - 1)),
            dma((3, 2, AH)),
            dma((3, 2, AH)),
            dma((3, 2)),
            dma((3, 2)),
            dma((NE - 1,)),
            dma((NE - 1,)),
        ],
        compiler_params=pltpu.CompilerParams(
            collective_id=0, has_side_effects=True, vmem_limit_bytes=48 * 1024 * 1024
        ),
        name="exchange_and_apply",
    )(*[pltpu.with_memory_space_constraint(v, pltpu.HBM) for v in operands])

    flat = jax.ShapeDtypeStruct((SYS // 8, 8 * N * N, ED), F32)
    new, left = pl.pallas_call(
        finish_kernel,
        out_shape=(flat, flat),
        in_specs=[vmem] * 4,
        out_specs=(hbm, hbm),
        scratch_shapes=[
            pltpu.VMEM(flat.shape, F32),
            pltpu.VMEM(flat.shape, F32),
            dma((SYS // 8, 2)),
        ],
        compiler_params=pltpu.CompilerParams(vmem_limit_bytes=16 * 1024 * 1024),
        name="finish",
    )(r0, q0, p0, coef)
    shape = (3, ZL, N, N, ED)
    return new.reshape(shape), left.reshape(shape)


def solution(mesh):
    in_specs = (
        P(None, "plane", None, None, "elem"),
        P(None, "elem"),
        P("elem", None),
        P("elem", None, None),
    )
    out_specs = (P(None, "plane", None, None, "elem"), P(None, "plane", None, None, "elem"))
    return jax.shard_map(
        on_device, mesh=mesh, in_specs=in_specs, out_specs=out_specs, check_vma=False
    )
```

```python
import functools
import math

import jax
import jax.numpy as jnp
import ml_dtypes
import numpy as np
from jax import lax
from jax.experimental import pallas as pl
from jax.experimental.pallas import tpu as pltpu
from jax.sharding import PartitionSpec as P

MESH = pl.DeviceIdType.MESH
F32 = jnp.float32
BF16 = jnp.bfloat16

N = 8
ED = 128
Z = 128
NP = 8
ZL = Z // NP
HALVES = 2
GROUPS = NP * HALVES
EG = ED // GROUPS
AH = N // 2
SYS = 3 * ZL
NX = 4
NZ = 8
NE = NX * NZ
PEN = 8.0
ROW_SAME, ROW_SWAP, ROW_AB, ROW_B = 0, AH * AH, 2 * AH * AH, 2 * AH * AH + AH
ROWS = 40
LAM = 4.0
STEP = 0.1


def node_tables():
    degree = N - 1
    points = -np.cos(np.pi * np.arange(N) / degree)
    scales = np.ones(N)
    scales[0] = 2.0
    scales[-1] = 2.0
    bary = (-1.0) ** np.arange(N) / scales
    deriv = np.zeros((N, N))
    for i in range(N):
        for j in range(N):
            if i != j:
                deriv[i, j] = bary[j] / bary[i] / (points[i] - points[j])
        deriv[i, i] = -np.sum(deriv[i])
    weights = np.zeros(N)
    for i in range(N):
        running = 0.0
        for k in range(1, degree // 2 + 1):
            factor = 1.0 if 2 * k == degree else 2.0
            running += factor / (4.0 * k * k - 1.0) * np.cos(2.0 * np.pi * i * k / degree)
        weights[i] = (1.0 if i in (0, degree) else 2.0) / degree * (1.0 - running)
    stiff = deriv.T @ (weights[:, None] * deriv)
    return deriv, weights, stiff


def mode_matrix():
    slots = np.arange(Z)
    harmonic = slots // 2
    angles = 2.0 * math.pi / Z * (harmonic[:, None] * slots[None, :] % Z)
    four = np.where((slots % 2 == 0)[:, None], np.cos(angles), np.sin(angles)) * (2.0 / Z)
    four[0] = 1.0 / Z
    four[1] = np.where(slots % 2 == 0, 1.0, -1.0) / Z
    dz = np.zeros((Z, Z))
    wave = STEP * np.arange(Z // 2)
    dz[0::2] = wave[:, None] * four[1::2]
    dz[1::2] = -wave[:, None] * four[0::2]
    return np.concatenate([four, -dz], axis=1)


def halves(table):
    high = table.astype(np.float32).astype(ml_dtypes.bfloat16)
    low = (table - high.astype(np.float64)).astype(np.float32).astype(ml_dtypes.bfloat16)
    return np.stack([high, low])


DERIV, WEIGHTS, STIFF = node_tables()


def split(x):
    high = x.astype(BF16)
    return high, (x - high.astype(F32)).astype(BF16)


def dot(x, y):
    return jnp.dot(x, y, preferred_element_type=F32)


def pick(x, table):
    high, low = split(x)
    return dot(high, table) + dot(low, table)


def turned(x, groups):
    shift = EG * (groups % GROUPS)
    return pltpu.roll(x, shift, x.ndim - 1) if shift else x


def block_transpose(rows, turned_before=False):
    if not turned_before:
        rows = [turned(x, i) for i, x in enumerate(rows)]
    lane = lax.broadcasted_iota(jnp.int32, rows[0].shape, rows[0].ndim - 1) // EG
    d = 1
    while d < GROUPS:
        clear = (lane & d) == 0
        rows = [jnp.where(clear, rows[i], rows[(i + d) % GROUPS]) for i in range(GROUPS)]
        d *= 2
    return [turned(rows[-g % GROUPS], -g) for g in range(GROUPS)]


def stiff_times(v, wanted):
    even = [v[p] + v[N - 1 - p] for p in range(N // 2)]
    odd = [v[p] - v[N - 1 - p] for p in range(N // 2)]
    out = [None] * N
    for a in wanted:
        s = [0.5 * (STIFF[a, p] + STIFF[a, N - 1 - p]) for p in range(N // 2)]
        t = [0.5 * (STIFF[a, p] - STIFF[a, N - 1 - p]) for p in range(N // 2)]
        e = sum(float(s[p]) * even[p] for p in range(1, N // 2)) + float(s[0]) * even[0]
        o = sum(float(t[p]) * odd[p] for p in range(1, N // 2)) + float(t[0]) * odd[0]
        out[a] = e + o
        out[N - 1 - a] = e - o
    return out


def kernel(
    vel,
    scale_in,
    ids_in,
    rows_in,
    mats_in,
    res,
    qv,
    pv,
    coef_out,
    vin,
    scale,
    ids,
    ctab,
    mats,
    xsend,
    xbuf,
    acc,
    bbuf,
    fsend,
    fbuf,
    geo,
    part_geo,
    hel,
    tables,
    face,
    edge,
    rsend,
    rrecv,
    qsend,
    qrecv,
    dots,
    rbuf,
    in_sem,
    s1,
    r1,
    s2,
    r2,
    hs1,
    hr1,
    hs2,
    hr2,
    rs,
    rr,
):
    e = lax.axis_index("elem")
    me = lax.axis_index("plane")
    y, core = me // 2, lax.rem(me, 2)
    z, x = e // NX, lax.rem(e, NX)
    plane_offsets = [(dy, dc) for dy in (2, 1, 3, 0) for dc in (0, 1) if (dy, dc) != (0, 0)]
    plane_peers = [lax.rem(y + dy, 4) * 2 + lax.rem(core + dc, 2) for dy, dc in plane_offsets]
    elem_peers = [
        lax.rem(z + dz, NZ) * NX + lax.rem(x + dx, NX)
        for dz in (4, 3, 5, 2, 6, 1, 7, 0)
        for dx in (2, 1, 3, 0)
        if (dz, dx) != (0, 0)
    ]
    up, down = lax.rem(e + 1, NE), lax.rem(e + NE - 1, NE)

    pairs = ((vel, vin), (scale_in, scale), (ids_in, ids), (rows_in, ctab), (mats_in, mats))
    loads = [pltpu.make_async_copy(src, dst, in_sem.at[i]) for i, (src, dst) in enumerate(pairs)]
    for load in loads:
        load.start()
    barrier = pltpu.get_barrier_semaphore()
    for t in plane_peers:
        pl.semaphore_signal(barrier, inc=1, device_id=(e, t), device_id_type=MESH)
    for t in elem_peers:
        pl.semaphore_signal(barrier, inc=1, device_id=(t, me), device_id_type=MESH)

    for load in loads[1:]:
        load.wait()

    lid = ids[...] & (ED - 1)
    growth = 1.0 + 2.0 * (ids[...] // 64).astype(F32) / 63.0
    circ = scale[0:1, :] * growth
    radial = scale[1:2, :]
    geo[0:1, :] = circ * radial
    geo[1:2, :] = radial / circ
    geo[2:3, :] = circ / radial
    for half in range(HALVES):
        share = []
        for val in (circ, radial):
            first = ED - EG * (HALVES * me + half)
            val = pltpu.roll(jnp.broadcast_to(val, (8, ED)), lax.rem(first, ED), 1)
            val = jnp.where(lax.broadcasted_iota(jnp.int32, (8, ED), 1) < EG, val, 0.0)
            for d in (1, 2, 4, 8):
                val = val + pltpu.roll(val, EG * d, 1)
            share.append(val[0:1, :])
        g_circ, g_radial = share
        part_geo[half, 0:1, :] = g_circ * g_radial
        part_geo[half, 1:2, :] = g_circ
        part_geo[half, 2:3, :] = g_radial * ctab[ROW_B : ROW_B + 1, :]

    def copy1(half, ah, i):
        t = plane_peers[i]
        return pltpu.make_async_remote_copy(
            src_ref=xsend.at[half, ah, t],
            dst_ref=xbuf.at[half, ah, :, pl.ds(pl.multiple_of(me * ZL, ZL), ZL), :],
            send_sem=s1.at[half, ah, i],
            recv_sem=r1.at[half, ah, i],
            device_id=(e, t),
            device_id_type=MESH,
        )

    def copy2(half, c, k, i):
        t = plane_peers[i]
        return pltpu.make_async_remote_copy(
            src_ref=fsend.at[half, c, pl.ds(2 * k, 2), pl.ds(pl.multiple_of(t * ZL, ZL), ZL), :],
            dst_ref=fbuf.at[half, c, me, pl.ds(2 * k, 2)],
            send_sem=s2.at[half, c, k, i],
            recv_sem=r2.at[half, c, k, i],
            device_id=(e, t),
            device_id_type=MESH,
        )

    def pack_first(ah):
        for c in range(3):
            for z8 in range(ZL // 8):
                nodes = pl.ds(pl.multiple_of(ah * 2 * N, 2 * N), 2 * N)
                tile = jnp.swapaxes(vin[pl.ds(c * ZL + z8 * 8, 8), nodes, :], 0, 1)
                for g, row in enumerate(block_transpose([tile[k] for k in range(2 * N)])):
                    xsend[g % HALVES, ah, g // HALVES, c, pl.ds(z8 * 8, 8), :] = row

    def send_first(half, ah):
        for i in range(NP - 1):
            copy1(half, ah, i).start()
        mine = pl.ds(pl.multiple_of(me * ZL, ZL), ZL)
        xbuf[half, ah, :, mine, :] = xsend[half, ah, me]

    loads[0].wait()
    pack_first(0)
    pl.semaphore_wait(barrier, NP - 1 + NE - 1)
    send_first(0, 0)

    def first(ah, carry):
        pack_first(ah)
        send_first(0, ah)
        return carry

    def first_rest(ah, carry):
        send_first(1, ah)
        return carry

    lax.fori_loop(1, AH, first, 0)
    lax.fori_loop(0, AH, first_rest, 0)

    acc[...] = jnp.zeros_like(acc)
    dots[...] = jnp.zeros_like(dots)
    row_i = lax.broadcasted_iota(jnp.int32, (ED, ED), 0)
    lane_i = lax.broadcasted_iota(jnp.int32, (ED, ED), 1)
    lid_l = jnp.broadcast_to(lid, (ED, ED))
    lid_t = jnp.transpose(lid_l.astype(F32)).astype(jnp.int32)

    def ones(where):
        return jnp.where(where, 1.0, 0.0).astype(BF16)

    tables[0] = ones(lid_t == ((lid_l & 64) | ((lid_l + 63) & 63)))
    tables[1] = ones(lid_t == ((lid_l & 64) | ((lid_l + 1) & 63)))
    tables[2] = ones((lid_t == (lid_l ^ 64)) & (lid_l >= 64))
    tables[3] = ones((lid_t == (lid_l ^ 64)) & (lid_l < 64))
    tables[4] = ones(lid_t == lane_i + 64)
    tables[5] = ones((lid_t == lane_i) & (lane_i >= 64))
    tables[6] = ones((lid_t == lane_i) & (lane_i < 64))
    tables[7] = ones(lid_t + 64 == lane_i)
    tables[8] = ones((row_i == lid_l) & (lid_l < 64))
    tables[9] = ones(row_i == lid_l + 64)
    tables[10] = ones(row_i + 64 == lid_l)
    tables[11] = ones((row_i == lid_l) & (lid_l >= 64))
    slot = me * ZL + (lax.broadcasted_iota(jnp.int32, (SYS, ED), 0) & (ZL - 1))
    kappa = jnp.where(slot == 1, Z // 2, slot // 2).astype(F32)
    hel[...] = (LAM + (STEP * kappa) * (STEP * kappa)) * geo[0:1, :]

    f_high = jnp.concatenate([mats[0], mats[1]], axis=1)
    f_low = jnp.concatenate([mats[2], mats[3]], axis=1)

    def between(half, carry):
        def arrive_first(ph, carry):
            for i in range(NP - 1):
                copy1(half, ph, i).wait_recv()
            w_ab = ctab[pl.ds(ROW_AB + ph, 1), :]
            mass = part_geo[half, 0:1, :] * w_ab
            g_y = part_geo[half, 1:2, :] * w_ab
            g_x = part_geo[half, 2:3, :]
            for c in range(3):
                fy_high, fy_low = split(xbuf[half, ph, 1] * xbuf[half, ph, c])
                dy = dot(fy_high, mats[4]) + dot(fy_low, mats[4]) + dot(fy_high, mats[5])
                acc[half, ph, c] += (LAM * mass) * xbuf[half, ph, c] - g_y * dy
                b_high, b_low = split(mass * (xbuf[half, ph, 2] * xbuf[half, ph, c]))
                bbuf[half, ph, 0, c] = b_high
                bbuf[half, ph, 1, c] = b_low
                for k in range(4):
                    rows = pl.ds(k * 32, 32)
                    fx = g_x * (xbuf[half, ph, 0, rows, :] * xbuf[half, ph, c, rows, :])
                    swap = pltpu.roll(fx, ED // 2, 1)
                    for ah in range(AH):
                        same = ctab[pl.ds(ROW_SAME + ph * AH + ah, 1), :]
                        other = ctab[pl.ds(ROW_SWAP + ph * AH + ah, 1), :]
                        acc[half, ah, c, rows, :] += same * fx + other * swap
            return carry

        def send_second(step, carry):
            c, k = step // 2, lax.rem(step, 2)
            for j in (0, 1):
                ah = 2 * k + j
                a_high, a_low = split(acc[half, ah, c])
                high = jnp.concatenate([a_high, bbuf[half, ah, 0, c]], axis=0)
                low = jnp.concatenate([a_low, bbuf[half, ah, 1, c]], axis=0)
                out = dot(f_high, high) + dot(f_high, low) + dot(f_low, high)
                fsend[half, c, ah] = pltpu.roll(out, EG * (HALVES * me + half), 1)
            for i in range(NP - 1):
                copy2(half, c, k, i).start()
            mine = pl.ds(pl.multiple_of(me * ZL, ZL), ZL)
            fbuf[half, c, me, pl.ds(2 * k, 2)] = fsend[half, c, pl.ds(2 * k, 2), mine, :]
            return carry

        lax.fori_loop(0, AH, arrive_first, 0)
        lax.fori_loop(0, 6, send_second, 0)
        return carry

    lax.fori_loop(0, HALVES, between, 0)

    def sys_rows(c):
        return pl.ds(pl.multiple_of(c * ZL, ZL), ZL)

    def r_halo(c, way):
        return pltpu.make_async_remote_copy(
            src_ref=rsend.at[c, way],
            dst_ref=rrecv.at[c, way],
            send_sem=hs1.at[c, way],
            recv_sem=hr1.at[c, way],
            device_id=((up, down)[way], me),
            device_id_type=MESH,
        )

    def q_halo(c, way):
        return pltpu.make_async_remote_copy(
            src_ref=qsend.at[c, way],
            dst_ref=qrecv.at[c, way],
            send_sem=hs2.at[c, way],
            recv_sem=hr2.at[c, way],
            device_id=((up, down)[way], me),
            device_id_type=MESH,
        )

    def side(v, rows, b, first, count):
        return jnp.concatenate([v[a * N + b, rows, :] for a in range(first, first + count)], axis=0)

    def pack_edges(v, c, pair, count):
        rows = sys_rows(c)
        packed = []
        for b, t in ((N - 1, 4), (0, 6)):
            for k in (0, 1):
                nodes = [v[(2 * (pair + i) + k) * N + b, rows, :] for i in range(count)]
                nodes = jnp.concatenate(nodes, axis=0) if count > 1 else nodes[0]
                packed.append(pick(nodes, tables[t + k]))
        return packed[0] + packed[1], packed[2] + packed[3]

    def send_q_edges(c):
        for way, got in enumerate(pack_edges(qv, c, 0, AH)):
            qsend[c, way] = got.reshape(AH, ZL, ED)
            q_halo(c, way).start()

    def take_edges(recv, c):
        for way in (0, 1):
            there = (e > 0) if way == 0 else (e < NE - 1)
            got = recv[c, way].reshape(AH * ZL, ED)
            for k in (0, 1):
                here = jnp.where(there, pick(got, tables[8 + 2 * way + k]), 0.0)
                here = here.reshape(AH, ZL, ED)
                for pair in range(AH):
                    edge[way, 2 * pair + k] = here[pair]

    def take_faces(v, c):
        sys = sys_rows(c)
        shape = (N, ZL, ED)
        face[2] = pick(side(v, sys, N - 1, 0, N), tables[2]).reshape(shape)
        face[3] = pick(side(v, sys, 0, 0, N), tables[3]).reshape(shape)
        face[0] = pick(v[(N - 1) * N : N * N, sys, :].reshape(N * ZL, ED), tables[0]).reshape(shape)
        face[1] = pick(v[0:N, sys, :].reshape(N * ZL, ED), tables[1]).reshape(shape)

    def apply_local(v, q, c, columns):
        def tile(h, carry):
            rows = pl.ds(pl.multiple_of(c * ZL + h * 8, 8), 8)
            frows = pl.ds(pl.multiple_of(h * 8, 8), 8)
            hm = hel[rows, :]
            kx = jnp.broadcast_to(geo[1:2, :], (8, ED))
            ky = jnp.broadcast_to(geo[2:3, :], (8, ED))
            nodes = [b for pair in columns for b in (pair, N - 1 - pair)]
            for b in nodes:
                col = stiff_times([v[a * N + b, rows, :] for a in range(N)], range(N // 2))
                scale_b = kx * float(WEIGHTS[b])
                for a in range(N):
                    q[a * N + b, rows, :] = scale_b * col[a]
            for a in range(N):
                vals = [v[a * N + b, rows, :] for b in range(N)]
                line = stiff_times(vals, columns)
                scale_a = ky * float(WEIGHTS[a])
                hm_a = hm * float(WEIGHTS[a])
                for b in nodes:
                    out = q[a * N + b, rows, :] + scale_a * line[b]
                    out = out + (hm_a * float(WEIGHTS[b])) * vals[b]
                    if a == 0:
                        out = out + float(PEN * WEIGHTS[b]) * (vals[b] - face[0, b, frows, :])
                    if a == N - 1:
                        out = out + float(PEN * WEIGHTS[b]) * (vals[b] - face[1, b, frows, :])
                    if b == 0:
                        out = out + float(PEN * WEIGHTS[a]) * (vals[b] - face[2, a, frows, :])
                    if b == N - 1:
                        out = out + float(PEN * WEIGHTS[a]) * (vals[b] - face[3, a, frows, :])
                    q[a * N + b, rows, :] = out
            return carry

        lax.fori_loop(0, ZL // 8, tile, 0)

    def add_edges(q, c):
        rows = sys_rows(c)
        for a in range(N):
            q[a * N, rows, :] -= float(PEN * WEIGHTS[a]) * edge[0, a]
            q[a * N + N - 1, rows, :] -= float(PEN * WEIGHTS[a]) * edge[1, a]

    def arrive_second(c, ah):
        groups = [fbuf[g % HALVES, c, g // HALVES, ah] for g in range(GROUPS)]
        for k, line in enumerate(block_transpose(groups, True)):
            res[ah * 2 * N + k, sys_rows(c), :] = line

    def dot_rows(first, k, count):
        return pl.ds(pl.multiple_of(first + (k % 2) * (ED // 2), 8), count)

    def begin(c):
        def arrive(ah, carry):
            arrive_second(c, ah)
            return carry

        def arrive_pair(k, carry):
            for half in range(HALVES):
                for i in range(NP - 1):
                    copy2(half, c, k, i).wait_recv()
            return lax.fori_loop(2 * k, 2 * k + 2, arrive, carry)

        lax.fori_loop(0, 2, arrive_pair, 0)
        for way, got in enumerate(pack_edges(res, c, 0, AH)):
            rsend[c, way] = got.reshape(AH, ZL, ED)
        take_faces(res, c)
        for way in (0, 1):
            r_halo(c, way).start()
        apply_local(res, qv, c, (0,))
        send_q_edges(c)
        apply_local(res, qv, c, (1, 2, 3))

    def end(c):
        for way in (0, 1):
            r_halo(c, way).wait_recv()
        take_edges(rrecv, c)
        add_edges(qv, c)
        take_faces(qv, c)
        apply_local(qv, pv, c, range(N // 2))

        def dot_tile(h, carry):
            rows = pl.ds(pl.multiple_of(c * ZL + h * 8, 8), 8)
            sums = [jnp.zeros((8, ED), F32) for _ in range(4)]
            for n in range(N * N):
                r_n, q_n, p_n = res[n, rows, :], qv[n, rows, :], pv[n, rows, :]
                for k, prod in enumerate((r_n * r_n, r_n * q_n, q_n * q_n, q_n * p_n)):
                    sums[k] = sums[k] + prod
            for k in range(4):
                dots[k // 2, dot_rows(c * ZL + h * 8, k, 8), :] = sums[k]
            return carry

        lax.fori_loop(0, ZL // 8, dot_tile, 0)
        for way in (0, 1):
            q_halo(c, way).wait_recv()
        take_edges(qrecv, c)
        rows = sys_rows(c)
        inner = jnp.broadcast_to(lid < 64, (ZL, ED)) & (e > 0)
        outer = jnp.broadcast_to(lid >= 64, (ZL, ED)) & (e < NE - 1)
        last = jnp.zeros((ZL, ED), F32)
        for a in range(N):
            w_a = float(PEN * WEIGHTS[a])
            for way, b, where in ((0, 0, inner), (1, N - 1, outer)):
                n = a * N + b
                got = w_a * (edge[way, a] - jnp.where(where, w_a * res[n, rows, :], 0.0))
                pv[n, rows, :] -= got
                last = last + qv[n, rows, :] * got
        dots[1, dot_rows(c * ZL, 3, ZL), :] -= last

    def begin_all(c, carry):
        begin(c)
        return carry

    def end_all(c, carry):
        end(c)
        return carry

    lax.fori_loop(0, 3, begin_all, 0)
    lax.fori_loop(0, 3, end_all, 0)

    one_rows = jnp.ones((8, ED), F32)
    for k in (0, 1):
        summed = lax.dot_general(
            one_rows,
            dots[k],
            (((1,), (1,)), ((), ())),
            precision=lax.Precision.HIGHEST,
            preferred_element_type=F32,
        )
        rbuf[0, k : k + 1, :] = summed[0:1, :]

    def spread(i):
        return pltpu.make_async_remote_copy(
            src_ref=rbuf.at[0],
            dst_ref=rbuf.at[i + 1],
            send_sem=rs.at[i],
            recv_sem=rr.at[i],
            device_id=(elem_peers[i], me),
            device_id_type=MESH,
        )

    for i in range(NE - 1):
        spread(i).start()
    for i in range(NE - 1):
        spread(i).wait_recv()
    part = jnp.sum(rbuf[...], axis=0)

    swapped = pltpu.roll(jnp.concatenate([part] * 4, axis=0), ED // 2, 1)
    aa, bb, cc, ee = part[0:1, :], swapped[0:1, :], part[1:2, :], swapped[1:2, :]
    alpha = aa / bb
    rr1 = alpha * alpha * cc - aa
    beta1 = 1.0 + rr1 / aa
    alpha1 = rr1 / (beta1 * beta1 * bb - 2.0 * beta1 * alpha * cc + alpha * alpha * ee)
    coef_s = alpha + alpha1 * beta1
    coef_t = alpha1 * alpha
    row8 = lax.broadcasted_iota(jnp.int32, (8, ED), 0)
    both = jnp.where(row8 == 0, coef_s, coef_t)
    both = jnp.where(lax.broadcasted_iota(jnp.int32, (8, ED), 1) < SYS, both, 0.0)
    both = jnp.transpose(jnp.concatenate([both] + [jnp.zeros((8, ED), F32)] * 15, axis=0))
    coef_out[0] = jnp.broadcast_to(both[0:SYS, 0:1], (SYS, ED))
    coef_out[1] = jnp.broadcast_to(both[0:SYS, 1:2], (SYS, ED))

    def drain(ah, carry):
        for half in range(HALVES):
            for i in range(NP - 1):
                copy1(half, ah, i).wait_send()
        return carry

    def drain2(step, carry):
        for half in range(HALVES):
            for i in range(NP - 1):
                copy2(half, step // 2, lax.rem(step, 2), i).wait_send()
        return carry

    def drain3(c, carry):
        for way in (0, 1):
            r_halo(c, way).wait_send()
            q_halo(c, way).wait_send()
        return carry

    lax.fori_loop(0, AH, drain, 0)
    lax.fori_loop(0, 6, drain2, 0)
    lax.fori_loop(0, 3, drain3, 0)
    for i in range(NE - 1):
        spread(i).wait_send()


def finish_kernel(r, q, p, coef, x_out, r_out, xs, rs, sem):
    def tile(st, carry):
        rows = pl.ds(pl.multiple_of(st * 8, 8), 8)
        s, t = coef[0, rows, :], coef[1, rows, :]
        for a in range(N):
            new, left = [], []
            for n in range(a * N, a * N + N):
                r_n, q_n, p_n = r[n, rows, :], q[n, rows, :], p[n, rows, :]
                new.append(s * r_n - t * q_n)
                left.append(r_n - s * q_n + t * p_n)
            for buf, vals in ((xs, new), (rs, left)):
                vals = jnp.swapaxes(jnp.stack(vals), 0, 1)
                for k in range(8):
                    buf[st, pl.ds(k * N * N + a * N, N), :] = vals[k]
        for copy in out_copies(st):
            copy.start()
        return carry

    def out_copies(st):
        return (
            pltpu.make_async_copy(xs.at[st], x_out.at[st], sem.at[st, 0]),
            pltpu.make_async_copy(rs.at[st], r_out.at[st], sem.at[st, 1]),
        )

    def drain(st, carry):
        for copy in out_copies(st):
            copy.wait()
        return carry

    lax.fori_loop(0, SYS // 8, tile, 0)
    lax.fori_loop(0, SYS // 8, drain, 0)


def on_device(velocity, elem_scale, elem_ids, edge_blocks):
    vel = velocity.reshape(SYS, N * N, ED)
    rows = np.zeros((ROWS, ED))
    table = -WEIGHTS[:, None] * DERIV
    for ph in range(AH):
        for ah in range(AH):
            for i in (0, 1):
                lanes = slice(i * ED // 2, (i + 1) * ED // 2)
                rows[ROW_SAME + ph * AH + ah, lanes] = table[2 * ah + i, 2 * ph + i]
                rows[ROW_SWAP + ph * AH + ah, lanes] = table[2 * ah + i, 2 * ph + 1 - i]
    for ah in range(AH):
        rows[ROW_AB + ah] = np.repeat(np.outer(WEIGHTS[2 * ah : 2 * ah + 2], WEIGHTS).ravel(), EG)
    rows[ROW_B] = np.repeat(np.tile(WEIGHTS, 2), EG)
    rows = jnp.asarray(rows, F32)
    four = halves(mode_matrix()).reshape(2, Z, 2, Z).transpose(0, 2, 1, 3).reshape(4, Z, Z)
    mats = jnp.asarray(np.concatenate([four, halves(np.kron(np.eye(2), np.kron(DERIV.T, np.eye(EG))))]))
    operands = (vel, elem_scale, elem_ids, rows, mats)
    vmem = pl.BlockSpec(memory_space=pltpu.VMEM)
    hbm = pl.BlockSpec(memory_space=pltpu.HBM)
    field = jax.ShapeDtypeStruct((N * N, SYS, ED), F32)
    dma = pltpu.SemaphoreType.DMA
    r0, q0, p0, coef = pl.pallas_call(
        kernel,
        out_shape=(field, field, field, jax.ShapeDtypeStruct((2, SYS, ED), F32)),
        in_specs=[hbm] * 5,
        out_specs=(vmem,) * 4,
        scratch_shapes=[
            pltpu.VMEM((SYS, N * N, ED), F32),
            pltpu.VMEM((2, ED), F32),
            pltpu.VMEM((1, ED), jnp.int32),
            pltpu.VMEM((ROWS, ED), F32),
            pltpu.VMEM((6, ED, ED), BF16),
            pltpu.VMEM((HALVES, AH, NP, 3, ZL, ED), F32),
            pltpu.VMEM((HALVES, AH, 3, Z, ED), F32),
            pltpu.VMEM((HALVES, AH, 3, Z, ED), F32),
            pltpu.VMEM((HALVES, AH, 2, 3, Z, ED), BF16),
            pltpu.VMEM((HALVES, 3, AH, Z, ED), F32),
            pltpu.VMEM((HALVES, 3, NP, AH, ZL, ED), F32),
            pltpu.VMEM((8, ED), F32),
            pltpu.VMEM((HALVES, 8, ED), F32),
            pltpu.VMEM((SYS, ED), F32),
            pltpu.VMEM((12, ED, ED), BF16),
            pltpu.VMEM((4, N, ZL, ED), F32),
            pltpu.VMEM((2, N, ZL, ED), F32),
            pltpu.VMEM((3, 2, AH, ZL, ED), F32),
            pltpu.VMEM((3, 2, AH, ZL, ED), F32),
            pltpu.VMEM((3, 2, AH, ZL, ED), F32),
            pltpu.VMEM((3, 2, AH, ZL, ED), F32),
            pltpu.VMEM((2, ED, ED), F32),
            pltpu.VMEM((NE, 2, ED), F32),
            dma((5,)),
            dma((HALVES, AH, NP - 1)),
            dma((HALVES, AH, NP - 1)),
            dma((HALVES, 3, 2, NP - 1)),
            dma((HALVES, 3, 2, NP - 1)),
            dma((3, 2)),
            dma((3, 2)),
            dma((3, 2)),
            dma((3, 2)),
            dma((NE - 1,)),
            dma((NE - 1,)),
        ],
        compiler_params=pltpu.CompilerParams(
            collective_id=0, has_side_effects=True, vmem_limit_bytes=48 * 1024 * 1024
        ),
        name="exchange_and_apply",
    )(*[pltpu.with_memory_space_constraint(v, pltpu.HBM) for v in operands])

    flat = jax.ShapeDtypeStruct((SYS // 8, 8 * N * N, ED), F32)
    new, left = pl.pallas_call(
        finish_kernel,
        out_shape=(flat, flat),
        in_specs=[vmem] * 4,
        out_specs=(hbm, hbm),
        scratch_shapes=[
            pltpu.VMEM(flat.shape, F32),
            pltpu.VMEM(flat.shape, F32),
            dma((SYS // 8, 2)),
        ],
        compiler_params=pltpu.CompilerParams(vmem_limit_bytes=16 * 1024 * 1024),
        name="finish",
    )(r0, q0, p0, coef)
    shape = (3, ZL, N, N, ED)
    return new.reshape(shape), left.reshape(shape)


def solution(mesh):
    in_specs = (
        P(None, "plane", None, None, "elem"),
        P(None, "elem"),
        P("elem", None),
        P("elem", None, None),
    )
    out_specs = (P(None, "plane", None, None, "elem"), P(None, "plane", None, None, "elem"))
    return jax.shard_map(
        on_device, mesh=mesh, in_specs=in_specs, out_specs=out_specs, check_vma=False
    )
```

```python
import functools
import math

import jax
import jax.numpy as jnp
import ml_dtypes
import numpy as np
from jax import lax
from jax.experimental import pallas as pl
from jax.experimental.pallas import tpu as pltpu
from jax.sharding import PartitionSpec as P

MESH = pl.DeviceIdType.MESH
F32 = jnp.float32
BF16 = jnp.bfloat16

N = 8
ED = 128
Z = 128
NP = 8
ZL = Z // NP
HALVES = 2
GROUPS = NP * HALVES
EG = ED // GROUPS
AH = N // 2
SYS = 3 * ZL
NX = 4
NZ = 8
NE = NX * NZ
PEN = 8.0
ROW_SAME, ROW_SWAP, ROW_AB, ROW_B = 0, AH * AH, 2 * AH * AH, 2 * AH * AH + AH
ROWS = 40
LAM = 4.0
STEP = 0.1


def node_tables():
    degree = N - 1
    points = -np.cos(np.pi * np.arange(N) / degree)
    scales = np.ones(N)
    scales[0] = 2.0
    scales[-1] = 2.0
    bary = (-1.0) ** np.arange(N) / scales
    deriv = np.zeros((N, N))
    for i in range(N):
        for j in range(N):
            if i != j:
                deriv[i, j] = bary[j] / bary[i] / (points[i] - points[j])
        deriv[i, i] = -np.sum(deriv[i])
    weights = np.zeros(N)
    for i in range(N):
        running = 0.0
        for k in range(1, degree // 2 + 1):
            factor = 1.0 if 2 * k == degree else 2.0
            running += factor / (4.0 * k * k - 1.0) * np.cos(2.0 * np.pi * i * k / degree)
        weights[i] = (1.0 if i in (0, degree) else 2.0) / degree * (1.0 - running)
    stiff = deriv.T @ (weights[:, None] * deriv)
    return deriv, weights, stiff


def mode_matrix():
    slots = np.arange(Z)
    harmonic = slots // 2
    angles = 2.0 * math.pi / Z * (harmonic[:, None] * slots[None, :] % Z)
    four = np.where((slots % 2 == 0)[:, None], np.cos(angles), np.sin(angles)) * (2.0 / Z)
    four[0] = 1.0 / Z
    four[1] = np.where(slots % 2 == 0, 1.0, -1.0) / Z
    dz = np.zeros((Z, Z))
    wave = STEP * np.arange(Z // 2)
    dz[0::2] = wave[:, None] * four[1::2]
    dz[1::2] = -wave[:, None] * four[0::2]
    return np.concatenate([four, -dz], axis=1)


def halves(table):
    high = table.astype(np.float32).astype(ml_dtypes.bfloat16)
    low = (table - high.astype(np.float64)).astype(np.float32).astype(ml_dtypes.bfloat16)
    return np.stack([high, low])


DERIV, WEIGHTS, STIFF = node_tables()


def split(x):
    high = x.astype(BF16)
    return high, (x - high.astype(F32)).astype(BF16)


def dot(x, y):
    return jnp.dot(x, y, preferred_element_type=F32)


def pick(x, table):
    high, low = split(x)
    return dot(high, table) + dot(low, table)


def turned(x, groups):
    shift = EG * (groups % GROUPS)
    return pltpu.roll(x, shift, x.ndim - 1) if shift else x


def block_transpose(rows, turned_before=False):
    if not turned_before:
        rows = [turned(x, i) for i, x in enumerate(rows)]
    lane = lax.broadcasted_iota(jnp.int32, rows[0].shape, rows[0].ndim - 1) // EG
    d = 1
    while d < GROUPS:
        clear = (lane & d) == 0
        rows = [jnp.where(clear, rows[i], rows[(i + d) % GROUPS]) for i in range(GROUPS)]
        d *= 2
    return [turned(rows[-g % GROUPS], -g) for g in range(GROUPS)]


def stiff_times(v, wanted):
    even = [v[p] + v[N - 1 - p] for p in range(N // 2)]
    odd = [v[p] - v[N - 1 - p] for p in range(N // 2)]
    out = [None] * N
    for a in wanted:
        s = [0.5 * (STIFF[a, p] + STIFF[a, N - 1 - p]) for p in range(N // 2)]
        t = [0.5 * (STIFF[a, p] - STIFF[a, N - 1 - p]) for p in range(N // 2)]
        e = sum(float(s[p]) * even[p] for p in range(1, N // 2)) + float(s[0]) * even[0]
        o = sum(float(t[p]) * odd[p] for p in range(1, N // 2)) + float(t[0]) * odd[0]
        out[a] = e + o
        out[N - 1 - a] = e - o
    return out


def kernel(
    vel,
    scale_in,
    ids_in,
    rows_in,
    mats_in,
    res,
    qv,
    pv,
    coef_out,
    vin,
    scale,
    ids,
    ctab,
    mats,
    xsend,
    xbuf,
    acc,
    bbuf,
    fsend,
    fbuf,
    geo,
    part_geo,
    hel,
    tables,
    face,
    edge,
    rsend,
    rrecv,
    qsend,
    qrecv,
    dots,
    rbuf,
    in_sem,
    s1,
    r1,
    s2,
    r2,
    hs1,
    hr1,
    hs2,
    hr2,
    rs,
    rr,
):
    e = lax.axis_index("elem")
    me = lax.axis_index("plane")
    y, core = me // 2, lax.rem(me, 2)
    z, x = e // NX, lax.rem(e, NX)
    plane_offsets = [(dy, dc) for dy in (2, 1, 3, 0) for dc in (0, 1) if (dy, dc) != (0, 0)]
    plane_peers = [lax.rem(y + dy, 4) * 2 + lax.rem(core + dc, 2) for dy, dc in plane_offsets]
    elem_peers = [
        lax.rem(z + dz, NZ) * NX + lax.rem(x + dx, NX)
        for dz in (4, 3, 5, 2, 6, 1, 7, 0)
        for dx in (2, 1, 3, 0)
        if (dz, dx) != (0, 0)
    ]
    up, down = lax.rem(e + 1, NE), lax.rem(e + NE - 1, NE)

    pairs = ((vel, vin), (scale_in, scale), (ids_in, ids), (rows_in, ctab), (mats_in, mats))
    loads = [pltpu.make_async_copy(src, dst, in_sem.at[i]) for i, (src, dst) in enumerate(pairs)]
    for load in loads:
        load.start()
    barrier = pltpu.get_barrier_semaphore()
    for t in plane_peers:
        pl.semaphore_signal(barrier, inc=1, device_id=(e, t), device_id_type=MESH)
    for t in elem_peers:
        pl.semaphore_signal(barrier, inc=1, device_id=(t, me), device_id_type=MESH)

    def copy1(half, ah, i):
        t = plane_peers[i]
        return pltpu.make_async_remote_copy(
            src_ref=xsend.at[half, ah, t],
            dst_ref=xbuf.at[half, ah, :, pl.ds(pl.multiple_of(me * ZL, ZL), ZL), :],
            send_sem=s1.at[half, ah, i],
            recv_sem=r1.at[half, ah, i],
            device_id=(e, t),
            device_id_type=MESH,
        )

    def copy2(half, c, k, i):
        t = plane_peers[i]
        return pltpu.make_async_remote_copy(
            src_ref=fsend.at[half, c, pl.ds(2 * k, 2), pl.ds(pl.multiple_of(t * ZL, ZL), ZL), :],
            dst_ref=fbuf.at[half, c, me, pl.ds(2 * k, 2)],
            send_sem=s2.at[half, c, k, i],
            recv_sem=r2.at[half, c, k, i],
            device_id=(e, t),
            device_id_type=MESH,
        )

    def pack_first(ah):
        for c in range(3):
            for z8 in range(ZL // 8):
                nodes = pl.ds(pl.multiple_of(ah * 2 * N, 2 * N), 2 * N)
                tile = jnp.swapaxes(vin[pl.ds(c * ZL + z8 * 8, 8), nodes, :], 0, 1)
                for g, row in enumerate(block_transpose([tile[k] for k in range(2 * N)])):
                    xsend[g % HALVES, ah, g // HALVES, c, pl.ds(z8 * 8, 8), :] = row

    def send_first(half, ah):
        for i in range(NP - 1):
            copy1(half, ah, i).start()
        mine = pl.ds(pl.multiple_of(me * ZL, ZL), ZL)
        xbuf[half, ah, :, mine, :] = xsend[half, ah, me]

    loads[0].wait()
    pack_first(0)
    pl.semaphore_wait(barrier, NP - 1 + NE - 1)
    send_first(0, 0)

    def first(ah, carry):
        pack_first(ah)
        send_first(0, ah)
        return carry

    def first_rest(ah, carry):
        send_first(1, ah)
        return carry

    lax.fori_loop(1, AH, first, 0)
    lax.fori_loop(0, AH, first_rest, 0)

    for load in loads[1:]:
        load.wait()

    lid = ids[...] & (ED - 1)
    growth = 1.0 + 2.0 * (ids[...] // 64).astype(F32) / 63.0
    circ = scale[0:1, :] * growth
    radial = scale[1:2, :]
    geo[0:1, :] = circ * radial
    geo[1:2, :] = radial / circ
    geo[2:3, :] = circ / radial
    for half in range(HALVES):
        share = []
        for val in (circ, radial):
            first = ED - EG * (HALVES * me + half)
            val = pltpu.roll(jnp.broadcast_to(val, (8, ED)), lax.rem(first, ED), 1)
            val = jnp.where(lax.broadcasted_iota(jnp.int32, (8, ED), 1) < EG, val, 0.0)
            for d in (1, 2, 4, 8):
                val = val + pltpu.roll(val, EG * d, 1)
            share.append(val[0:1, :])
        g_circ, g_radial = share
        part_geo[half, 0:1, :] = g_circ * g_radial
        part_geo[half, 1:2, :] = g_circ
        part_geo[half, 2:3, :] = g_radial * ctab[ROW_B : ROW_B + 1, :]

    acc[...] = jnp.zeros_like(acc)
    dots[...] = jnp.zeros_like(dots)
    row_i = lax.broadcasted_iota(jnp.int32, (ED, ED), 0)
    lane_i = lax.broadcasted_iota(jnp.int32, (ED, ED), 1)
    lid_l = jnp.broadcast_to(lid, (ED, ED))
    lid_t = jnp.transpose(lid_l.astype(F32)).astype(jnp.int32)

    def ones(where):
        return jnp.where(where, 1.0, 0.0).astype(BF16)

    tables[0] = ones(lid_t == ((lid_l & 64) | ((lid_l + 63) & 63)))
    tables[1] = ones(lid_t == ((lid_l & 64) | ((lid_l + 1) & 63)))
    tables[2] = ones((lid_t == (lid_l ^ 64)) & (lid_l >= 64))
    tables[3] = ones((lid_t == (lid_l ^ 64)) & (lid_l < 64))
    tables[4] = ones(lid_t == lane_i + 64)
    tables[5] = ones((lid_t == lane_i) & (lane_i >= 64))
    tables[6] = ones((lid_t == lane_i) & (lane_i < 64))
    tables[7] = ones(lid_t + 64 == lane_i)
    tables[8] = ones((row_i == lid_l) & (lid_l < 64))
    tables[9] = ones(row_i == lid_l + 64)
    tables[10] = ones(row_i + 64 == lid_l)
    tables[11] = ones((row_i == lid_l) & (lid_l >= 64))
    slot = me * ZL + (lax.broadcasted_iota(jnp.int32, (SYS, ED), 0) & (ZL - 1))
    kappa = jnp.where(slot == 1, Z // 2, slot // 2).astype(F32)
    hel[...] = (LAM + (STEP * kappa) * (STEP * kappa)) * geo[0:1, :]

    f_high = jnp.concatenate([mats[0], mats[1]], axis=1)
    f_low = jnp.concatenate([mats[2], mats[3]], axis=1)

    def between(half, carry):
        def arrive_first(ph, carry):
            for i in range(NP - 1):
                copy1(half, ph, i).wait_recv()
            w_ab = ctab[pl.ds(ROW_AB + ph, 1), :]
            mass = part_geo[half, 0:1, :] * w_ab
            g_y = part_geo[half, 1:2, :] * w_ab
            g_x = part_geo[half, 2:3, :]
            for c in range(3):
                fy_high, fy_low = split(xbuf[half, ph, 1] * xbuf[half, ph, c])
                dy = dot(fy_high, mats[4]) + dot(fy_low, mats[4]) + dot(fy_high, mats[5])
                acc[half, ph, c] += (LAM * mass) * xbuf[half, ph, c] - g_y * dy
                b_high, b_low = split(mass * (xbuf[half, ph, 2] * xbuf[half, ph, c]))
                bbuf[half, ph, 0, c] = b_high
                bbuf[half, ph, 1, c] = b_low
                for k in range(4):
                    rows = pl.ds(k * 32, 32)
                    fx = g_x * (xbuf[half, ph, 0, rows, :] * xbuf[half, ph, c, rows, :])
                    swap = pltpu.roll(fx, ED // 2, 1)
                    for ah in range(AH):
                        same = ctab[pl.ds(ROW_SAME + ph * AH + ah, 1), :]
                        other = ctab[pl.ds(ROW_SWAP + ph * AH + ah, 1), :]
                        acc[half, ah, c, rows, :] += same * fx + other * swap
            return carry

        def send_second(step, carry):
            c, k = step // 2, lax.rem(step, 2)
            for j in (0, 1):
                ah = 2 * k + j
                a_high, a_low = split(acc[half, ah, c])
                high = jnp.concatenate([a_high, bbuf[half, ah, 0, c]], axis=0)
                low = jnp.concatenate([a_low, bbuf[half, ah, 1, c]], axis=0)
                out = dot(f_high, high) + dot(f_high, low) + dot(f_low, high)
                fsend[half, c, ah] = pltpu.roll(out, EG * (HALVES * me + half), 1)
            for i in range(NP - 1):
                copy2(half, c, k, i).start()
            mine = pl.ds(pl.multiple_of(me * ZL, ZL), ZL)
            fbuf[half, c, me, pl.ds(2 * k, 2)] = fsend[half, c, pl.ds(2 * k, 2), mine, :]
            return carry

        lax.fori_loop(0, AH, arrive_first, 0)
        lax.fori_loop(0, 6, send_second, 0)
        return carry

    lax.fori_loop(0, HALVES, between, 0)

    def sys_rows(c):
        return pl.ds(pl.multiple_of(c * ZL, ZL), ZL)

    def r_halo(c, way, k):
        return pltpu.make_async_remote_copy(
            src_ref=rsend.at[c, way, pl.ds(2 * k, 2)],
            dst_ref=rrecv.at[c, way, pl.ds(2 * k, 2)],
            send_sem=hs1.at[c, way, k],
            recv_sem=hr1.at[c, way, k],
            device_id=((up, down)[way], me),
            device_id_type=MESH,
        )

    def q_halo(c, way):
        return pltpu.make_async_remote_copy(
            src_ref=qsend.at[c, way],
            dst_ref=qrecv.at[c, way],
            send_sem=hs2.at[c, way],
            recv_sem=hr2.at[c, way],
            device_id=((up, down)[way], me),
            device_id_type=MESH,
        )

    def side(v, rows, b, first, count):
        return jnp.concatenate([v[a * N + b, rows, :] for a in range(first, first + count)], axis=0)

    def pack_edges(v, c, pair, count):
        rows = sys_rows(c)
        packed = []
        for b, t in ((N - 1, 4), (0, 6)):
            for k in (0, 1):
                nodes = [v[(2 * (pair + i) + k) * N + b, rows, :] for i in range(count)]
                nodes = jnp.concatenate(nodes, axis=0) if count > 1 else nodes[0]
                packed.append(pick(nodes, tables[t + k]))
        return packed[0] + packed[1], packed[2] + packed[3]

    def send_q_edges(c):
        for way, got in enumerate(pack_edges(qv, c, 0, AH)):
            qsend[c, way] = got.reshape(AH, ZL, ED)
            q_halo(c, way).start()

    def take_edges(recv, c):
        for way in (0, 1):
            there = (e > 0) if way == 0 else (e < NE - 1)
            got = recv[c, way].reshape(AH * ZL, ED)
            for k in (0, 1):
                here = jnp.where(there, pick(got, tables[8 + 2 * way + k]), 0.0)
                here = here.reshape(AH, ZL, ED)
                for pair in range(AH):
                    edge[way, 2 * pair + k] = here[pair]

    def take_faces(v, c):
        sys = sys_rows(c)
        shape = (N, ZL, ED)
        face[2] = pick(side(v, sys, N - 1, 0, N), tables[2]).reshape(shape)
        face[3] = pick(side(v, sys, 0, 0, N), tables[3]).reshape(shape)
        face[0] = pick(v[(N - 1) * N : N * N, sys, :].reshape(N * ZL, ED), tables[0]).reshape(shape)
        face[1] = pick(v[0:N, sys, :].reshape(N * ZL, ED), tables[1]).reshape(shape)

    def apply_local(v, q, c, columns):
        def tile(h, carry):
            rows = pl.ds(pl.multiple_of(c * ZL + h * 8, 8), 8)
            frows = pl.ds(pl.multiple_of(h * 8, 8), 8)
            hm = hel[rows, :]
            kx = jnp.broadcast_to(geo[1:2, :], (8, ED))
            ky = jnp.broadcast_to(geo[2:3, :], (8, ED))
            nodes = [b for pair in columns for b in (pair, N - 1 - pair)]
            for b in nodes:
                col = stiff_times([v[a * N + b, rows, :] for a in range(N)], range(N // 2))
                scale_b = kx * float(WEIGHTS[b])
                for a in range(N):
                    q[a * N + b, rows, :] = scale_b * col[a]
            for a in range(N):
                vals = [v[a * N + b, rows, :] for b in range(N)]
                line = stiff_times(vals, columns)
                scale_a = ky * float(WEIGHTS[a])
                hm_a = hm * float(WEIGHTS[a])
                for b in nodes:
                    out = q[a * N + b, rows, :] + scale_a * line[b]
                    out = out + (hm_a * float(WEIGHTS[b])) * vals[b]
                    if a == 0:
                        out = out + float(PEN * WEIGHTS[b]) * (vals[b] - face[0, b, frows, :])
                    if a == N - 1:
                        out = out + float(PEN * WEIGHTS[b]) * (vals[b] - face[1, b, frows, :])
                    if b == 0:
                        out = out + float(PEN * WEIGHTS[a]) * (vals[b] - face[2, a, frows, :])
                    if b == N - 1:
                        out = out + float(PEN * WEIGHTS[a]) * (vals[b] - face[3, a, frows, :])
                    q[a * N + b, rows, :] = out
            return carry

        lax.fori_loop(0, ZL // 8, tile, 0)

    def add_edges(q, c):
        rows = sys_rows(c)
        for a in range(N):
            q[a * N, rows, :] -= float(PEN * WEIGHTS[a]) * edge[0, a]
            q[a * N + N - 1, rows, :] -= float(PEN * WEIGHTS[a]) * edge[1, a]

    def arrive_second(c, ah):
        groups = [fbuf[g % HALVES, c, g // HALVES, ah] for g in range(GROUPS)]
        for k, line in enumerate(block_transpose(groups, True)):
            res[ah * 2 * N + k, sys_rows(c), :] = line

    def dot_rows(first, k, count):
        return pl.ds(pl.multiple_of(first + (k % 2) * (ED // 2), 8), count)

    def begin(c):
        def arrive(ah, carry):
            arrive_second(c, ah)
            return carry

        for k in (0, 1):
            for half in range(HALVES):
                for i in range(NP - 1):
                    copy2(half, c, k, i).wait_recv()
            lax.fori_loop(2 * k, 2 * k + 2, arrive, 0)
            for way, got in enumerate(pack_edges(res, c, 2 * k, 2)):
                rsend[c, way, pl.ds(2 * k, 2)] = got.reshape(2, ZL, ED)
            if k == 1:
                take_faces(res, c)
            for way in (0, 1):
                r_halo(c, way, k).start()
        apply_local(res, qv, c, (0,))
        send_q_edges(c)
        apply_local(res, qv, c, (1, 2, 3))

    def end(c):
        for way in (0, 1):
            for k in (0, 1):
                r_halo(c, way, k).wait_recv()
        take_edges(rrecv, c)
        add_edges(qv, c)
        take_faces(qv, c)
        apply_local(qv, pv, c, range(N // 2))

        def dot_tile(h, carry):
            rows = pl.ds(pl.multiple_of(c * ZL + h * 8, 8), 8)
            sums = [jnp.zeros((8, ED), F32) for _ in range(4)]
            for n in range(N * N):
                r_n, q_n, p_n = res[n, rows, :], qv[n, rows, :], pv[n, rows, :]
                for k, prod in enumerate((r_n * r_n, r_n * q_n, q_n * q_n, q_n * p_n)):
                    sums[k] = sums[k] + prod
            for k in range(4):
                dots[k // 2, dot_rows(c * ZL + h * 8, k, 8), :] = sums[k]
            return carry

        lax.fori_loop(0, ZL // 8, dot_tile, 0)
        for way in (0, 1):
            q_halo(c, way).wait_recv()
        take_edges(qrecv, c)
        rows = sys_rows(c)
        inner = jnp.broadcast_to(lid < 64, (ZL, ED)) & (e > 0)
        outer = jnp.broadcast_to(lid >= 64, (ZL, ED)) & (e < NE - 1)
        last = jnp.zeros((ZL, ED), F32)
        for a in range(N):
            w_a = float(PEN * WEIGHTS[a])
            for way, b, where in ((0, 0, inner), (1, N - 1, outer)):
                n = a * N + b
                got = w_a * (edge[way, a] - jnp.where(where, w_a * res[n, rows, :], 0.0))
                pv[n, rows, :] -= got
                last = last + qv[n, rows, :] * got
        dots[1, dot_rows(c * ZL, 3, ZL), :] -= last

    def begin_all(c, carry):
        begin(c)
        return carry

    def end_all(c, carry):
        end(c)
        return carry

    lax.fori_loop(0, 2, begin_all, 0)
    end(0)
    begin(2)
    lax.fori_loop(1, 3, end_all, 0)

    one_rows = jnp.ones((8, ED), F32)
    for k in (0, 1):
        summed = lax.dot_general(
            one_rows,
            dots[k],
            (((1,), (1,)), ((), ())),
            precision=lax.Precision.HIGHEST,
            preferred_element_type=F32,
        )
        rbuf[0, k : k + 1, :] = summed[0:1, :]

    def spread(i):
        return pltpu.make_async_remote_copy(
            src_ref=rbuf.at[0],
            dst_ref=rbuf.at[i + 1],
            send_sem=rs.at[i],
            recv_sem=rr.at[i],
            device_id=(elem_peers[i], me),
            device_id_type=MESH,
        )

    for i in range(NE - 1):
        spread(i).start()
    for i in range(NE - 1):
        spread(i).wait_recv()
    part = jnp.sum(rbuf[...], axis=0)

    swapped = pltpu.roll(jnp.concatenate([part] * 4, axis=0), ED // 2, 1)
    aa, bb, cc, ee = part[0:1, :], swapped[0:1, :], part[1:2, :], swapped[1:2, :]
    alpha = aa / bb
    rr1 = alpha * alpha * cc - aa
    beta1 = 1.0 + rr1 / aa
    alpha1 = rr1 / (beta1 * beta1 * bb - 2.0 * beta1 * alpha * cc + alpha * alpha * ee)
    coef_s = alpha + alpha1 * beta1
    coef_t = alpha1 * alpha
    row8 = lax.broadcasted_iota(jnp.int32, (8, ED), 0)
    both = jnp.where(row8 == 0, coef_s, coef_t)
    both = jnp.where(lax.broadcasted_iota(jnp.int32, (8, ED), 1) < SYS, both, 0.0)
    both = jnp.transpose(jnp.concatenate([both] + [jnp.zeros((8, ED), F32)] * 15, axis=0))
    coef_out[0] = jnp.broadcast_to(both[0:SYS, 0:1], (SYS, ED))
    coef_out[1] = jnp.broadcast_to(both[0:SYS, 1:2], (SYS, ED))

    def drain(ah, carry):
        for half in range(HALVES):
            for i in range(NP - 1):
                copy1(half, ah, i).wait_send()
        return carry

    def drain2(step, carry):
        for half in range(HALVES):
            for i in range(NP - 1):
                copy2(half, step // 2, lax.rem(step, 2), i).wait_send()
        return carry

    def drain3(c, carry):
        for way in (0, 1):
            for k in (0, 1):
                r_halo(c, way, k).wait_send()
            q_halo(c, way).wait_send()
        return carry

    lax.fori_loop(0, AH, drain, 0)
    lax.fori_loop(0, 6, drain2, 0)
    lax.fori_loop(0, 3, drain3, 0)
    for i in range(NE - 1):
        spread(i).wait_send()


def finish_kernel(r, q, p, coef, x_out, r_out, xs, rs, sem):
    def tile(st, carry):
        rows = pl.ds(pl.multiple_of(st * 8, 8), 8)
        s, t = coef[0, rows, :], coef[1, rows, :]
        for a in range(N):
            new, left = [], []
            for n in range(a * N, a * N + N):
                r_n, q_n, p_n = r[n, rows, :], q[n, rows, :], p[n, rows, :]
                new.append(s * r_n - t * q_n)
                left.append(r_n - s * q_n + t * p_n)
            for buf, vals in ((xs, new), (rs, left)):
                vals = jnp.swapaxes(jnp.stack(vals), 0, 1)
                for k in range(8):
                    buf[st, pl.ds(k * N * N + a * N, N), :] = vals[k]
        for copy in out_copies(st):
            copy.start()
        return carry

    def out_copies(st):
        return (
            pltpu.make_async_copy(xs.at[st], x_out.at[st], sem.at[st, 0]),
            pltpu.make_async_copy(rs.at[st], r_out.at[st], sem.at[st, 1]),
        )

    def drain(st, carry):
        for copy in out_copies(st):
            copy.wait()
        return carry

    lax.fori_loop(0, SYS // 8, tile, 0)
    lax.fori_loop(0, SYS // 8, drain, 0)


def on_device(velocity, elem_scale, elem_ids, edge_blocks):
    vel = velocity.reshape(SYS, N * N, ED)
    rows = np.zeros((ROWS, ED))
    table = -WEIGHTS[:, None] * DERIV
    for ph in range(AH):
        for ah in range(AH):
            for i in (0, 1):
                lanes = slice(i * ED // 2, (i + 1) * ED // 2)
                rows[ROW_SAME + ph * AH + ah, lanes] = table[2 * ah + i, 2 * ph + i]
                rows[ROW_SWAP + ph * AH + ah, lanes] = table[2 * ah + i, 2 * ph + 1 - i]
    for ah in range(AH):
        rows[ROW_AB + ah] = np.repeat(np.outer(WEIGHTS[2 * ah : 2 * ah + 2], WEIGHTS).ravel(), EG)
    rows[ROW_B] = np.repeat(np.tile(WEIGHTS, 2), EG)
    rows = jnp.asarray(rows, F32)
    four = halves(mode_matrix()).reshape(2, Z, 2, Z).transpose(0, 2, 1, 3).reshape(4, Z, Z)
    mats = jnp.asarray(np.concatenate([four, halves(np.kron(np.eye(2), np.kron(DERIV.T, np.eye(EG))))]))
    operands = (vel, elem_scale, elem_ids, rows, mats)
    vmem = pl.BlockSpec(memory_space=pltpu.VMEM)
    hbm = pl.BlockSpec(memory_space=pltpu.HBM)
    field = jax.ShapeDtypeStruct((N * N, SYS, ED), F32)
    dma = pltpu.SemaphoreType.DMA
    r0, q0, p0, coef = pl.pallas_call(
        kernel,
        out_shape=(field, field, field, jax.ShapeDtypeStruct((2, SYS, ED), F32)),
        in_specs=[hbm] * 5,
        out_specs=(vmem,) * 4,
        scratch_shapes=[
            pltpu.VMEM((SYS, N * N, ED), F32),
            pltpu.VMEM((2, ED), F32),
            pltpu.VMEM((1, ED), jnp.int32),
            pltpu.VMEM((ROWS, ED), F32),
            pltpu.VMEM((6, ED, ED), BF16),
            pltpu.VMEM((HALVES, AH, NP, 3, ZL, ED), F32),
            pltpu.VMEM((HALVES, AH, 3, Z, ED), F32),
            pltpu.VMEM((HALVES, AH, 3, Z, ED), F32),
            pltpu.VMEM((HALVES, AH, 2, 3, Z, ED), BF16),
            pltpu.VMEM((HALVES, 3, AH, Z, ED), F32),
            pltpu.VMEM((HALVES, 3, NP, AH, ZL, ED), F32),
            pltpu.VMEM((8, ED), F32),
            pltpu.VMEM((HALVES, 8, ED), F32),
            pltpu.VMEM((SYS, ED), F32),
            pltpu.VMEM((12, ED, ED), BF16),
            pltpu.VMEM((4, N, ZL, ED), F32),
            pltpu.VMEM((2, N, ZL, ED), F32),
            pltpu.VMEM((3, 2, AH, ZL, ED), F32),
            pltpu.VMEM((3, 2, AH, ZL, ED), F32),
            pltpu.VMEM((3, 2, AH, ZL, ED), F32),
            pltpu.VMEM((3, 2, AH, ZL, ED), F32),
            pltpu.VMEM((2, ED, ED), F32),
            pltpu.VMEM((NE, 2, ED), F32),
            dma((5,)),
            dma((HALVES, AH, NP - 1)),
            dma((HALVES, AH, NP - 1)),
            dma((HALVES, 3, 2, NP - 1)),
            dma((HALVES, 3, 2, NP - 1)),
            dma((3, 2, 2)),
            dma((3, 2, 2)),
            dma((3, 2)),
            dma((3, 2)),
            dma((NE - 1,)),
            dma((NE - 1,)),
        ],
        compiler_params=pltpu.CompilerParams(
            collective_id=0, has_side_effects=True, vmem_limit_bytes=48 * 1024 * 1024
        ),
        name="exchange_and_apply",
    )(*[pltpu.with_memory_space_constraint(v, pltpu.HBM) for v in operands])

    flat = jax.ShapeDtypeStruct((SYS // 8, 8 * N * N, ED), F32)
    new, left = pl.pallas_call(
        finish_kernel,
        out_shape=(flat, flat),
        in_specs=[vmem] * 4,
        out_specs=(hbm, hbm),
        scratch_shapes=[
            pltpu.VMEM(flat.shape, F32),
            pltpu.VMEM(flat.shape, F32),
            dma((SYS // 8, 2)),
        ],
        compiler_params=pltpu.CompilerParams(vmem_limit_bytes=16 * 1024 * 1024),
        name="finish",
    )(r0, q0, p0, coef)
    shape = (3, ZL, N, N, ED)
    return new.reshape(shape), left.reshape(shape)


def solution(mesh):
    in_specs = (
        P(None, "plane", None, None, "elem"),
        P(None, "elem"),
        P("elem", None),
        P("elem", None, None),
    )
    out_specs = (P(None, "plane", None, None, "elem"), P(None, "plane", None, None, "elem"))
    return jax.shard_map(
        on_device, mesh=mesh, in_specs=in_specs, out_specs=out_specs, check_vma=False
    )
```

```python
import functools
import math

import jax
import jax.numpy as jnp
import ml_dtypes
import numpy as np
from jax import lax
from jax.experimental import pallas as pl
from jax.experimental.pallas import tpu as pltpu
from jax.sharding import PartitionSpec as P

MESH = pl.DeviceIdType.MESH
F32 = jnp.float32
BF16 = jnp.bfloat16

N = 8
ED = 128
Z = 128
NP = 8
ZL = Z // NP
HALVES = 2
GROUPS = NP * HALVES
EG = ED // GROUPS
AH = N // 2
SYS = 3 * ZL
NX = 4
NZ = 8
NE = NX * NZ
EARLY = 5
PEN = 8.0
ROW_SAME, ROW_SWAP, ROW_AB, ROW_B = 0, AH * AH, 2 * AH * AH, 2 * AH * AH + AH
ROWS = 40
LAM = 4.0
STEP = 0.1


def node_tables():
    degree = N - 1
    points = -np.cos(np.pi * np.arange(N) / degree)
    scales = np.ones(N)
    scales[0] = 2.0
    scales[-1] = 2.0
    bary = (-1.0) ** np.arange(N) / scales
    deriv = np.zeros((N, N))
    for i in range(N):
        for j in range(N):
            if i != j:
                deriv[i, j] = bary[j] / bary[i] / (points[i] - points[j])
        deriv[i, i] = -np.sum(deriv[i])
    weights = np.zeros(N)
    for i in range(N):
        running = 0.0
        for k in range(1, degree // 2 + 1):
            factor = 1.0 if 2 * k == degree else 2.0
            running += factor / (4.0 * k * k - 1.0) * np.cos(2.0 * np.pi * i * k / degree)
        weights[i] = (1.0 if i in (0, degree) else 2.0) / degree * (1.0 - running)
    stiff = deriv.T @ (weights[:, None] * deriv)
    return deriv, weights, stiff


def mode_matrix():
    slots = np.arange(Z)
    harmonic = slots // 2
    angles = 2.0 * math.pi / Z * (harmonic[:, None] * slots[None, :] % Z)
    four = np.where((slots % 2 == 0)[:, None], np.cos(angles), np.sin(angles)) * (2.0 / Z)
    four[0] = 1.0 / Z
    four[1] = np.where(slots % 2 == 0, 1.0, -1.0) / Z
    dz = np.zeros((Z, Z))
    wave = STEP * np.arange(Z // 2)
    dz[0::2] = wave[:, None] * four[1::2]
    dz[1::2] = -wave[:, None] * four[0::2]
    return np.concatenate([four, -dz], axis=1)


def halves(table):
    high = table.astype(np.float32).astype(ml_dtypes.bfloat16)
    low = (table - high.astype(np.float64)).astype(np.float32).astype(ml_dtypes.bfloat16)
    return np.stack([high, low])


DERIV, WEIGHTS, STIFF = node_tables()


def split(x):
    high = x.astype(BF16)
    return high, (x - high.astype(F32)).astype(BF16)


def dot(x, y):
    return jnp.dot(x, y, preferred_element_type=F32)


def pick(x, table):
    high, low = split(x)
    return dot(high, table) + dot(low, table)


def turned(x, groups):
    shift = EG * (groups % GROUPS)
    return pltpu.roll(x, shift, x.ndim - 1) if shift else x


def block_transpose(rows, turned_before=False):
    if not turned_before:
        rows = [turned(x, i) for i, x in enumerate(rows)]
    lane = lax.broadcasted_iota(jnp.int32, rows[0].shape, rows[0].ndim - 1) // EG
    d = 1
    while d < GROUPS:
        clear = (lane & d) == 0
        rows = [jnp.where(clear, rows[i], rows[(i + d) % GROUPS]) for i in range(GROUPS)]
        d *= 2
    return [turned(rows[-g % GROUPS], -g) for g in range(GROUPS)]


def stiff_times(v, wanted):
    even = [v[p] + v[N - 1 - p] for p in range(N // 2)]
    odd = [v[p] - v[N - 1 - p] for p in range(N // 2)]
    out = [None] * N
    for a in wanted:
        s = [0.5 * (STIFF[a, p] + STIFF[a, N - 1 - p]) for p in range(N // 2)]
        t = [0.5 * (STIFF[a, p] - STIFF[a, N - 1 - p]) for p in range(N // 2)]
        e = sum(float(s[p]) * even[p] for p in range(1, N // 2)) + float(s[0]) * even[0]
        o = sum(float(t[p]) * odd[p] for p in range(1, N // 2)) + float(t[0]) * odd[0]
        out[a] = e + o
        out[N - 1 - a] = e - o
    return out


def kernel(
    vel,
    scale_in,
    ids_in,
    rows_in,
    mats_in,
    res,
    qv,
    pv,
    coef_out,
    vin,
    scale,
    ids,
    ctab,
    mats,
    xsend,
    xbuf,
    acc,
    bbuf,
    fsend,
    fbuf,
    geo,
    part_geo,
    hel,
    tables,
    face,
    edge,
    rsend,
    rrecv,
    qsend,
    qrecv,
    dots,
    rbuf,
    in_sem,
    s1,
    r1,
    s2,
    r2,
    hs1,
    hr1,
    hs2,
    hr2,
    rs,
    rr,
):
    e = lax.axis_index("elem")
    me = lax.axis_index("plane")
    y, core = me // 2, lax.rem(me, 2)
    z, x = e // NX, lax.rem(e, NX)
    plane_offsets = [(dy, dc) for dy in (2, 1, 3, 0) for dc in (0, 1) if (dy, dc) != (0, 0)]
    plane_peers = [lax.rem(y + dy, 4) * 2 + lax.rem(core + dc, 2) for dy, dc in plane_offsets]
    elem_peers = [
        lax.rem(z + dz, NZ) * NX + lax.rem(x + dx, NX)
        for dz in (4, 3, 5, 2, 6, 1, 7, 0)
        for dx in (2, 1, 3, 0)
        if (dz, dx) != (0, 0)
    ]
    up, down = lax.rem(e + 1, NE), lax.rem(e + NE - 1, NE)

    pairs = ((vel, vin), (scale_in, scale), (ids_in, ids), (rows_in, ctab), (mats_in, mats))
    loads = [pltpu.make_async_copy(src, dst, in_sem.at[i]) for i, (src, dst) in enumerate(pairs)]
    for load in loads:
        load.start()
    barrier = pltpu.get_barrier_semaphore()
    for t in plane_peers:
        pl.semaphore_signal(barrier, inc=1, device_id=(e, t), device_id_type=MESH)
    for t in elem_peers:
        pl.semaphore_signal(barrier, inc=1, device_id=(t, me), device_id_type=MESH)

    def copy1(half, ah, i):
        t = plane_peers[i]
        return pltpu.make_async_remote_copy(
            src_ref=xsend.at[half, ah, t],
            dst_ref=xbuf.at[half, ah, :, pl.ds(pl.multiple_of(me * ZL, ZL), ZL), :],
            send_sem=s1.at[half, ah, i],
            recv_sem=r1.at[half, ah, i],
            device_id=(e, t),
            device_id_type=MESH,
        )

    def copy2(half, c, k, i):
        t = plane_peers[i]
        return pltpu.make_async_remote_copy(
            src_ref=fsend.at[half, c, pl.ds(2 * k, 2), pl.ds(pl.multiple_of(t * ZL, ZL), ZL), :],
            dst_ref=fbuf.at[half, c, me, pl.ds(2 * k, 2)],
            send_sem=s2.at[half, c, k, i],
            recv_sem=r2.at[half, c, k, i],
            device_id=(e, t),
            device_id_type=MESH,
        )

    def pack_first(ah):
        for c in range(3):
            for z8 in range(ZL // 8):
                nodes = pl.ds(pl.multiple_of(ah * 2 * N, 2 * N), 2 * N)
                tile = jnp.swapaxes(vin[pl.ds(c * ZL + z8 * 8, 8), nodes, :], 0, 1)
                for g, row in enumerate(block_transpose([tile[k] for k in range(2 * N)])):
                    xsend[g % HALVES, ah, g // HALVES, c, pl.ds(z8 * 8, 8), :] = row

    def send_first(half, ah):
        for i in range(NP - 1):
            copy1(half, ah, i).start()
        mine = pl.ds(pl.multiple_of(me * ZL, ZL), ZL)
        xbuf[half, ah, :, mine, :] = xsend[half, ah, me]

    loads[0].wait()
    pack_first(0)
    pl.semaphore_wait(barrier, NP - 1 + NE - 1)
    send_first(0, 0)

    def first(ah, carry):
        pack_first(ah)
        send_first(0, ah)
        return carry

    def first_rest(ah, carry):
        send_first(1, ah)
        return carry

    lax.fori_loop(1, AH, first, 0)
    lax.fori_loop(0, AH, first_rest, 0)

    for load in loads[1:]:
        load.wait()

    lid = ids[...] & (ED - 1)
    growth = 1.0 + 2.0 * (ids[...] // 64).astype(F32) / 63.0
    circ = scale[0:1, :] * growth
    radial = scale[1:2, :]
    geo[0:1, :] = circ * radial
    geo[1:2, :] = radial / circ
    geo[2:3, :] = circ / radial
    for half in range(HALVES):
        share = []
        for val in (circ, radial):
            first = ED - EG * (HALVES * me + half)
            val = pltpu.roll(jnp.broadcast_to(val, (8, ED)), lax.rem(first, ED), 1)
            val = jnp.where(lax.broadcasted_iota(jnp.int32, (8, ED), 1) < EG, val, 0.0)
            for d in (1, 2, 4, 8):
                val = val + pltpu.roll(val, EG * d, 1)
            share.append(val[0:1, :])
        g_circ, g_radial = share
        part_geo[half, 0:1, :] = g_circ * g_radial
        part_geo[half, 1:2, :] = g_circ
        part_geo[half, 2:3, :] = g_radial * ctab[ROW_B : ROW_B + 1, :]

    acc[...] = jnp.zeros_like(acc)
    dots[...] = jnp.zeros_like(dots)
    row_i = lax.broadcasted_iota(jnp.int32, (ED, ED), 0)
    lane_i = lax.broadcasted_iota(jnp.int32, (ED, ED), 1)
    lid_l = jnp.broadcast_to(lid, (ED, ED))
    lid_t = jnp.transpose(lid_l.astype(F32)).astype(jnp.int32)

    def ones(where):
        return jnp.where(where, 1.0, 0.0).astype(BF16)

    tables[0] = ones(lid_t == ((lid_l & 64) | ((lid_l + 63) & 63)))
    tables[1] = ones(lid_t == ((lid_l & 64) | ((lid_l + 1) & 63)))
    tables[2] = ones((lid_t == (lid_l ^ 64)) & (lid_l >= 64))
    tables[3] = ones((lid_t == (lid_l ^ 64)) & (lid_l < 64))
    tables[4] = ones(lid_t == lane_i + 64)
    tables[5] = ones((lid_t == lane_i) & (lane_i >= 64))
    tables[6] = ones((lid_t == lane_i) & (lane_i < 64))
    tables[7] = ones(lid_t + 64 == lane_i)
    tables[8] = ones((row_i == lid_l) & (lid_l < 64))
    tables[9] = ones(row_i == lid_l + 64)
    tables[10] = ones(row_i + 64 == lid_l)
    tables[11] = ones((row_i == lid_l) & (lid_l >= 64))
    slot = me * ZL + (lax.broadcasted_iota(jnp.int32, (SYS, ED), 0) & (ZL - 1))
    kappa = jnp.where(slot == 1, Z // 2, slot // 2).astype(F32)
    hel[...] = (LAM + (STEP * kappa) * (STEP * kappa)) * geo[0:1, :]

    f_high = jnp.concatenate([mats[0], mats[1]], axis=1)
    f_low = jnp.concatenate([mats[2], mats[3]], axis=1)

    def between(half, carry):
        def arrive_first(ph, carry):
            for i in range(NP - 1):
                copy1(half, ph, i).wait_recv()
            w_ab = ctab[pl.ds(ROW_AB + ph, 1), :]
            mass = part_geo[half, 0:1, :] * w_ab
            g_y = part_geo[half, 1:2, :] * w_ab
            g_x = part_geo[half, 2:3, :]
            for c in range(3):
                fy_high, fy_low = split(xbuf[half, ph, 1] * xbuf[half, ph, c])
                dy = dot(fy_high, mats[4]) + dot(fy_low, mats[4]) + dot(fy_high, mats[5])
                acc[half, ph, c] += (LAM * mass) * xbuf[half, ph, c] - g_y * dy
                b_high, b_low = split(mass * (xbuf[half, ph, 2] * xbuf[half, ph, c]))
                bbuf[half, ph, 0, c] = b_high
                bbuf[half, ph, 1, c] = b_low
                for k in range(4):
                    rows = pl.ds(k * 32, 32)
                    fx = g_x * (xbuf[half, ph, 0, rows, :] * xbuf[half, ph, c, rows, :])
                    swap = pltpu.roll(fx, ED // 2, 1)
                    for ah in range(AH):
                        same = ctab[pl.ds(ROW_SAME + ph * AH + ah, 1), :]
                        other = ctab[pl.ds(ROW_SWAP + ph * AH + ah, 1), :]
                        acc[half, ah, c, rows, :] += same * fx + other * swap
            return carry

        def send_second(step, carry):
            c, k = step // 2, lax.rem(step, 2)
            for j in (0, 1):
                ah = 2 * k + j
                a_high, a_low = split(acc[half, ah, c])
                high = jnp.concatenate([a_high, bbuf[half, ah, 0, c]], axis=0)
                low = jnp.concatenate([a_low, bbuf[half, ah, 1, c]], axis=0)
                out = dot(f_high, high) + dot(f_high, low) + dot(f_low, high)
                fsend[half, c, ah] = pltpu.roll(out, EG * (HALVES * me + half), 1)
            @pl.when((half == 0) | (step < EARLY))
            def _():
                for i in range(NP - 1):
                    copy2(half, c, k, i).start()

            mine = pl.ds(pl.multiple_of(me * ZL, ZL), ZL)
            fbuf[half, c, me, pl.ds(2 * k, 2)] = fsend[half, c, pl.ds(2 * k, 2), mine, :]
            return carry

        lax.fori_loop(0, AH, arrive_first, 0)
        lax.fori_loop(0, 6, send_second, 0)
        return carry

    lax.fori_loop(0, HALVES, between, 0)

    def sys_rows(c):
        return pl.ds(pl.multiple_of(c * ZL, ZL), ZL)

    def r_halo(c, way, k):
        return pltpu.make_async_remote_copy(
            src_ref=rsend.at[c, way, pl.ds(2 * k, 2)],
            dst_ref=rrecv.at[c, way, pl.ds(2 * k, 2)],
            send_sem=hs1.at[c, way, k],
            recv_sem=hr1.at[c, way, k],
            device_id=((up, down)[way], me),
            device_id_type=MESH,
        )

    def q_halo(c, way):
        return pltpu.make_async_remote_copy(
            src_ref=qsend.at[c, way],
            dst_ref=qrecv.at[c, way],
            send_sem=hs2.at[c, way],
            recv_sem=hr2.at[c, way],
            device_id=((up, down)[way], me),
            device_id_type=MESH,
        )

    def side(v, rows, b, first, count):
        return jnp.concatenate([v[a * N + b, rows, :] for a in range(first, first + count)], axis=0)

    def pack_edges(v, c, pair, count):
        rows = sys_rows(c)
        packed = []
        for b, t in ((N - 1, 4), (0, 6)):
            for k in (0, 1):
                nodes = [v[(2 * (pair + i) + k) * N + b, rows, :] for i in range(count)]
                nodes = jnp.concatenate(nodes, axis=0) if count > 1 else nodes[0]
                packed.append(pick(nodes, tables[t + k]))
        return packed[0] + packed[1], packed[2] + packed[3]

    def send_q_edges(c):
        for way, got in enumerate(pack_edges(qv, c, 0, AH)):
            qsend[c, way] = got.reshape(AH, ZL, ED)
            q_halo(c, way).start()

    def take_edges(recv, c):
        for way in (0, 1):
            there = (e > 0) if way == 0 else (e < NE - 1)
            got = recv[c, way].reshape(AH * ZL, ED)
            for k in (0, 1):
                here = jnp.where(there, pick(got, tables[8 + 2 * way + k]), 0.0)
                here = here.reshape(AH, ZL, ED)
                for pair in range(AH):
                    edge[way, 2 * pair + k] = here[pair]

    def take_faces(v, c):
        sys = sys_rows(c)
        shape = (N, ZL, ED)
        face[2] = pick(side(v, sys, N - 1, 0, N), tables[2]).reshape(shape)
        face[3] = pick(side(v, sys, 0, 0, N), tables[3]).reshape(shape)
        face[0] = pick(v[(N - 1) * N : N * N, sys, :].reshape(N * ZL, ED), tables[0]).reshape(shape)
        face[1] = pick(v[0:N, sys, :].reshape(N * ZL, ED), tables[1]).reshape(shape)

    def apply_local(v, q, c, columns):
        def tile(h, carry):
            rows = pl.ds(pl.multiple_of(c * ZL + h * 8, 8), 8)
            frows = pl.ds(pl.multiple_of(h * 8, 8), 8)
            hm = hel[rows, :]
            kx = jnp.broadcast_to(geo[1:2, :], (8, ED))
            ky = jnp.broadcast_to(geo[2:3, :], (8, ED))
            nodes = [b for pair in columns for b in (pair, N - 1 - pair)]
            for b in nodes:
                col = stiff_times([v[a * N + b, rows, :] for a in range(N)], range(N // 2))
                scale_b = kx * float(WEIGHTS[b])
                for a in range(N):
                    q[a * N + b, rows, :] = scale_b * col[a]
            for a in range(N):
                vals = [v[a * N + b, rows, :] for b in range(N)]
                line = stiff_times(vals, columns)
                scale_a = ky * float(WEIGHTS[a])
                hm_a = hm * float(WEIGHTS[a])
                for b in nodes:
                    out = q[a * N + b, rows, :] + scale_a * line[b]
                    out = out + (hm_a * float(WEIGHTS[b])) * vals[b]
                    if a == 0:
                        out = out + float(PEN * WEIGHTS[b]) * (vals[b] - face[0, b, frows, :])
                    if a == N - 1:
                        out = out + float(PEN * WEIGHTS[b]) * (vals[b] - face[1, b, frows, :])
                    if b == 0:
                        out = out + float(PEN * WEIGHTS[a]) * (vals[b] - face[2, a, frows, :])
                    if b == N - 1:
                        out = out + float(PEN * WEIGHTS[a]) * (vals[b] - face[3, a, frows, :])
                    q[a * N + b, rows, :] = out
            return carry

        lax.fori_loop(0, ZL // 8, tile, 0)

    def add_edges(q, c):
        rows = sys_rows(c)
        for a in range(N):
            q[a * N, rows, :] -= float(PEN * WEIGHTS[a]) * edge[0, a]
            q[a * N + N - 1, rows, :] -= float(PEN * WEIGHTS[a]) * edge[1, a]

    def arrive_second(c, ah):
        groups = [fbuf[g % HALVES, c, g // HALVES, ah] for g in range(GROUPS)]
        for k, line in enumerate(block_transpose(groups, True)):
            res[ah * 2 * N + k, sys_rows(c), :] = line

    def dot_rows(first, k, count):
        return pl.ds(pl.multiple_of(first + (k % 2) * (ED // 2), 8), count)

    def begin(c):
        def arrive(ah, carry):
            arrive_second(c, ah)
            return carry

        for k in (0, 1):
            for half in range(HALVES):
                for i in range(NP - 1):
                    copy2(half, c, k, i).wait_recv()
            lax.fori_loop(2 * k, 2 * k + 2, arrive, 0)
            for way, got in enumerate(pack_edges(res, c, 2 * k, 2)):
                rsend[c, way, pl.ds(2 * k, 2)] = got.reshape(2, ZL, ED)
            if k == 1:
                take_faces(res, c)
            for way in (0, 1):
                r_halo(c, way, k).start()
        apply_local(res, qv, c, (0,))
        send_q_edges(c)
        apply_local(res, qv, c, (1, 2, 3))

    def end(c):
        for way in (0, 1):
            for k in (0, 1):
                r_halo(c, way, k).wait_recv()
        take_edges(rrecv, c)
        add_edges(qv, c)
        take_faces(qv, c)
        apply_local(qv, pv, c, range(N // 2))

        def dot_tile(h, carry):
            rows = pl.ds(pl.multiple_of(c * ZL + h * 8, 8), 8)
            sums = [jnp.zeros((8, ED), F32) for _ in range(4)]
            for n in range(N * N):
                r_n, q_n, p_n = res[n, rows, :], qv[n, rows, :], pv[n, rows, :]
                for k, prod in enumerate((r_n * r_n, r_n * q_n, q_n * q_n, q_n * p_n)):
                    sums[k] = sums[k] + prod
            for k in range(4):
                dots[k // 2, dot_rows(c * ZL + h * 8, k, 8), :] = sums[k]
            return carry

        lax.fori_loop(0, ZL // 8, dot_tile, 0)
        for way in (0, 1):
            q_halo(c, way).wait_recv()
        take_edges(qrecv, c)
        rows = sys_rows(c)
        inner = jnp.broadcast_to(lid < 64, (ZL, ED)) & (e > 0)
        outer = jnp.broadcast_to(lid >= 64, (ZL, ED)) & (e < NE - 1)
        last = jnp.zeros((ZL, ED), F32)
        for a in range(N):
            w_a = float(PEN * WEIGHTS[a])
            for way, b, where in ((0, 0, inner), (1, N - 1, outer)):
                n = a * N + b
                got = w_a * (edge[way, a] - jnp.where(where, w_a * res[n, rows, :], 0.0))
                pv[n, rows, :] -= got
                last = last + qv[n, rows, :] * got
        dots[1, dot_rows(c * ZL, 3, ZL), :] -= last

    def begin_all(c, carry):
        begin(c)

        @pl.when(c == 0)
        def _():
            for step in range(EARLY, 6):
                for i in range(NP - 1):
                    copy2(1, step // 2, step % 2, i).start()

        return carry

    def end_all(c, carry):
        end(c)
        return carry

    lax.fori_loop(0, 3, begin_all, 0)
    lax.fori_loop(0, 3, end_all, 0)

    one_rows = jnp.ones((8, ED), F32)
    for k in (0, 1):
        summed = lax.dot_general(
            one_rows,
            dots[k],
            (((1,), (1,)), ((), ())),
            precision=lax.Precision.HIGHEST,
            preferred_element_type=F32,
        )
        rbuf[0, k : k + 1, :] = summed[0:1, :]

    def spread(i):
        return pltpu.make_async_remote_copy(
            src_ref=rbuf.at[0],
            dst_ref=rbuf.at[i + 1],
            send_sem=rs.at[i],
            recv_sem=rr.at[i],
            device_id=(elem_peers[i], me),
            device_id_type=MESH,
        )

    for i in range(NE - 1):
        spread(i).start()
    for i in range(NE - 1):
        spread(i).wait_recv()
    part = jnp.sum(rbuf[...], axis=0)

    swapped = pltpu.roll(jnp.concatenate([part] * 4, axis=0), ED // 2, 1)
    aa, bb, cc, ee = part[0:1, :], swapped[0:1, :], part[1:2, :], swapped[1:2, :]
    alpha = aa / bb
    rr1 = alpha * alpha * cc - aa
    beta1 = 1.0 + rr1 / aa
    alpha1 = rr1 / (beta1 * beta1 * bb - 2.0 * beta1 * alpha * cc + alpha * alpha * ee)
    coef_s = alpha + alpha1 * beta1
    coef_t = alpha1 * alpha
    row8 = lax.broadcasted_iota(jnp.int32, (8, ED), 0)
    both = jnp.where(row8 == 0, coef_s, coef_t)
    both = jnp.where(lax.broadcasted_iota(jnp.int32, (8, ED), 1) < SYS, both, 0.0)
    both = jnp.transpose(jnp.concatenate([both] + [jnp.zeros((8, ED), F32)] * 15, axis=0))
    coef_out[0] = jnp.broadcast_to(both[0:SYS, 0:1], (SYS, ED))
    coef_out[1] = jnp.broadcast_to(both[0:SYS, 1:2], (SYS, ED))

    def drain(ah, carry):
        for half in range(HALVES):
            for i in range(NP - 1):
                copy1(half, ah, i).wait_send()
        return carry

    def drain2(step, carry):
        for half in range(HALVES):
            for i in range(NP - 1):
                copy2(half, step // 2, lax.rem(step, 2), i).wait_send()
        return carry

    def drain3(c, carry):
        for way in (0, 1):
            for k in (0, 1):
                r_halo(c, way, k).wait_send()
            q_halo(c, way).wait_send()
        return carry

    lax.fori_loop(0, AH, drain, 0)
    lax.fori_loop(0, 6, drain2, 0)
    lax.fori_loop(0, 3, drain3, 0)
    for i in range(NE - 1):
        spread(i).wait_send()


def finish_kernel(r, q, p, coef, x_out, r_out, xs, rs, sem):
    def tile(st, carry):
        rows = pl.ds(pl.multiple_of(st * 8, 8), 8)
        s, t = coef[0, rows, :], coef[1, rows, :]
        for a in range(N):
            new, left = [], []
            for n in range(a * N, a * N + N):
                r_n, q_n, p_n = r[n, rows, :], q[n, rows, :], p[n, rows, :]
                new.append(s * r_n - t * q_n)
                left.append(r_n - s * q_n + t * p_n)
            for buf, vals in ((xs, new), (rs, left)):
                vals = jnp.swapaxes(jnp.stack(vals), 0, 1)
                for k in range(8):
                    buf[st, pl.ds(k * N * N + a * N, N), :] = vals[k]
        for copy in out_copies(st):
            copy.start()
        return carry

    def out_copies(st):
        return (
            pltpu.make_async_copy(xs.at[st], x_out.at[st], sem.at[st, 0]),
            pltpu.make_async_copy(rs.at[st], r_out.at[st], sem.at[st, 1]),
        )

    def drain(st, carry):
        for copy in out_copies(st):
            copy.wait()
        return carry

    lax.fori_loop(0, SYS // 8, tile, 0)
    lax.fori_loop(0, SYS // 8, drain, 0)


def on_device(velocity, elem_scale, elem_ids, edge_blocks):
    vel = velocity.reshape(SYS, N * N, ED)
    rows = np.zeros((ROWS, ED))
    table = -WEIGHTS[:, None] * DERIV
    for ph in range(AH):
        for ah in range(AH):
            for i in (0, 1):
                lanes = slice(i * ED // 2, (i + 1) * ED // 2)
                rows[ROW_SAME + ph * AH + ah, lanes] = table[2 * ah + i, 2 * ph + i]
                rows[ROW_SWAP + ph * AH + ah, lanes] = table[2 * ah + i, 2 * ph + 1 - i]
    for ah in range(AH):
        rows[ROW_AB + ah] = np.repeat(np.outer(WEIGHTS[2 * ah : 2 * ah + 2], WEIGHTS).ravel(), EG)
    rows[ROW_B] = np.repeat(np.tile(WEIGHTS, 2), EG)
    rows = jnp.asarray(rows, F32)
    four = halves(mode_matrix()).reshape(2, Z, 2, Z).transpose(0, 2, 1, 3).reshape(4, Z, Z)
    mats = jnp.asarray(np.concatenate([four, halves(np.kron(np.eye(2), np.kron(DERIV.T, np.eye(EG))))]))
    operands = (vel, elem_scale, elem_ids, rows, mats)
    vmem = pl.BlockSpec(memory_space=pltpu.VMEM)
    hbm = pl.BlockSpec(memory_space=pltpu.HBM)
    field = jax.ShapeDtypeStruct((N * N, SYS, ED), F32)
    dma = pltpu.SemaphoreType.DMA
    r0, q0, p0, coef = pl.pallas_call(
        kernel,
        out_shape=(field, field, field, jax.ShapeDtypeStruct((2, SYS, ED), F32)),
        in_specs=[hbm] * 5,
        out_specs=(vmem,) * 4,
        scratch_shapes=[
            pltpu.VMEM((SYS, N * N, ED), F32),
            pltpu.VMEM((2, ED), F32),
            pltpu.VMEM((1, ED), jnp.int32),
            pltpu.VMEM((ROWS, ED), F32),
            pltpu.VMEM((6, ED, ED), BF16),
            pltpu.VMEM((HALVES, AH, NP, 3, ZL, ED), F32),
            pltpu.VMEM((HALVES, AH, 3, Z, ED), F32),
            pltpu.VMEM((HALVES, AH, 3, Z, ED), F32),
            pltpu.VMEM((HALVES, AH, 2, 3, Z, ED), BF16),
            pltpu.VMEM((HALVES, 3, AH, Z, ED), F32),
            pltpu.VMEM((HALVES, 3, NP, AH, ZL, ED), F32),
            pltpu.VMEM((8, ED), F32),
            pltpu.VMEM((HALVES, 8, ED), F32),
            pltpu.VMEM((SYS, ED), F32),
            pltpu.VMEM((12, ED, ED), BF16),
            pltpu.VMEM((4, N, ZL, ED), F32),
            pltpu.VMEM((2, N, ZL, ED), F32),
            pltpu.VMEM((3, 2, AH, ZL, ED), F32),
            pltpu.VMEM((3, 2, AH, ZL, ED), F32),
            pltpu.VMEM((3, 2, AH, ZL, ED), F32),
            pltpu.VMEM((3, 2, AH, ZL, ED), F32),
            pltpu.VMEM((2, ED, ED), F32),
            pltpu.VMEM((NE, 2, ED), F32),
            dma((5,)),
            dma((HALVES, AH, NP - 1)),
            dma((HALVES, AH, NP - 1)),
            dma((HALVES, 3, 2, NP - 1)),
            dma((HALVES, 3, 2, NP - 1)),
            dma((3, 2, 2)),
            dma((3, 2, 2)),
            dma((3, 2)),
            dma((3, 2)),
            dma((NE - 1,)),
            dma((NE - 1,)),
        ],
        compiler_params=pltpu.CompilerParams(
            collective_id=0, has_side_effects=True, vmem_limit_bytes=48 * 1024 * 1024
        ),
        name="exchange_and_apply",
    )(*[pltpu.with_memory_space_constraint(v, pltpu.HBM) for v in operands])

    flat = jax.ShapeDtypeStruct((SYS // 8, 8 * N * N, ED), F32)
    new, left = pl.pallas_call(
        finish_kernel,
        out_shape=(flat, flat),
        in_specs=[vmem] * 4,
        out_specs=(hbm, hbm),
        scratch_shapes=[
            pltpu.VMEM(flat.shape, F32),
            pltpu.VMEM(flat.shape, F32),
            dma((SYS // 8, 2)),
        ],
        compiler_params=pltpu.CompilerParams(vmem_limit_bytes=16 * 1024 * 1024),
        name="finish",
    )(r0, q0, p0, coef)
    shape = (3, ZL, N, N, ED)
    return new.reshape(shape), left.reshape(shape)


def solution(mesh):
    in_specs = (
        P(None, "plane", None, None, "elem"),
        P(None, "elem"),
        P("elem", None),
        P("elem", None, None),
    )
    out_specs = (P(None, "plane", None, None, "elem"), P(None, "plane", None, None, "elem"))
    return jax.shard_map(
        on_device, mesh=mesh, in_specs=in_specs, out_specs=out_specs, check_vma=False
    )
```

```python
import functools
import math

import jax
import jax.numpy as jnp
import ml_dtypes
import numpy as np
from jax import lax
from jax.experimental import pallas as pl
from jax.experimental.pallas import tpu as pltpu
from jax.sharding import PartitionSpec as P

MESH = pl.DeviceIdType.MESH
F32 = jnp.float32
BF16 = jnp.bfloat16

N = 8
ED = 128
Z = 128
NP = 8
ZL = Z // NP
HALVES = 2
GROUPS = NP * HALVES
EG = ED // GROUPS
AH = N // 2
SYS = 3 * ZL
NX = 4
NZ = 8
NE = NX * NZ
EARLY = 5
PEN = 8.0
ROW_SAME, ROW_SWAP, ROW_AB, ROW_B = 0, AH * AH, 2 * AH * AH, 2 * AH * AH + AH
ROWS = 40
LAM = 4.0
STEP = 0.1


def node_tables():
    degree = N - 1
    points = -np.cos(np.pi * np.arange(N) / degree)
    scales = np.ones(N)
    scales[0] = 2.0
    scales[-1] = 2.0
    bary = (-1.0) ** np.arange(N) / scales
    deriv = np.zeros((N, N))
    for i in range(N):
        for j in range(N):
            if i != j:
                deriv[i, j] = bary[j] / bary[i] / (points[i] - points[j])
        deriv[i, i] = -np.sum(deriv[i])
    weights = np.zeros(N)
    for i in range(N):
        running = 0.0
        for k in range(1, degree // 2 + 1):
            factor = 1.0 if 2 * k == degree else 2.0
            running += factor / (4.0 * k * k - 1.0) * np.cos(2.0 * np.pi * i * k / degree)
        weights[i] = (1.0 if i in (0, degree) else 2.0) / degree * (1.0 - running)
    stiff = deriv.T @ (weights[:, None] * deriv)
    return deriv, weights, stiff


def mode_matrix():
    slots = np.arange(Z)
    harmonic = slots // 2
    angles = 2.0 * math.pi / Z * (harmonic[:, None] * slots[None, :] % Z)
    four = np.where((slots % 2 == 0)[:, None], np.cos(angles), np.sin(angles)) * (2.0 / Z)
    four[0] = 1.0 / Z
    four[1] = np.where(slots % 2 == 0, 1.0, -1.0) / Z
    dz = np.zeros((Z, Z))
    wave = STEP * np.arange(Z // 2)
    dz[0::2] = wave[:, None] * four[1::2]
    dz[1::2] = -wave[:, None] * four[0::2]
    return np.concatenate([four, -dz], axis=1)


def halves(table):
    high = table.astype(np.float32).astype(ml_dtypes.bfloat16)
    low = (table - high.astype(np.float64)).astype(np.float32).astype(ml_dtypes.bfloat16)
    return np.stack([high, low])


DERIV, WEIGHTS, STIFF = node_tables()


def split(x):
    high = x.astype(BF16)
    return high, (x - high.astype(F32)).astype(BF16)


def dot(x, y):
    return jnp.dot(x, y, preferred_element_type=F32)


def pick(x, table):
    high, low = split(x)
    return dot(high, table) + dot(low, table)


def turned(x, groups):
    shift = EG * (groups % GROUPS)
    return pltpu.roll(x, shift, x.ndim - 1) if shift else x


def block_transpose(rows, turned_before=False):
    if not turned_before:
        rows = [turned(x, i) for i, x in enumerate(rows)]
    lane = lax.broadcasted_iota(jnp.int32, rows[0].shape, rows[0].ndim - 1) // EG
    d = 1
    while d < GROUPS:
        clear = (lane & d) == 0
        rows = [jnp.where(clear, rows[i], rows[(i + d) % GROUPS]) for i in range(GROUPS)]
        d *= 2
    return [turned(rows[-g % GROUPS], -g) for g in range(GROUPS)]


def stiff_times(v, wanted):
    even = [v[p] + v[N - 1 - p] for p in range(N // 2)]
    odd = [v[p] - v[N - 1 - p] for p in range(N // 2)]
    out = [None] * N
    for a in wanted:
        s = [0.5 * (STIFF[a, p] + STIFF[a, N - 1 - p]) for p in range(N // 2)]
        t = [0.5 * (STIFF[a, p] - STIFF[a, N - 1 - p]) for p in range(N // 2)]
        e = sum(float(s[p]) * even[p] for p in range(1, N // 2)) + float(s[0]) * even[0]
        o = sum(float(t[p]) * odd[p] for p in range(1, N // 2)) + float(t[0]) * odd[0]
        out[a] = e + o
        out[N - 1 - a] = e - o
    return out


def kernel(
    vel,
    scale_in,
    ids_in,
    rows_in,
    mats_in,
    res,
    qv,
    pv,
    coef_out,
    vin,
    scale,
    ids,
    ctab,
    mats,
    xsend,
    xbuf,
    acc,
    bbuf,
    fsend,
    fbuf,
    geo,
    part_geo,
    hel,
    tables,
    face,
    edge,
    rsend,
    rrecv,
    qsend,
    qrecv,
    dots,
    rbuf,
    in_sem,
    s1,
    r1,
    s2,
    r2,
    hs1,
    hr1,
    hs2,
    hr2,
    rs,
    rr,
):
    e = lax.axis_index("elem")
    me = lax.axis_index("plane")
    y, core = me // 2, lax.rem(me, 2)
    z, x = e // NX, lax.rem(e, NX)
    plane_offsets = [(dy, dc) for dy in (2, 1, 3, 0) for dc in (0, 1) if (dy, dc) != (0, 0)]
    plane_peers = [lax.rem(y + dy, 4) * 2 + lax.rem(core + dc, 2) for dy, dc in plane_offsets]
    elem_peers = [
        lax.rem(z + dz, NZ) * NX + lax.rem(x + dx, NX)
        for dz in (4, 3, 5, 2, 6, 1, 7, 0)
        for dx in (2, 1, 3, 0)
        if (dz, dx) != (0, 0)
    ]
    up, down = lax.rem(e + 1, NE), lax.rem(e + NE - 1, NE)

    def load_nodes(ah):
        nodes = pl.ds(pl.multiple_of(ah * 2 * N, 2 * N), 2 * N)
        return pltpu.make_async_copy(vel.at[:, nodes, :], vin.at[:, nodes, :], in_sem.at[ah])

    for ah in range(AH):
        load_nodes(ah).start()
    pairs = ((scale_in, scale), (ids_in, ids), (rows_in, ctab), (mats_in, mats))
    loads = [
        pltpu.make_async_copy(src, dst, in_sem.at[AH + i]) for i, (src, dst) in enumerate(pairs)
    ]
    for load in loads:
        load.start()
    barrier = pltpu.get_barrier_semaphore()
    for t in plane_peers:
        pl.semaphore_signal(barrier, inc=1, device_id=(e, t), device_id_type=MESH)
    for t in elem_peers:
        pl.semaphore_signal(barrier, inc=1, device_id=(t, me), device_id_type=MESH)

    def copy1(half, ah, i):
        t = plane_peers[i]
        return pltpu.make_async_remote_copy(
            src_ref=xsend.at[half, ah, t],
            dst_ref=xbuf.at[half, ah, :, pl.ds(pl.multiple_of(me * ZL, ZL), ZL), :],
            send_sem=s1.at[half, ah, i],
            recv_sem=r1.at[half, ah, i],
            device_id=(e, t),
            device_id_type=MESH,
        )

    def copy2(half, c, k, i):
        t = plane_peers[i]
        return pltpu.make_async_remote_copy(
            src_ref=fsend.at[half, c, pl.ds(2 * k, 2), pl.ds(pl.multiple_of(t * ZL, ZL), ZL), :],
            dst_ref=fbuf.at[half, c, me, pl.ds(2 * k, 2)],
            send_sem=s2.at[half, c, k, i],
            recv_sem=r2.at[half, c, k, i],
            device_id=(e, t),
            device_id_type=MESH,
        )

    def pack_first(ah):
        load_nodes(ah).wait()
        for c in range(3):
            for z8 in range(ZL // 8):
                nodes = pl.ds(pl.multiple_of(ah * 2 * N, 2 * N), 2 * N)
                tile = jnp.swapaxes(vin[pl.ds(c * ZL + z8 * 8, 8), nodes, :], 0, 1)
                for g, row in enumerate(block_transpose([tile[k] for k in range(2 * N)])):
                    xsend[g % HALVES, ah, g // HALVES, c, pl.ds(z8 * 8, 8), :] = row

    def send_first(half, ah):
        for i in range(NP - 1):
            copy1(half, ah, i).start()
        mine = pl.ds(pl.multiple_of(me * ZL, ZL), ZL)
        xbuf[half, ah, :, mine, :] = xsend[half, ah, me]

    pack_first(0)
    pl.semaphore_wait(barrier, NP - 1 + NE - 1)
    send_first(0, 0)

    def first(ah, carry):
        pack_first(ah)
        send_first(0, ah)
        return carry

    def first_rest(ah, carry):
        send_first(1, ah)
        return carry

    lax.fori_loop(1, AH, first, 0)
    lax.fori_loop(0, AH, first_rest, 0)

    for load in loads:
        load.wait()

    lid = ids[...] & (ED - 1)
    growth = 1.0 + 2.0 * (ids[...] // 64).astype(F32) / 63.0
    circ = scale[0:1, :] * growth
    radial = scale[1:2, :]
    geo[0:1, :] = circ * radial
    geo[1:2, :] = radial / circ
    geo[2:3, :] = circ / radial
    for half in range(HALVES):
        share = []
        for val in (circ, radial):
            first = ED - EG * (HALVES * me + half)
            val = pltpu.roll(jnp.broadcast_to(val, (8, ED)), lax.rem(first, ED), 1)
            val = jnp.where(lax.broadcasted_iota(jnp.int32, (8, ED), 1) < EG, val, 0.0)
            for d in (1, 2, 4, 8):
                val = val + pltpu.roll(val, EG * d, 1)
            share.append(val[0:1, :])
        g_circ, g_radial = share
        part_geo[half, 0:1, :] = g_circ * g_radial
        part_geo[half, 1:2, :] = g_circ
        part_geo[half, 2:3, :] = g_radial * ctab[ROW_B : ROW_B + 1, :]

    acc[...] = jnp.zeros_like(acc)
    dots[...] = jnp.zeros_like(dots)
    row_i = lax.broadcasted_iota(jnp.int32, (ED, ED), 0)
    lane_i = lax.broadcasted_iota(jnp.int32, (ED, ED), 1)
    lid_l = jnp.broadcast_to(lid, (ED, ED))
    lid_t = jnp.transpose(lid_l.astype(F32)).astype(jnp.int32)

    def ones(where):
        return jnp.where(where, 1.0, 0.0).astype(BF16)

    tables[0] = ones(lid_t == ((lid_l & 64) | ((lid_l + 63) & 63)))
    tables[1] = ones(lid_t == ((lid_l & 64) | ((lid_l + 1) & 63)))
    tables[2] = ones((lid_t == (lid_l ^ 64)) & (lid_l >= 64))
    tables[3] = ones((lid_t == (lid_l ^ 64)) & (lid_l < 64))
    tables[4] = ones(lid_t == lane_i + 64)
    tables[5] = ones((lid_t == lane_i) & (lane_i >= 64))
    tables[6] = ones((lid_t == lane_i) & (lane_i < 64))
    tables[7] = ones(lid_t + 64 == lane_i)
    tables[8] = ones((row_i == lid_l) & (lid_l < 64))
    tables[9] = ones(row_i == lid_l + 64)
    tables[10] = ones(row_i + 64 == lid_l)
    tables[11] = ones((row_i == lid_l) & (lid_l >= 64))
    slot = me * ZL + (lax.broadcasted_iota(jnp.int32, (SYS, ED), 0) & (ZL - 1))
    kappa = jnp.where(slot == 1, Z // 2, slot // 2).astype(F32)
    hel[...] = (LAM + (STEP * kappa) * (STEP * kappa)) * geo[0:1, :]

    f_high = jnp.concatenate([mats[0], mats[1]], axis=1)
    f_low = jnp.concatenate([mats[2], mats[3]], axis=1)

    def between(half, carry):
        def arrive_first(ph, carry):
            for i in range(NP - 1):
                copy1(half, ph, i).wait_recv()
            w_ab = ctab[pl.ds(ROW_AB + ph, 1), :]
            mass = part_geo[half, 0:1, :] * w_ab
            g_y = part_geo[half, 1:2, :] * w_ab
            g_x = part_geo[half, 2:3, :]
            for c in range(3):
                fy_high, fy_low = split(xbuf[half, ph, 1] * xbuf[half, ph, c])
                dy = dot(fy_high, mats[4]) + dot(fy_low, mats[4]) + dot(fy_high, mats[5])
                acc[half, ph, c] += (LAM * mass) * xbuf[half, ph, c] - g_y * dy
                b_high, b_low = split(mass * (xbuf[half, ph, 2] * xbuf[half, ph, c]))
                bbuf[half, ph, 0, c] = b_high
                bbuf[half, ph, 1, c] = b_low
                for k in range(4):
                    rows = pl.ds(k * 32, 32)
                    fx = g_x * (xbuf[half, ph, 0, rows, :] * xbuf[half, ph, c, rows, :])
                    swap = pltpu.roll(fx, ED // 2, 1)
                    for ah in range(AH):
                        same = ctab[pl.ds(ROW_SAME + ph * AH + ah, 1), :]
                        other = ctab[pl.ds(ROW_SWAP + ph * AH + ah, 1), :]
                        acc[half, ah, c, rows, :] += same * fx + other * swap
            return carry

        def send_second(step, carry):
            c, k = step // 2, lax.rem(step, 2)
            for j in (0, 1):
                ah = 2 * k + j
                a_high, a_low = split(acc[half, ah, c])
                high = jnp.concatenate([a_high, bbuf[half, ah, 0, c]], axis=0)
                low = jnp.concatenate([a_low, bbuf[half, ah, 1, c]], axis=0)
                out = dot(f_high, high) + dot(f_high, low) + dot(f_low, high)
                fsend[half, c, ah] = pltpu.roll(out, EG * (HALVES * me + half), 1)
            @pl.when((half == 0) | (step < EARLY))
            def _():
                for i in range(NP - 1):
                    copy2(half, c, k, i).start()

            mine = pl.ds(pl.multiple_of(me * ZL, ZL), ZL)
            fbuf[half, c, me, pl.ds(2 * k, 2)] = fsend[half, c, pl.ds(2 * k, 2), mine, :]
            return carry

        lax.fori_loop(0, AH, arrive_first, 0)
        lax.fori_loop(0, 6, send_second, 0)
        return carry

    lax.fori_loop(0, HALVES, between, 0)

    def sys_rows(c):
        return pl.ds(pl.multiple_of(c * ZL, ZL), ZL)

    def r_halo(c, way, k):
        return pltpu.make_async_remote_copy(
            src_ref=rsend.at[c, way, pl.ds(2 * k, 2)],
            dst_ref=rrecv.at[c, way, pl.ds(2 * k, 2)],
            send_sem=hs1.at[c, way, k],
            recv_sem=hr1.at[c, way, k],
            device_id=((up, down)[way], me),
            device_id_type=MESH,
        )

    def q_halo(c, way):
        return pltpu.make_async_remote_copy(
            src_ref=qsend.at[c, way],
            dst_ref=qrecv.at[c, way],
            send_sem=hs2.at[c, way],
            recv_sem=hr2.at[c, way],
            device_id=((up, down)[way], me),
            device_id_type=MESH,
        )

    def side(v, rows, b, first, count):
        return jnp.concatenate([v[a * N + b, rows, :] for a in range(first, first + count)], axis=0)

    def pack_edges(v, c, pair, count):
        rows = sys_rows(c)
        packed = []
        for b, t in ((N - 1, 4), (0, 6)):
            for k in (0, 1):
                nodes = [v[(2 * (pair + i) + k) * N + b, rows, :] for i in range(count)]
                nodes = jnp.concatenate(nodes, axis=0) if count > 1 else nodes[0]
                packed.append(pick(nodes, tables[t + k]))
        return packed[0] + packed[1], packed[2] + packed[3]

    def send_q_edges(c):
        for way, got in enumerate(pack_edges(qv, c, 0, AH)):
            qsend[c, way] = got.reshape(AH, ZL, ED)
            q_halo(c, way).start()

    def take_edges(recv, c):
        for way in (0, 1):
            there = (e > 0) if way == 0 else (e < NE - 1)
            got = recv[c, way].reshape(AH * ZL, ED)
            for k in (0, 1):
                here = jnp.where(there, pick(got, tables[8 + 2 * way + k]), 0.0)
                here = here.reshape(AH, ZL, ED)
                for pair in range(AH):
                    edge[way, 2 * pair + k] = here[pair]

    def take_faces(v, c):
        sys = sys_rows(c)
        shape = (N, ZL, ED)
        face[2] = pick(side(v, sys, N - 1, 0, N), tables[2]).reshape(shape)
        face[3] = pick(side(v, sys, 0, 0, N), tables[3]).reshape(shape)
        face[0] = pick(v[(N - 1) * N : N * N, sys, :].reshape(N * ZL, ED), tables[0]).reshape(shape)
        face[1] = pick(v[0:N, sys, :].reshape(N * ZL, ED), tables[1]).reshape(shape)

    def apply_local(v, q, c, columns):
        def tile(h, carry):
            rows = pl.ds(pl.multiple_of(c * ZL + h * 8, 8), 8)
            frows = pl.ds(pl.multiple_of(h * 8, 8), 8)
            hm = hel[rows, :]
            kx = jnp.broadcast_to(geo[1:2, :], (8, ED))
            ky = jnp.broadcast_to(geo[2:3, :], (8, ED))
            nodes = [b for pair in columns for b in (pair, N - 1 - pair)]
            for b in nodes:
                col = stiff_times([v[a * N + b, rows, :] for a in range(N)], range(N // 2))
                scale_b = kx * float(WEIGHTS[b])
                for a in range(N):
                    q[a * N + b, rows, :] = scale_b * col[a]
            for a in range(N):
                vals = [v[a * N + b, rows, :] for b in range(N)]
                line = stiff_times(vals, columns)
                scale_a = ky * float(WEIGHTS[a])
                hm_a = hm * float(WEIGHTS[a])
                for b in nodes:
                    out = q[a * N + b, rows, :] + scale_a * line[b]
                    out = out + (hm_a * float(WEIGHTS[b])) * vals[b]
                    if a == 0:
                        out = out + float(PEN * WEIGHTS[b]) * (vals[b] - face[0, b, frows, :])
                    if a == N - 1:
                        out = out + float(PEN * WEIGHTS[b]) * (vals[b] - face[1, b, frows, :])
                    if b == 0:
                        out = out + float(PEN * WEIGHTS[a]) * (vals[b] - face[2, a, frows, :])
                    if b == N - 1:
                        out = out + float(PEN * WEIGHTS[a]) * (vals[b] - face[3, a, frows, :])
                    q[a * N + b, rows, :] = out
            return carry

        lax.fori_loop(0, ZL // 8, tile, 0)

    def add_edges(q, c):
        rows = sys_rows(c)
        for a in range(N):
            q[a * N, rows, :] -= float(PEN * WEIGHTS[a]) * edge[0, a]
            q[a * N + N - 1, rows, :] -= float(PEN * WEIGHTS[a]) * edge[1, a]

    def arrive_second(c, ah):
        groups = [fbuf[g % HALVES, c, g // HALVES, ah] for g in range(GROUPS)]
        for k, line in enumerate(block_transpose(groups, True)):
            res[ah * 2 * N + k, sys_rows(c), :] = line

    def dot_rows(first, k, count):
        return pl.ds(pl.multiple_of(first + (k % 2) * (ED // 2), 8), count)

    def begin(c):
        def arrive(ah, carry):
            arrive_second(c, ah)
            return carry

        for k in (0, 1):
            for half in range(HALVES):
                for i in range(NP - 1):
                    copy2(half, c, k, i).wait_recv()
            lax.fori_loop(2 * k, 2 * k + 2, arrive, 0)
            for way, got in enumerate(pack_edges(res, c, 2 * k, 2)):
                rsend[c, way, pl.ds(2 * k, 2)] = got.reshape(2, ZL, ED)
            if k == 1:
                take_faces(res, c)
            for way in (0, 1):
                r_halo(c, way, k).start()
        apply_local(res, qv, c, (0,))
        send_q_edges(c)
        apply_local(res, qv, c, (1, 2, 3))

    def end(c):
        for way in (0, 1):
            for k in (0, 1):
                r_halo(c, way, k).wait_recv()
        take_edges(rrecv, c)
        add_edges(qv, c)
        take_faces(qv, c)
        apply_local(qv, pv, c, range(N // 2))

        def dot_tile(h, carry):
            rows = pl.ds(pl.multiple_of(c * ZL + h * 8, 8), 8)
            sums = [jnp.zeros((8, ED), F32) for _ in range(4)]
            for n in range(N * N):
                r_n, q_n, p_n = res[n, rows, :], qv[n, rows, :], pv[n, rows, :]
                for k, prod in enumerate((r_n * r_n, r_n * q_n, q_n * q_n, q_n * p_n)):
                    sums[k] = sums[k] + prod
            for k in range(4):
                dots[k // 2, dot_rows(c * ZL + h * 8, k, 8), :] = sums[k]
            return carry

        lax.fori_loop(0, ZL // 8, dot_tile, 0)
        for way in (0, 1):
            q_halo(c, way).wait_recv()
        take_edges(qrecv, c)
        rows = sys_rows(c)
        inner = jnp.broadcast_to(lid < 64, (ZL, ED)) & (e > 0)
        outer = jnp.broadcast_to(lid >= 64, (ZL, ED)) & (e < NE - 1)
        last = jnp.zeros((ZL, ED), F32)
        for a in range(N):
            w_a = float(PEN * WEIGHTS[a])
            for way, b, where in ((0, 0, inner), (1, N - 1, outer)):
                n = a * N + b
                got = w_a * (edge[way, a] - jnp.where(where, w_a * res[n, rows, :], 0.0))
                pv[n, rows, :] -= got
                last = last + qv[n, rows, :] * got
        dots[1, dot_rows(c * ZL, 3, ZL), :] -= last

    def begin_all(c, carry):
        begin(c)

        @pl.when(c == 0)
        def _():
            for step in range(EARLY, 6):
                for i in range(NP - 1):
                    copy2(1, step // 2, step % 2, i).start()

        return carry

    def end_all(c, carry):
        end(c)
        return carry

    lax.fori_loop(0, 3, begin_all, 0)
    lax.fori_loop(0, 3, end_all, 0)

    one_rows = jnp.ones((8, ED), F32)
    for k in (0, 1):
        summed = lax.dot_general(
            one_rows,
            dots[k],
            (((1,), (1,)), ((), ())),
            precision=lax.Precision.HIGHEST,
            preferred_element_type=F32,
        )
        rbuf[0, k : k + 1, :] = summed[0:1, :]

    def spread(i):
        return pltpu.make_async_remote_copy(
            src_ref=rbuf.at[0],
            dst_ref=rbuf.at[i + 1],
            send_sem=rs.at[i],
            recv_sem=rr.at[i],
            device_id=(elem_peers[i], me),
            device_id_type=MESH,
        )

    for i in range(NE - 1):
        spread(i).start()

    def drain(ah, carry):
        for half in range(HALVES):
            for i in range(NP - 1):
                copy1(half, ah, i).wait_send()
        return carry

    def drain2(step, carry):
        for half in range(HALVES):
            for i in range(NP - 1):
                copy2(half, step // 2, lax.rem(step, 2), i).wait_send()
        return carry

    def drain3(c, carry):
        for way in (0, 1):
            for k in (0, 1):
                r_halo(c, way, k).wait_send()
            q_halo(c, way).wait_send()
        return carry

    lax.fori_loop(0, AH, drain, 0)
    lax.fori_loop(0, 6, drain2, 0)
    lax.fori_loop(0, 3, drain3, 0)
    for i in range(NE - 1):
        spread(i).wait_send()

    for i in range(NE - 1):
        spread(i).wait_recv()
    part = jnp.sum(rbuf[...], axis=0)

    swapped = pltpu.roll(jnp.concatenate([part] * 4, axis=0), ED // 2, 1)
    aa, bb, cc, ee = part[0:1, :], swapped[0:1, :], part[1:2, :], swapped[1:2, :]
    alpha = aa / bb
    rr1 = alpha * alpha * cc - aa
    beta1 = 1.0 + rr1 / aa
    alpha1 = rr1 / (beta1 * beta1 * bb - 2.0 * beta1 * alpha * cc + alpha * alpha * ee)
    coef_s = alpha + alpha1 * beta1
    coef_t = alpha1 * alpha
    row8 = lax.broadcasted_iota(jnp.int32, (8, ED), 0)
    both = jnp.where(row8 == 0, coef_s, coef_t)
    both = jnp.where(lax.broadcasted_iota(jnp.int32, (8, ED), 1) < SYS, both, 0.0)
    both = jnp.transpose(jnp.concatenate([both] + [jnp.zeros((8, ED), F32)] * 15, axis=0))
    coef_out[0] = jnp.broadcast_to(both[0:SYS, 0:1], (SYS, ED))
    coef_out[1] = jnp.broadcast_to(both[0:SYS, 1:2], (SYS, ED))


def finish_kernel(r, q, p, coef, x_out, r_out, xs, rs, sem):
    def tile(st, carry):
        rows = pl.ds(pl.multiple_of(st * 8, 8), 8)
        s, t = coef[0, rows, :], coef[1, rows, :]
        for a in range(N):
            new, left = [], []
            for n in range(a * N, a * N + N):
                r_n, q_n, p_n = r[n, rows, :], q[n, rows, :], p[n, rows, :]
                new.append(s * r_n - t * q_n)
                left.append(r_n - s * q_n + t * p_n)
            for buf, vals in ((xs, new), (rs, left)):
                vals = jnp.swapaxes(jnp.stack(vals), 0, 1)
                for k in range(8):
                    buf[st, pl.ds(k * N * N + a * N, N), :] = vals[k]
        for copy in out_copies(st):
            copy.start()
        return carry

    def out_copies(st):
        return (
            pltpu.make_async_copy(xs.at[st], x_out.at[st], sem.at[st, 0]),
            pltpu.make_async_copy(rs.at[st], r_out.at[st], sem.at[st, 1]),
        )

    def drain(st, carry):
        for copy in out_copies(st):
            copy.wait()
        return carry

    lax.fori_loop(0, SYS // 8, tile, 0)
    lax.fori_loop(0, SYS // 8, drain, 0)


def on_device(velocity, elem_scale, elem_ids, edge_blocks):
    vel = velocity.reshape(SYS, N * N, ED)
    rows = np.zeros((ROWS, ED))
    table = -WEIGHTS[:, None] * DERIV
    for ph in range(AH):
        for ah in range(AH):
            for i in (0, 1):
                lanes = slice(i * ED // 2, (i + 1) * ED // 2)
                rows[ROW_SAME + ph * AH + ah, lanes] = table[2 * ah + i, 2 * ph + i]
                rows[ROW_SWAP + ph * AH + ah, lanes] = table[2 * ah + i, 2 * ph + 1 - i]
    for ah in range(AH):
        rows[ROW_AB + ah] = np.repeat(np.outer(WEIGHTS[2 * ah : 2 * ah + 2], WEIGHTS).ravel(), EG)
    rows[ROW_B] = np.repeat(np.tile(WEIGHTS, 2), EG)
    rows = jnp.asarray(rows, F32)
    four = halves(mode_matrix()).reshape(2, Z, 2, Z).transpose(0, 2, 1, 3).reshape(4, Z, Z)
    mats = jnp.asarray(np.concatenate([four, halves(np.kron(np.eye(2), np.kron(DERIV.T, np.eye(EG))))]))
    operands = (vel, elem_scale, elem_ids, rows, mats)
    vmem = pl.BlockSpec(memory_space=pltpu.VMEM)
    hbm = pl.BlockSpec(memory_space=pltpu.HBM)
    field = jax.ShapeDtypeStruct((N * N, SYS, ED), F32)
    dma = pltpu.SemaphoreType.DMA
    r0, q0, p0, coef = pl.pallas_call(
        kernel,
        out_shape=(field, field, field, jax.ShapeDtypeStruct((2, SYS, ED), F32)),
        in_specs=[hbm] * 5,
        out_specs=(vmem,) * 4,
        scratch_shapes=[
            pltpu.VMEM((SYS, N * N, ED), F32),
            pltpu.VMEM((2, ED), F32),
            pltpu.VMEM((1, ED), jnp.int32),
            pltpu.VMEM((ROWS, ED), F32),
            pltpu.VMEM((6, ED, ED), BF16),
            pltpu.VMEM((HALVES, AH, NP, 3, ZL, ED), F32),
            pltpu.VMEM((HALVES, AH, 3, Z, ED), F32),
            pltpu.VMEM((HALVES, AH, 3, Z, ED), F32),
            pltpu.VMEM((HALVES, AH, 2, 3, Z, ED), BF16),
            pltpu.VMEM((HALVES, 3, AH, Z, ED), F32),
            pltpu.VMEM((HALVES, 3, NP, AH, ZL, ED), F32),
            pltpu.VMEM((8, ED), F32),
            pltpu.VMEM((HALVES, 8, ED), F32),
            pltpu.VMEM((SYS, ED), F32),
            pltpu.VMEM((12, ED, ED), BF16),
            pltpu.VMEM((4, N, ZL, ED), F32),
            pltpu.VMEM((2, N, ZL, ED), F32),
            pltpu.VMEM((3, 2, AH, ZL, ED), F32),
            pltpu.VMEM((3, 2, AH, ZL, ED), F32),
            pltpu.VMEM((3, 2, AH, ZL, ED), F32),
            pltpu.VMEM((3, 2, AH, ZL, ED), F32),
            pltpu.VMEM((2, ED, ED), F32),
            pltpu.VMEM((NE, 2, ED), F32),
            dma((AH + 4,)),
            dma((HALVES, AH, NP - 1)),
            dma((HALVES, AH, NP - 1)),
            dma((HALVES, 3, 2, NP - 1)),
            dma((HALVES, 3, 2, NP - 1)),
            dma((3, 2, 2)),
            dma((3, 2, 2)),
            dma((3, 2)),
            dma((3, 2)),
            dma((NE - 1,)),
            dma((NE - 1,)),
        ],
        compiler_params=pltpu.CompilerParams(
            collective_id=0, has_side_effects=True, vmem_limit_bytes=48 * 1024 * 1024
        ),
        name="exchange_and_apply",
    )(*[pltpu.with_memory_space_constraint(v, pltpu.HBM) for v in operands])

    flat = jax.ShapeDtypeStruct((SYS // 8, 8 * N * N, ED), F32)
    new, left = pl.pallas_call(
        finish_kernel,
        out_shape=(flat, flat),
        in_specs=[vmem] * 4,
        out_specs=(hbm, hbm),
        scratch_shapes=[
            pltpu.VMEM(flat.shape, F32),
            pltpu.VMEM(flat.shape, F32),
            dma((SYS // 8, 2)),
        ],
        compiler_params=pltpu.CompilerParams(vmem_limit_bytes=16 * 1024 * 1024),
        name="finish",
    )(r0, q0, p0, coef)
    shape = (3, ZL, N, N, ED)
    return new.reshape(shape), left.reshape(shape)


def solution(mesh):
    in_specs = (
        P(None, "plane", None, None, "elem"),
        P(None, "elem"),
        P("elem", None),
        P("elem", None, None),
    )
    out_specs = (P(None, "plane", None, None, "elem"), P(None, "plane", None, None, "elem"))
    return jax.shard_map(
        on_device, mesh=mesh, in_specs=in_specs, out_specs=out_specs, check_vma=False
    )
```

```python
import functools
import math

import jax
import jax.numpy as jnp
import ml_dtypes
import numpy as np
from jax import lax
from jax.experimental import pallas as pl
from jax.experimental.pallas import tpu as pltpu
from jax.sharding import PartitionSpec as P

MESH = pl.DeviceIdType.MESH
F32 = jnp.float32
BF16 = jnp.bfloat16

N = 8
ED = 128
Z = 128
NP = 8
ZL = Z // NP
HALVES = 2
GROUPS = NP * HALVES
EG = ED // GROUPS
AH = N // 2
SYS = 3 * ZL
NX = 4
NZ = 8
NE = NX * NZ
EARLY = 5
PEN = 8.0
ROW_SAME, ROW_SWAP, ROW_AB, ROW_B = 0, AH * AH, 2 * AH * AH, 2 * AH * AH + AH
ROWS = 40
LAM = 4.0
STEP = 0.1


def node_tables():
    degree = N - 1
    points = -np.cos(np.pi * np.arange(N) / degree)
    scales = np.ones(N)
    scales[0] = 2.0
    scales[-1] = 2.0
    bary = (-1.0) ** np.arange(N) / scales
    deriv = np.zeros((N, N))
    for i in range(N):
        for j in range(N):
            if i != j:
                deriv[i, j] = bary[j] / bary[i] / (points[i] - points[j])
        deriv[i, i] = -np.sum(deriv[i])
    weights = np.zeros(N)
    for i in range(N):
        running = 0.0
        for k in range(1, degree // 2 + 1):
            factor = 1.0 if 2 * k == degree else 2.0
            running += factor / (4.0 * k * k - 1.0) * np.cos(2.0 * np.pi * i * k / degree)
        weights[i] = (1.0 if i in (0, degree) else 2.0) / degree * (1.0 - running)
    stiff = deriv.T @ (weights[:, None] * deriv)
    return deriv, weights, stiff


def mode_matrix():
    slots = np.arange(Z)
    harmonic = slots // 2
    angles = 2.0 * math.pi / Z * (harmonic[:, None] * slots[None, :] % Z)
    four = np.where((slots % 2 == 0)[:, None], np.cos(angles), np.sin(angles)) * (2.0 / Z)
    four[0] = 1.0 / Z
    four[1] = np.where(slots % 2 == 0, 1.0, -1.0) / Z
    dz = np.zeros((Z, Z))
    wave = STEP * np.arange(Z // 2)
    dz[0::2] = wave[:, None] * four[1::2]
    dz[1::2] = -wave[:, None] * four[0::2]
    return np.concatenate([four, -dz], axis=1)


def halves(table):
    high = table.astype(np.float32).astype(ml_dtypes.bfloat16)
    low = (table - high.astype(np.float64)).astype(np.float32).astype(ml_dtypes.bfloat16)
    return np.stack([high, low])


DERIV, WEIGHTS, STIFF = node_tables()


def split(x):
    high = x.astype(BF16)
    return high, (x - high.astype(F32)).astype(BF16)


def dot(x, y):
    return jnp.dot(x, y, preferred_element_type=F32)


def pick(x, table):
    high, low = split(x)
    return dot(high, table) + dot(low, table)


def turned(x, groups):
    shift = EG * (groups % GROUPS)
    return pltpu.roll(x, shift, x.ndim - 1) if shift else x


def block_transpose(rows, turned_before=False):
    if not turned_before:
        rows = [turned(x, i) for i, x in enumerate(rows)]
    lane = lax.broadcasted_iota(jnp.int32, rows[0].shape, rows[0].ndim - 1) // EG
    d = 1
    while d < GROUPS:
        clear = (lane & d) == 0
        rows = [jnp.where(clear, rows[i], rows[(i + d) % GROUPS]) for i in range(GROUPS)]
        d *= 2
    return [turned(rows[-g % GROUPS], -g) for g in range(GROUPS)]


def stiff_times(v, wanted):
    even = [v[p] + v[N - 1 - p] for p in range(N // 2)]
    odd = [v[p] - v[N - 1 - p] for p in range(N // 2)]
    out = [None] * N
    for a in wanted:
        s = [0.5 * (STIFF[a, p] + STIFF[a, N - 1 - p]) for p in range(N // 2)]
        t = [0.5 * (STIFF[a, p] - STIFF[a, N - 1 - p]) for p in range(N // 2)]
        e = sum(float(s[p]) * even[p] for p in range(1, N // 2)) + float(s[0]) * even[0]
        o = sum(float(t[p]) * odd[p] for p in range(1, N // 2)) + float(t[0]) * odd[0]
        out[a] = e + o
        out[N - 1 - a] = e - o
    return out


def kernel(
    vel,
    scale_in,
    ids_in,
    rows_in,
    mats_in,
    res,
    qv,
    pv,
    coef_out,
    vin,
    scale,
    ids,
    ctab,
    mats,
    xsend,
    xbuf,
    acc,
    bbuf,
    fsend,
    fbuf,
    geo,
    part_geo,
    hel,
    tables,
    face,
    edge,
    rsend,
    rrecv,
    qsend,
    qrecv,
    dots,
    rbuf,
    in_sem,
    s1,
    r1,
    s2,
    r2,
    hs1,
    hr1,
    hs2,
    hr2,
    rs,
    rr,
):
    e = lax.axis_index("elem")
    me = lax.axis_index("plane")
    y, core = me // 2, lax.rem(me, 2)
    z, x = e // NX, lax.rem(e, NX)
    plane_offsets = [(dy, dc) for dy in (2, 1, 3, 0) for dc in (0, 1) if (dy, dc) != (0, 0)]
    plane_peers = [lax.rem(y + dy, 4) * 2 + lax.rem(core + dc, 2) for dy, dc in plane_offsets]
    elem_peers = [
        lax.rem(z + dz, NZ) * NX + lax.rem(x + dx, NX)
        for dz in (4, 3, 5, 2, 6, 1, 7, 0)
        for dx in (2, 1, 3, 0)
        if (dz, dx) != (0, 0)
    ]
    up, down = lax.rem(e + 1, NE), lax.rem(e + NE - 1, NE)

    barrier = pltpu.get_barrier_semaphore()
    for t in plane_peers:
        pl.semaphore_signal(barrier, inc=1, device_id=(e, t), device_id_type=MESH)

    def load_nodes(ah):
        nodes = pl.ds(pl.multiple_of(ah * 2 * N, 2 * N), 2 * N)
        return pltpu.make_async_copy(vel.at[:, nodes, :], vin.at[:, nodes, :], in_sem.at[ah])

    for ah in range(AH):
        load_nodes(ah).start()
    pairs = ((scale_in, scale), (ids_in, ids), (rows_in, ctab), (mats_in, mats))
    loads = [
        pltpu.make_async_copy(src, dst, in_sem.at[AH + i]) for i, (src, dst) in enumerate(pairs)
    ]
    for load in loads:
        load.start()
    for t in elem_peers:
        pl.semaphore_signal(barrier, inc=1, device_id=(t, me), device_id_type=MESH)

    def copy1(half, ah, i):
        t = plane_peers[i]
        return pltpu.make_async_remote_copy(
            src_ref=xsend.at[half, ah, t],
            dst_ref=xbuf.at[half, ah, :, pl.ds(pl.multiple_of(me * ZL, ZL), ZL), :],
            send_sem=s1.at[half, ah, i],
            recv_sem=r1.at[half, ah, i],
            device_id=(e, t),
            device_id_type=MESH,
        )

    def copy2(half, c, k, i):
        t = plane_peers[i]
        return pltpu.make_async_remote_copy(
            src_ref=fsend.at[half, c, pl.ds(2 * k, 2), pl.ds(pl.multiple_of(t * ZL, ZL), ZL), :],
            dst_ref=fbuf.at[half, c, me, pl.ds(2 * k, 2)],
            send_sem=s2.at[half, c, k, i],
            recv_sem=r2.at[half, c, k, i],
            device_id=(e, t),
            device_id_type=MESH,
        )

    def pack_first(ah):
        load_nodes(ah).wait()
        for c in range(3):
            for z8 in range(ZL // 8):
                nodes = pl.ds(pl.multiple_of(ah * 2 * N, 2 * N), 2 * N)
                tile = jnp.swapaxes(vin[pl.ds(c * ZL + z8 * 8, 8), nodes, :], 0, 1)
                for g, row in enumerate(block_transpose([tile[k] for k in range(2 * N)])):
                    xsend[g % HALVES, ah, g // HALVES, c, pl.ds(z8 * 8, 8), :] = row

    def send_first(half, ah):
        for i in range(NP - 1):
            copy1(half, ah, i).start()
        mine = pl.ds(pl.multiple_of(me * ZL, ZL), ZL)
        xbuf[half, ah, :, mine, :] = xsend[half, ah, me]

    pack_first(0)
    pl.semaphore_wait(barrier, NP - 1 + NE - 1)
    send_first(0, 0)

    def first(ah, carry):
        pack_first(ah)
        send_first(0, ah)
        return carry

    def first_rest(ah, carry):
        send_first(1, ah)
        return carry

    lax.fori_loop(1, AH, first, 0)
    lax.fori_loop(0, AH, first_rest, 0)

    for load in loads:
        load.wait()

    lid = ids[...] & (ED - 1)
    growth = 1.0 + 2.0 * (ids[...] // 64).astype(F32) / 63.0
    circ = scale[0:1, :] * growth
    radial = scale[1:2, :]
    geo[0:1, :] = circ * radial
    geo[1:2, :] = radial / circ
    geo[2:3, :] = circ / radial
    for half in range(HALVES):
        share = []
        for val in (circ, radial):
            first = ED - EG * (HALVES * me + half)
            val = pltpu.roll(jnp.broadcast_to(val, (8, ED)), lax.rem(first, ED), 1)
            val = jnp.where(lax.broadcasted_iota(jnp.int32, (8, ED), 1) < EG, val, 0.0)
            for d in (1, 2, 4, 8):
                val = val + pltpu.roll(val, EG * d, 1)
            share.append(val[0:1, :])
        g_circ, g_radial = share
        part_geo[half, 0:1, :] = g_circ * g_radial
        part_geo[half, 1:2, :] = g_circ
        part_geo[half, 2:3, :] = g_radial * ctab[ROW_B : ROW_B + 1, :]

    acc[...] = jnp.zeros_like(acc)
    dots[...] = jnp.zeros_like(dots)
    row_i = lax.broadcasted_iota(jnp.int32, (ED, ED), 0)
    lane_i = lax.broadcasted_iota(jnp.int32, (ED, ED), 1)
    lid_l = jnp.broadcast_to(lid, (ED, ED))
    lid_t = jnp.transpose(lid_l.astype(F32)).astype(jnp.int32)

    def ones(where):
        return jnp.where(where, 1.0, 0.0).astype(BF16)

    tables[0] = ones(lid_t == ((lid_l & 64) | ((lid_l + 63) & 63)))
    tables[1] = ones(lid_t == ((lid_l & 64) | ((lid_l + 1) & 63)))
    tables[2] = ones((lid_t == (lid_l ^ 64)) & (lid_l >= 64))
    tables[3] = ones((lid_t == (lid_l ^ 64)) & (lid_l < 64))
    tables[4] = ones(lid_t == lane_i + 64)
    tables[5] = ones((lid_t == lane_i) & (lane_i >= 64))
    tables[6] = ones((lid_t == lane_i) & (lane_i < 64))
    tables[7] = ones(lid_t + 64 == lane_i)
    tables[8] = ones((row_i == lid_l) & (lid_l < 64))
    tables[9] = ones(row_i == lid_l + 64)
    tables[10] = ones(row_i + 64 == lid_l)
    tables[11] = ones((row_i == lid_l) & (lid_l >= 64))
    slot = me * ZL + (lax.broadcasted_iota(jnp.int32, (SYS, ED), 0) & (ZL - 1))
    kappa = jnp.where(slot == 1, Z // 2, slot // 2).astype(F32)
    hel[...] = (LAM + (STEP * kappa) * (STEP * kappa)) * geo[0:1, :]

    f_high = jnp.concatenate([mats[0], mats[1]], axis=1)
    f_low = jnp.concatenate([mats[2], mats[3]], axis=1)

    def between(half, carry):
        def arrive_first(ph, carry):
            for i in range(NP - 1):
                copy1(half, ph, i).wait_recv()
            w_ab = ctab[pl.ds(ROW_AB + ph, 1), :]
            mass = part_geo[half, 0:1, :] * w_ab
            g_y = part_geo[half, 1:2, :] * w_ab
            g_x = part_geo[half, 2:3, :]
            for c in range(3):
                fy_high, fy_low = split(xbuf[half, ph, 1] * xbuf[half, ph, c])
                dy = dot(fy_high, mats[4]) + dot(fy_low, mats[4]) + dot(fy_high, mats[5])
                acc[half, ph, c] += (LAM * mass) * xbuf[half, ph, c] - g_y * dy
                b_high, b_low = split(mass * (xbuf[half, ph, 2] * xbuf[half, ph, c]))
                bbuf[half, ph, 0, c] = b_high
                bbuf[half, ph, 1, c] = b_low
                for k in range(4):
                    rows = pl.ds(k * 32, 32)
                    fx = g_x * (xbuf[half, ph, 0, rows, :] * xbuf[half, ph, c, rows, :])
                    swap = pltpu.roll(fx, ED // 2, 1)
                    for ah in range(AH):
                        same = ctab[pl.ds(ROW_SAME + ph * AH + ah, 1), :]
                        other = ctab[pl.ds(ROW_SWAP + ph * AH + ah, 1), :]
                        acc[half, ah, c, rows, :] += same * fx + other * swap
            return carry

        def send_second(step, carry):
            c, k = step // 2, lax.rem(step, 2)
            for j in (0, 1):
                ah = 2 * k + j
                a_high, a_low = split(acc[half, ah, c])
                high = jnp.concatenate([a_high, bbuf[half, ah, 0, c]], axis=0)
                low = jnp.concatenate([a_low, bbuf[half, ah, 1, c]], axis=0)
                out = dot(f_high, high) + dot(f_high, low) + dot(f_low, high)
                fsend[half, c, ah] = pltpu.roll(out, EG * (HALVES * me + half), 1)
            @pl.when((half == 0) | (step < EARLY))
            def _():
                for i in range(NP - 1):
                    copy2(half, c, k, i).start()

            mine = pl.ds(pl.multiple_of(me * ZL, ZL), ZL)
            fbuf[half, c, me, pl.ds(2 * k, 2)] = fsend[half, c, pl.ds(2 * k, 2), mine, :]
            return carry

        lax.fori_loop(0, AH, arrive_first, 0)
        lax.fori_loop(0, 6, send_second, 0)
        return carry

    lax.fori_loop(0, HALVES, between, 0)

    def sys_rows(c):
        return pl.ds(pl.multiple_of(c * ZL, ZL), ZL)

    def r_halo(c, way, k):
        return pltpu.make_async_remote_copy(
            src_ref=rsend.at[c, way, pl.ds(2 * k, 2)],
            dst_ref=rrecv.at[c, way, pl.ds(2 * k, 2)],
            send_sem=hs1.at[c, way, k],
            recv_sem=hr1.at[c, way, k],
            device_id=((up, down)[way], me),
            device_id_type=MESH,
        )

    def q_halo(c, way):
        return pltpu.make_async_remote_copy(
            src_ref=qsend.at[c, way],
            dst_ref=qrecv.at[c, way],
            send_sem=hs2.at[c, way],
            recv_sem=hr2.at[c, way],
            device_id=((up, down)[way], me),
            device_id_type=MESH,
        )

    def side(v, rows, b, first, count):
        return jnp.concatenate([v[a * N + b, rows, :] for a in range(first, first + count)], axis=0)

    def pack_edges(v, c, pair, count):
        rows = sys_rows(c)
        packed = []
        for b, t in ((N - 1, 4), (0, 6)):
            for k in (0, 1):
                nodes = [v[(2 * (pair + i) + k) * N + b, rows, :] for i in range(count)]
                nodes = jnp.concatenate(nodes, axis=0) if count > 1 else nodes[0]
                packed.append(pick(nodes, tables[t + k]))
        return packed[0] + packed[1], packed[2] + packed[3]

    def send_q_edges(c):
        for way, got in enumerate(pack_edges(qv, c, 0, AH)):
            qsend[c, way] = got.reshape(AH, ZL, ED)
            q_halo(c, way).start()

    def take_edges(recv, c):
        for way in (0, 1):
            there = (e > 0) if way == 0 else (e < NE - 1)
            got = recv[c, way].reshape(AH * ZL, ED)
            for k in (0, 1):
                here = jnp.where(there, pick(got, tables[8 + 2 * way + k]), 0.0)
                here = here.reshape(AH, ZL, ED)
                for pair in range(AH):
                    edge[way, 2 * pair + k] = here[pair]

    def take_faces(v, c):
        sys = sys_rows(c)
        shape = (N, ZL, ED)
        face[2] = pick(side(v, sys, N - 1, 0, N), tables[2]).reshape(shape)
        face[3] = pick(side(v, sys, 0, 0, N), tables[3]).reshape(shape)
        face[0] = pick(v[(N - 1) * N : N * N, sys, :].reshape(N * ZL, ED), tables[0]).reshape(shape)
        face[1] = pick(v[0:N, sys, :].reshape(N * ZL, ED), tables[1]).reshape(shape)

    def apply_local(v, q, c, columns):
        def tile(h, carry):
            rows = pl.ds(pl.multiple_of(c * ZL + h * 8, 8), 8)
            frows = pl.ds(pl.multiple_of(h * 8, 8), 8)
            hm = hel[rows, :]
            kx = jnp.broadcast_to(geo[1:2, :], (8, ED))
            ky = jnp.broadcast_to(geo[2:3, :], (8, ED))
            nodes = [b for pair in columns for b in (pair, N - 1 - pair)]
            for b in nodes:
                col = stiff_times([v[a * N + b, rows, :] for a in range(N)], range(N // 2))
                scale_b = kx * float(WEIGHTS[b])
                for a in range(N):
                    q[a * N + b, rows, :] = scale_b * col[a]
            for a in range(N):
                vals = [v[a * N + b, rows, :] for b in range(N)]
                line = stiff_times(vals, columns)
                scale_a = ky * float(WEIGHTS[a])
                hm_a = hm * float(WEIGHTS[a])
                for b in nodes:
                    out = q[a * N + b, rows, :] + scale_a * line[b]
                    out = out + (hm_a * float(WEIGHTS[b])) * vals[b]
                    if a == 0:
                        out = out + float(PEN * WEIGHTS[b]) * (vals[b] - face[0, b, frows, :])
                    if a == N - 1:
                        out = out + float(PEN * WEIGHTS[b]) * (vals[b] - face[1, b, frows, :])
                    if b == 0:
                        out = out + float(PEN * WEIGHTS[a]) * (vals[b] - face[2, a, frows, :])
                    if b == N - 1:
                        out = out + float(PEN * WEIGHTS[a]) * (vals[b] - face[3, a, frows, :])
                    q[a * N + b, rows, :] = out
            return carry

        lax.fori_loop(0, ZL // 8, tile, 0)

    def add_edges(q, c):
        rows = sys_rows(c)
        for a in range(N):
            q[a * N, rows, :] -= float(PEN * WEIGHTS[a]) * edge[0, a]
            q[a * N + N - 1, rows, :] -= float(PEN * WEIGHTS[a]) * edge[1, a]

    def arrive_second(c, ah):
        groups = [fbuf[g % HALVES, c, g // HALVES, ah] for g in range(GROUPS)]
        for k, line in enumerate(block_transpose(groups, True)):
            res[ah * 2 * N + k, sys_rows(c), :] = line

    def dot_rows(first, k, count):
        return pl.ds(pl.multiple_of(first + (k % 2) * (ED // 2), 8), count)

    def begin(c):
        def arrive(ah, carry):
            arrive_second(c, ah)
            return carry

        for k in (0, 1):
            for half in range(HALVES):
                for i in range(NP - 1):
                    copy2(half, c, k, i).wait_recv()
            lax.fori_loop(2 * k, 2 * k + 2, arrive, 0)
            for way, got in enumerate(pack_edges(res, c, 2 * k, 2)):
                rsend[c, way, pl.ds(2 * k, 2)] = got.reshape(2, ZL, ED)
            if k == 1:
                take_faces(res, c)
            for way in (0, 1):
                r_halo(c, way, k).start()
        apply_local(res, qv, c, (0,))
        send_q_edges(c)
        apply_local(res, qv, c, (1, 2, 3))

    def end(c):
        for way in (0, 1):
            for k in (0, 1):
                r_halo(c, way, k).wait_recv()
        take_edges(rrecv, c)
        add_edges(qv, c)
        take_faces(qv, c)
        apply_local(qv, pv, c, range(N // 2))

        def dot_tile(h, carry):
            rows = pl.ds(pl.multiple_of(c * ZL + h * 8, 8), 8)
            sums = [jnp.zeros((8, ED), F32) for _ in range(4)]
            for n in range(N * N):
                r_n, q_n, p_n = res[n, rows, :], qv[n, rows, :], pv[n, rows, :]
                for k, prod in enumerate((r_n * r_n, r_n * q_n, q_n * q_n, q_n * p_n)):
                    sums[k] = sums[k] + prod
            for k in range(4):
                dots[k // 2, dot_rows(c * ZL + h * 8, k, 8), :] = sums[k]
            return carry

        lax.fori_loop(0, ZL // 8, dot_tile, 0)
        for way in (0, 1):
            q_halo(c, way).wait_recv()
        take_edges(qrecv, c)
        rows = sys_rows(c)
        inner = jnp.broadcast_to(lid < 64, (ZL, ED)) & (e > 0)
        outer = jnp.broadcast_to(lid >= 64, (ZL, ED)) & (e < NE - 1)
        last = jnp.zeros((ZL, ED), F32)
        for a in range(N):
            w_a = float(PEN * WEIGHTS[a])
            for way, b, where in ((0, 0, inner), (1, N - 1, outer)):
                n = a * N + b
                got = w_a * (edge[way, a] - jnp.where(where, w_a * res[n, rows, :], 0.0))
                pv[n, rows, :] -= got
                last = last + qv[n, rows, :] * got
        dots[1, dot_rows(c * ZL, 3, ZL), :] -= last

    def begin_all(c, carry):
        begin(c)

        @pl.when(c == 0)
        def _():
            for step in range(EARLY, 6):
                for i in range(NP - 1):
                    copy2(1, step // 2, step % 2, i).start()

        return carry

    def end_all(c, carry):
        end(c)
        return carry

    lax.fori_loop(0, 3, begin_all, 0)
    lax.fori_loop(0, 3, end_all, 0)

    one_rows = jnp.ones((8, ED), BF16)
    for k in (0, 1):
        high, rest = split(dots[k])
        low = dots[k] - high.astype(F32) - rest.astype(F32)
        summed = jnp.zeros((8, ED), F32)
        for term in (low.astype(BF16), rest, high):
            summed = summed + lax.dot_general(
                one_rows, term, (((1,), (1,)), ((), ())), preferred_element_type=F32
            )
        rbuf[0, k : k + 1, :] = summed[0:1, :]

    def spread(i):
        return pltpu.make_async_remote_copy(
            src_ref=rbuf.at[0],
            dst_ref=rbuf.at[i + 1],
            send_sem=rs.at[i],
            recv_sem=rr.at[i],
            device_id=(elem_peers[i], me),
            device_id_type=MESH,
        )

    for i in range(NE - 1):
        spread(i).start()

    def drain(ah, carry):
        for half in range(HALVES):
            for i in range(NP - 1):
                copy1(half, ah, i).wait_send()
        return carry

    def drain2(step, carry):
        for half in range(HALVES):
            for i in range(NP - 1):
                copy2(half, step // 2, lax.rem(step, 2), i).wait_send()
        return carry

    def drain3(c, carry):
        for way in (0, 1):
            for k in (0, 1):
                r_halo(c, way, k).wait_send()
            q_halo(c, way).wait_send()
        return carry

    lax.fori_loop(0, AH, drain, 0)
    lax.fori_loop(0, 6, drain2, 0)
    lax.fori_loop(0, 3, drain3, 0)
    for i in range(NE - 1):
        spread(i).wait_send()

    for i in range(NE - 1):
        spread(i).wait_recv()
    part = jnp.sum(rbuf[...], axis=0)

    swapped = pltpu.roll(jnp.concatenate([part] * 4, axis=0), ED // 2, 1)
    aa, bb, cc, ee = part[0:1, :], swapped[0:1, :], part[1:2, :], swapped[1:2, :]
    alpha = aa / bb
    rr1 = alpha * alpha * cc - aa
    beta1 = 1.0 + rr1 / aa
    alpha1 = rr1 / (beta1 * beta1 * bb - 2.0 * beta1 * alpha * cc + alpha * alpha * ee)
    coef_s = alpha + alpha1 * beta1
    coef_t = alpha1 * alpha
    row8 = lax.broadcasted_iota(jnp.int32, (8, ED), 0)
    both = jnp.where(row8 == 0, coef_s, coef_t)
    both = jnp.where(lax.broadcasted_iota(jnp.int32, (8, ED), 1) < SYS, both, 0.0)
    both = jnp.transpose(jnp.concatenate([both] + [jnp.zeros((8, ED), F32)] * 15, axis=0))
    coef_out[0] = jnp.broadcast_to(both[0:SYS, 0:1], (SYS, ED))
    coef_out[1] = jnp.broadcast_to(both[0:SYS, 1:2], (SYS, ED))


def finish_kernel(r, q, p, coef, x_out, r_out, xs, rs, sem):
    def tile(st, carry):
        rows = pl.ds(pl.multiple_of(st * 8, 8), 8)
        s, t = coef[0, rows, :], coef[1, rows, :]
        for a in range(N):
            new, left = [], []
            for n in range(a * N, a * N + N):
                r_n, q_n, p_n = r[n, rows, :], q[n, rows, :], p[n, rows, :]
                new.append(s * r_n - t * q_n)
                left.append(r_n - s * q_n + t * p_n)
            for buf, vals in ((xs, new), (rs, left)):
                vals = jnp.swapaxes(jnp.stack(vals), 0, 1)
                for k in range(8):
                    buf[st, pl.ds(k * N * N + a * N, N), :] = vals[k]
        for copy in out_copies(st):
            copy.start()
        return carry

    def out_copies(st):
        return (
            pltpu.make_async_copy(xs.at[st], x_out.at[st], sem.at[st, 0]),
            pltpu.make_async_copy(rs.at[st], r_out.at[st], sem.at[st, 1]),
        )

    def drain(st, carry):
        for copy in out_copies(st):
            copy.wait()
        return carry

    lax.fori_loop(0, SYS // 8, tile, 0)
    lax.fori_loop(0, SYS // 8, drain, 0)


def on_device(velocity, elem_scale, elem_ids, edge_blocks):
    vel = velocity.reshape(SYS, N * N, ED)
    rows = np.zeros((ROWS, ED))
    table = -WEIGHTS[:, None] * DERIV
    for ph in range(AH):
        for ah in range(AH):
            for i in (0, 1):
                lanes = slice(i * ED // 2, (i + 1) * ED // 2)
                rows[ROW_SAME + ph * AH + ah, lanes] = table[2 * ah + i, 2 * ph + i]
                rows[ROW_SWAP + ph * AH + ah, lanes] = table[2 * ah + i, 2 * ph + 1 - i]
    for ah in range(AH):
        rows[ROW_AB + ah] = np.repeat(np.outer(WEIGHTS[2 * ah : 2 * ah + 2], WEIGHTS).ravel(), EG)
    rows[ROW_B] = np.repeat(np.tile(WEIGHTS, 2), EG)
    rows = jnp.asarray(rows, F32)
    four = halves(mode_matrix()).reshape(2, Z, 2, Z).transpose(0, 2, 1, 3).reshape(4, Z, Z)
    mats = jnp.asarray(np.concatenate([four, halves(np.kron(np.eye(2), np.kron(DERIV.T, np.eye(EG))))]))
    operands = (vel, elem_scale, elem_ids, rows, mats)
    vmem = pl.BlockSpec(memory_space=pltpu.VMEM)
    hbm = pl.BlockSpec(memory_space=pltpu.HBM)
    field = jax.ShapeDtypeStruct((N * N, SYS, ED), F32)
    dma = pltpu.SemaphoreType.DMA
    r0, q0, p0, coef = pl.pallas_call(
        kernel,
        out_shape=(field, field, field, jax.ShapeDtypeStruct((2, SYS, ED), F32)),
        in_specs=[hbm] * 5,
        out_specs=(vmem,) * 4,
        scratch_shapes=[
            pltpu.VMEM((SYS, N * N, ED), F32),
            pltpu.VMEM((2, ED), F32),
            pltpu.VMEM((1, ED), jnp.int32),
            pltpu.VMEM((ROWS, ED), F32),
            pltpu.VMEM((6, ED, ED), BF16),
            pltpu.VMEM((HALVES, AH, NP, 3, ZL, ED), F32),
            pltpu.VMEM((HALVES, AH, 3, Z, ED), F32),
            pltpu.VMEM((HALVES, AH, 3, Z, ED), F32),
            pltpu.VMEM((HALVES, AH, 2, 3, Z, ED), BF16),
            pltpu.VMEM((HALVES, 3, AH, Z, ED), F32),
            pltpu.VMEM((HALVES, 3, NP, AH, ZL, ED), F32),
            pltpu.VMEM((8, ED), F32),
            pltpu.VMEM((HALVES, 8, ED), F32),
            pltpu.VMEM((SYS, ED), F32),
            pltpu.VMEM((12, ED, ED), BF16),
            pltpu.VMEM((4, N, ZL, ED), F32),
            pltpu.VMEM((2, N, ZL, ED), F32),
            pltpu.VMEM((3, 2, AH, ZL, ED), F32),
            pltpu.VMEM((3, 2, AH, ZL, ED), F32),
            pltpu.VMEM((3, 2, AH, ZL, ED), F32),
            pltpu.VMEM((3, 2, AH, ZL, ED), F32),
            pltpu.VMEM((2, ED, ED), F32),
            pltpu.VMEM((NE, 2, ED), F32),
            dma((AH + 4,)),
            dma((HALVES, AH, NP - 1)),
            dma((HALVES, AH, NP - 1)),
            dma((HALVES, 3, 2, NP - 1)),
            dma((HALVES, 3, 2, NP - 1)),
            dma((3, 2, 2)),
            dma((3, 2, 2)),
            dma((3, 2)),
            dma((3, 2)),
            dma((NE - 1,)),
            dma((NE - 1,)),
        ],
        compiler_params=pltpu.CompilerParams(
            collective_id=0, has_side_effects=True, vmem_limit_bytes=48 * 1024 * 1024
        ),
        name="exchange_and_apply",
    )(*[pltpu.with_memory_space_constraint(v, pltpu.HBM) for v in operands])

    flat = jax.ShapeDtypeStruct((SYS // 8, 8 * N * N, ED), F32)
    new, left = pl.pallas_call(
        finish_kernel,
        out_shape=(flat, flat),
        in_specs=[vmem] * 4,
        out_specs=(hbm, hbm),
        scratch_shapes=[
            pltpu.VMEM(flat.shape, F32),
            pltpu.VMEM(flat.shape, F32),
            dma((SYS // 8, 2)),
        ],
        compiler_params=pltpu.CompilerParams(vmem_limit_bytes=16 * 1024 * 1024),
        name="finish",
    )(r0, q0, p0, coef)
    shape = (3, ZL, N, N, ED)
    return new.reshape(shape), left.reshape(shape)


def solution(mesh):
    in_specs = (
        P(None, "plane", None, None, "elem"),
        P(None, "elem"),
        P("elem", None),
        P("elem", None, None),
    )
    out_specs = (P(None, "plane", None, None, "elem"), P(None, "plane", None, None, "elem"))
    return jax.shard_map(
        on_device, mesh=mesh, in_specs=in_specs, out_specs=out_specs, check_vma=False
    )
```
